32 devices in a mesh: seq: 8 (over z, y), batch: 4 (over x, core).
Axes of the slice: x: 2, y: 2, z: 4, core: 2. Of those that a mesh axis runs over, the one named last changes fastest.
Arguments:
- tokens: int32 [16, 1536], P('batch', 'seq'), may hold values from 0 to 255
- loss_mask: int32 [16, 512], P('batch', 'seq'), may hold values 0 or 1
- cotangent: bfloat16 [16, 512, 512], P('batch', 'seq'), may hold values from -6 to 6
- embed: bfloat16 [256, 512], replicated, may hold values from -6 to 6
- gain_attn: bfloat16 [2, 512], replicated, may hold values from 0.5 to 1.5
- w_qkv: bfloat16 [2, 512, 1536], replicated, may hold values from -0.25 to 0.25
- w_out: bfloat16 [2, 512, 512], replicated, may hold values from -2 to 2
- gain_ffn: bfloat16 [2, 512], replicated, may hold values from 0.5 to 1.5
- w_up: bfloat16 [2, 512, 2048], replicated, may hold values from -0.25 to 0.25
- w_down: bfloat16 [2, 2048, 512], replicated, may hold values from -0.125 to 0.125
- w_pool: bfloat16 [1536, 512], replicated, may hold values from -0.15625 to 0.15625
Outputs:
- full_out: bfloat16 [16, 1536, 512], P('batch', 'seq')
- short_out: bfloat16 [16, 512, 512], P('batch', 'seq')
- input_grad: float32 [16, 1536, 512], P('batch', 'seq')
- embed_grad: float32 [256, 512], P('batch', 'seq')
- gain_attn_grad: float32 [2, 512], replicated
- w_qkv_grad: float32 [2, 512, 1536], P(None, 'batch', 'seq')
- w_out_grad: float32 [2, 512, 512], P(None, 'batch', 'seq')
- gain_ffn_grad: float32 [2, 512], replicated
- w_up_grad: float32 [2, 512, 2048], P(None, 'batch', 'seq')
- w_down_grad: float32 [2, 2048, 512], P(None, 'batch', 'seq')
- w_pool_grad: float32 [1536, 512], P('batch', 'seq')
The draws below stay inside these ranges and needn't reach their ends.
All inputs are finite; a program needn't handle non-finite values. No bound on the sum of `loss_mask` on one device may be relied on, other than what follows from the above.
Results may differ from the reference program's by a relative error of at most 0.02.
Values may be sent and summed in bfloat16 or wider, within the bound.
No kernel may reach another device: no remote copies, remote signals or barrier semaphores. Data moves between devices by JAX's collectives and lax.ppermute only.
A program may use at most 320 MiB of HBM per device.

```python
import math
import jax
import jax.numpy as jnp
import numpy as np
from jax import lax

D = 512
H = 8
DH = 64
FF = 2048
VOCAB = 256
ROWS = 16
SEQ_LEN = 1536
SHORT_LEN = 512


def set_ends(drawn, key, least, top_value):
    extent = drawn.shape
    spot = [jax.random.randint(jax.random.fold_in(key, axis), (), 0, extent[axis]) for axis in range(len(extent))]
    drawn = drawn.at[tuple(spot)].set(least)
    longest = extent.index(max(extent))
    spot[longest] = (spot[longest] + 1) % extent[longest]
    return drawn.at[tuple(spot)].set(top_value)


def level_of(own_key, shape, cuts, low, high):
    level = 1.0
    for dim, blocks in cuts:
        draws = jax.random.uniform(jax.random.fold_in(jax.random.fold_in(own_key, 6), dim), (blocks,), jnp.float32, low / len(cuts), high / len(cuts))
        level = level * jnp.repeat(jnp.exp(draws), shape[dim] // blocks).reshape((-1,) + (1,) * (len(shape) - 1 - dim))
    return level


def rank_bounds(number_of, slope):
    loads = [(1 << 20) // math.isqrt(grade ** slope) + 1 for grade in range(1, number_of + 1)]
    spread = 1 + sum(loads) // (1 << 30)
    return np.cumsum(np.array([max(1, weight // spread) for weight in loads]))


def skewed_ids(own_key, extent, amount, skew):
    table = rank_bounds(amount, skew)
    lot = jax.random.randint(jax.random.fold_in(own_key, 1), extent, 0, int(table[amount - 1]))
    rank = jnp.searchsorted(jnp.asarray(table, jnp.int32), lot, side="right")
    return jax.random.permutation(jax.random.fold_in(own_key, 2), amount)[rank].astype(jnp.int32)


def noise(own_key, dims, spread, limit, pieces=(), dtype=jnp.bfloat16):
    values = spread * jax.random.normal(own_key, dims, jnp.float32)
    if pieces:
        values = values * level_of(own_key, dims, pieces, -0.22, 0.18)
    return jnp.clip(values, -limit, limit).astype(dtype)


def setup_inputs(seed: int = 0) -> dict:
    splits = jax.random.split(jax.random.key(seed), 12)
    return {
        "tokens": set_ends(skewed_ids(splits[0], (ROWS, SEQ_LEN), VOCAB, 2), jax.random.fold_in(splits[0], 3), 0, VOCAB - 1).astype(jnp.int32),
        "loss_mask": set_ends((jax.random.randint(splits[1], (ROWS, SHORT_LEN), 0, 2) < 1).astype(jnp.int32), jax.random.fold_in(splits[1], 1), 0, 1),
        "cotangent": noise(splits[2], (ROWS, SHORT_LEN, D), 1.0, 6.0, ((0, 4), (1, 8))),
        "embed": noise(splits[3], (VOCAB, D), 1.0, 6.0),
        "gain_attn": jnp.clip(1.0 + 0.1 * jax.random.normal(splits[4], (2, D), jnp.float32), 0.5, 1.5).astype(jnp.bfloat16),
        "w_qkv": noise(splits[5], (2, D, 3 * D), D ** -0.5, 0.25),
        "w_out": noise(splits[6], (2, D, D), (max(D // 64, 1)) ** -0.5, 2.0),
        "gain_ffn": jnp.clip(1.0 + 0.1 * jax.random.normal(splits[7], (2, D), jnp.float32), 0.5, 1.5).astype(jnp.bfloat16),
        "w_up": noise(splits[8], (2, D, FF), D ** -0.5, 0.25),
        "w_down": noise(splits[9], (2, FF, D), FF ** -0.5, 0.125),
        "w_pool": noise(splits[10], (3 * D, D), (3 * D) ** -0.5, 0.15625),
    }


@jax.custom_vjp
def low(v):
    return lax.optimization_barrier(v.astype(jnp.bfloat16)).astype(jnp.float32)

@jax.custom_vjp
def low_back(v):
    return v

def low_keep(v):
    return (low(v), None)

def low_pass(kept, grad):
    return (grad,)

def back_keep(v):
    return (v, None)

def back_low(kept, grad):
    return (low(grad),)
low.defvjp(low_keep, low_pass)
low_back.defvjp(back_keep, back_low)
epsilon = 1e-05
masked_score = -1e+30

def exact_dot(left, right):
    return jnp.dot(left, right, precision=lax.Precision.HIGHEST)

def normalize(inputs, gain):
    centred = inputs - lax.optimization_barrier(jnp.mean(inputs, -1, keepdims=True))
    inverse = lax.rsqrt(lax.optimization_barrier(jnp.mean(centred * centred, -1, keepdims=True)) + epsilon)
    return centred * inverse * gain

def angles(positions, head_size):
    half_size = head_size // 2
    freqs = 10000.0 ** (-jnp.arange(half_size).astype(jnp.float32) / half_size)
    phase = positions.astype(jnp.float32)[:, None] * freqs[None, :]
    return (jnp.cos(phase)[:, None, :], jnp.sin(phase)[:, None, :])

def rotate(inputs, cosine, sine):
    half_size = inputs.shape[-1] // 2
    leading = inputs[..., :half_size]
    trailing = inputs[..., half_size:]
    return jnp.concatenate([leading * cosine - trailing * sine, leading * sine + trailing * cosine], -1)

def layer_block(inputs, gain_attn, w_qkv, w_out, gain_ffn, w_up, w_down):
    length = inputs.shape[0]
    where_at = jnp.arange(length)
    cosine, sine = angles(where_at, DH)
    normed_attn = low(normalize(inputs, gain_attn))
    joined = low_back(exact_dot(normed_attn, w_qkv)).reshape(length, 3, H, DH)
    queries = low(rotate(joined[:, 0], cosine, sine) * DH ** (-0.5))
    keys = low(rotate(joined[:, 1], cosine, sine))
    values = low(joined[:, 2])
    scores = low_back(jnp.einsum('qhd,khd->hqk', queries, keys, precision=lax.Precision.HIGHEST))
    allowed = where_at[None, :] <= where_at[:, None]
    scores = jnp.where(allowed[None], scores, masked_score)
    probs = low(jax.nn.softmax(scores, axis=-1))
    mixed = jnp.einsum('hqk,khd->qhd', probs, values, precision=lax.Precision.HIGHEST).reshape(length, D)
    mixed = low(low_back(mixed))
    middle = inputs + low_back(exact_dot(mixed, w_out))
    normed_ffn = low(normalize(middle, gain_ffn))
    hidden = low_back(exact_dot(normed_ffn, w_up))
    active = low(jax.nn.gelu(hidden, approximate=True))
    return middle + low_back(exact_dot(active, w_down))

def run_rows(inputs, params, index):

    def one_row(row):
        return layer_block(row, *[member[index] for member in params])
    return lax.map(jax.checkpoint(one_row), inputs)

def forward(inputs, gain_attn, w_qkv, w_out, gain_ffn, w_up, w_down, w_pool):
    params = (gain_attn, w_qkv, w_out, gain_ffn, w_up, w_down)
    first = run_rows(inputs, params, 0)
    length = first.shape[1]
    shifted = jnp.pad(first, ((0, 0), (2, 0), (0, 0)))[:, :length]
    grouped = low(shifted.reshape(first.shape[0], length // 3, 3 * D))
    pooled = low_back(jnp.einsum('rtc,cd->rtd', grouped, w_pool, precision=lax.Precision.HIGHEST))
    second = run_rows(pooled, params, 1)
    return (first, second)

def reference(tokens, loss_mask, cotangent, embed, gain_attn, w_qkv, w_out, gain_ffn, w_up, w_down, w_pool):

    def widen(array):
        return array.astype(jnp.float32)
    table = widen(embed)
    inputs, embed_back = jax.vjp(lambda source: jnp.take(source, tokens, axis=0), table)
    (first, second), back = jax.vjp(forward, inputs, widen(gain_attn), widen(w_qkv), widen(w_out), widen(gain_ffn), widen(w_up), widen(w_down), widen(w_pool))
    start_grad = widen(cotangent) * loss_mask.astype(jnp.float32)[..., None]
    grads = back((jnp.zeros_like(first), start_grad))
    embed_grad, = embed_back(grads[0])
    return (first.astype(jnp.bfloat16), second.astype(jnp.bfloat16), grads[0], embed_grad, grads[1], grads[2], grads[3], grads[4], grads[5], grads[6], grads[7])
```

```python
import jax
import jax.numpy as jnp
from jax import lax
from jax.sharding import PartitionSpec as P

D = 512
H = 8
DH = 64

epsilon = 1e-05
masked_score = -1e30
AXES = ("seq", "batch")


def matmul(left, right):
    return jnp.dot(left, right, preferred_element_type=jnp.float32)


def left_grad(left, grad):
    return lax.dot_general(left, grad, (((0,), (0,)), ((), ())), preferred_element_type=jnp.float32)


def right_grad(grad, weight):
    return lax.dot_general(
        grad, weight, (((1,), (1,)), ((), ())), preferred_element_type=jnp.float32
    )


class Plan:
    def __init__(self, rows):
        self.S = lax.axis_size("seq")
        self.B = lax.axis_size("batch")
        self.R = rows
        self.P = self.S // rows
        self.s = lax.axis_index("seq")
        self.b = lax.axis_index("batch")
        line = self.s * 2 + self.b % 2
        self.h = line % self.P
        self.row = (line // self.P) % self.R
        self.part = self.s // self.P

    def pairs(self):
        for pair in range(self.B // 2):
            for core in range(2):
                for part in range(self.R):
                    for member in range(self.P):
                        yield pair, core, part, member

    def worker(self, pair, core, row, member):
        line = (core * self.R + row) * self.P + member
        return (line // 2) * self.B + 2 * pair + line % 2

    def home(self, pair, core, part, member):
        return (self.P * part + member) * self.B + 2 * pair + core

    def to_worker(self, held):
        got = []
        for step in range(self.R):
            perm = [
                (self.home(p, c, i, h), self.worker(p, c, (step + i) % self.R, h))
                for p, c, i, h in self.pairs()
            ]
            piece = lax.dynamic_index_in_dim(held, (step + self.part) % self.R, 0, keepdims=False)
            got.append(lax.ppermute(piece, AXES, perm))
        got = jnp.stack(got[::-1] + got[::-1])
        return lax.dynamic_slice_in_dim(got, (self.R - 1 - self.row) % self.R, self.R, 0)

    def to_home(self, made):
        got = []
        for step in range(self.R):
            perm = [
                (self.worker(p, c, (step + i) % self.R, h), self.home(p, c, i, h))
                for p, c, i, h in self.pairs()
            ]
            piece = lax.dynamic_index_in_dim(made, (self.row - step) % self.R, 0, keepdims=False)
            got.append(lax.ppermute(piece, AXES, perm))
        got = jnp.stack(got + got)
        return lax.dynamic_slice_in_dim(got, (self.R - self.part) % self.R, self.R, 0)

    def shift(self, value, by):
        perm = []
        for pair, core, row, member in self.pairs():
            perm.append((
                self.worker(pair, core, row, member),
                self.worker(pair, core, row, (member + by) % self.P),
            ))
        return lax.ppermute(value, AXES, perm)

    def others(self, value):
        return [self.shift(value, by) for by in range(1, self.P)]

    def swap(self, value, axis, bit):
        count = lax.axis_size(axis)
        return lax.ppermute(value, axis, [(n, n ^ bit) for n in range(count)])

    def bits(self, axis):
        count = lax.axis_size(axis)
        return [1 << n for n in range(count.bit_length() - 1)]

    def reduce_scatter(self, blocks, order):
        nb, ns = len(self.bits("batch")), len(self.bits("seq"))
        rest = blocks.shape[2:]
        value = blocks.astype(jnp.bfloat16).reshape((2,) * (nb + ns) + rest)
        dims = [("batch", 1 << (nb - 1 - n)) for n in range(nb)]
        dims += [("seq", 1 << (ns - 1 - n)) for n in range(ns)]
        for axis, bit in order:
            where = dims.index((axis, bit))
            dims.pop(where)
            index = self.b if axis == "batch" else self.s
            mine = (index // bit) % 2
            keep = lax.dynamic_index_in_dim(value, mine, where, keepdims=False)
            send = lax.dynamic_index_in_dim(value, 1 - mine, where, keepdims=False)
            total = keep.astype(jnp.float32) + self.swap(send, axis, bit).astype(jnp.float32)
            value = total if not dims else total.astype(jnp.bfloat16)
        return value

    def all_sum(self, value):
        for axis in ("batch", "seq"):
            for bit in self.bits(axis):
                value = value + self.swap(value, axis, bit)
        return value


def normalize(inputs, gain):
    centred = inputs - jnp.mean(inputs, -1, keepdims=True)
    inverse = lax.rsqrt(jnp.mean(centred * centred, -1, keepdims=True) + epsilon)
    normed = centred * inverse
    return ((normed * gain).astype(jnp.bfloat16), normed, inverse)


def normalize_back(grad, normed, inverse, gain):
    scaled = grad * gain
    result = inverse * (
        scaled
        - jnp.mean(scaled, -1, keepdims=True)
        - normed * jnp.mean(scaled * normed, -1, keepdims=True)
    )
    return (result, jnp.sum(grad * normed, axis=0, keepdims=True))


def angles(positions):
    half_size = DH // 2
    freqs = 10000.0 ** (-jnp.arange(half_size).astype(jnp.float32) / half_size)
    phase = positions.astype(jnp.float32)[:, None] * freqs[None, :]
    cosine, sine = jnp.cos(phase), jnp.sin(phase)
    return (jnp.concatenate([cosine] * 4, 1), jnp.concatenate([-sine, sine] * 2, 1))


def rotate(inputs, cosine, sine):
    count = inputs.shape[1] // 128
    lanes = lax.broadcasted_iota(jnp.int32, inputs.shape, 1)
    other = jnp.where(lanes % 64 < 32, jnp.roll(inputs, -32, 1), jnp.roll(inputs, 32, 1))
    return inputs * jnp.concatenate([cosine] * count, 1) + other * jnp.concatenate([sine] * count, 1)


def pre_attention(inputs, gain, w_qkv, cosine, sine):
    low, unused, unused2 = normalize(inputs, gain)
    joined = matmul(low, w_qkv)
    queries = (rotate(joined[:, :D], cosine, sine) * DH ** (-0.5)).astype(jnp.bfloat16)
    keys = rotate(joined[:, D : 2 * D], cosine, sine).astype(jnp.bfloat16)
    values = joined[:, 2 * D :].astype(jnp.bfloat16)
    return (queries, jnp.stack([keys, values]))


def visible(member, members, span):
    rows = lax.broadcasted_iota(jnp.int32, (span, members * span), 0)
    columns = lax.broadcasted_iota(jnp.int32, (span, members * span), 1)
    other = (member - columns // span + members) % members
    own = columns <= rows
    return jnp.where(columns < span, own, other < member)


def gathered(own, others, parts, index):
    pieces = [value[index].reshape(parts, -1, D) for value in [own] + others]
    return jnp.stack(pieces, 1)


def heads(value):
    return value.reshape(-1, H, DH)


def attention(queries, own, others, parts, seen):
    span = queries.shape[0] // parts
    keys, values = gathered(own, others, parts, 0), gathered(own, others, parts, 1)
    width = keys.shape[1] * span
    mixed, logsum = [], []
    for part in range(parts):
        query = heads(queries[part * span : (part + 1) * span])
        key = heads(keys[: part + 1].reshape(-1, D))
        value = heads(values[: part + 1].reshape(-1, D))
        scores = jnp.einsum("qhd,khd->hqk", query, key, preferred_element_type=jnp.float32)
        last = jnp.where(seen[None], scores[..., part * width :], masked_score)
        scores = jnp.concatenate([scores[..., : part * width], last], -1)
        highest = jnp.max(scores, -1, keepdims=True)
        expon = jnp.exp(scores - highest)
        totals = jnp.sum(expon, -1, keepdims=True)
        probs = (expon / totals).astype(jnp.bfloat16)
        mixed.append(
            jnp.einsum("hqk,khd->qhd", probs, value, preferred_element_type=jnp.float32).reshape(span, D)
        )
        logsum.append((highest + jnp.log(totals))[..., 0])
    return (jnp.concatenate(mixed).astype(jnp.bfloat16), logsum)


def attention_back(queries, own, others, parts, seen, mixed, logsum, grad_mixed):
    span = queries.shape[0] // parts
    keys, values = gathered(own, others, parts, 0), gathered(own, others, parts, 1)
    members = keys.shape[1]
    width = members * span
    grad_queries = []
    grad_keys = jnp.zeros((parts * width, H, DH), jnp.float32)
    grad_values = jnp.zeros((parts * width, H, DH), jnp.float32)
    for part in range(parts):
        rows = slice(part * span, (part + 1) * span)
        query, grad = heads(queries[rows]), heads(grad_mixed[rows])
        key = heads(keys[: part + 1].reshape(-1, D))
        value = heads(values[: part + 1].reshape(-1, D))
        scores = jnp.einsum("qhd,khd->hqk", query, key, preferred_element_type=jnp.float32)
        last = jnp.where(seen[None], scores[..., part * width :], masked_score)
        scores = jnp.concatenate([scores[..., : part * width], last], -1)
        probs = jnp.exp(scores - logsum[part][..., None])
        grad_probs = jnp.einsum("qhd,khd->hqk", grad, value, preferred_element_type=jnp.float32)
        delta = jnp.sum(
            grad.astype(jnp.float32) * heads(mixed[rows]).astype(jnp.float32), -1
        ).T[..., None]
        grad_scores = (probs * (grad_probs - delta)).astype(jnp.bfloat16)
        grad_queries.append(
            jnp.einsum("hqk,khd->qhd", grad_scores, key, preferred_element_type=jnp.float32).reshape(span, D)
        )
        seen_keys = (part + 1) * width
        grad_keys = grad_keys.at[:seen_keys].add(
            jnp.einsum("hqk,qhd->khd", grad_scores, query, preferred_element_type=jnp.float32)
        )
        grad_values = grad_values.at[:seen_keys].add(
            jnp.einsum("hqk,qhd->khd", probs.astype(jnp.bfloat16), grad, preferred_element_type=jnp.float32)
        )
    both = jnp.stack([grad_keys, grad_values]).astype(jnp.bfloat16)
    both = both.reshape(2, parts, members, span, D)
    pieces = [both[:, :, member].reshape(2, parts * span, D) for member in range(members)]
    return (jnp.concatenate(grad_queries).astype(jnp.bfloat16), pieces)


def post_attention(inputs, mixed, weights):
    gain_attn, w_qkv, w_out, gain_ffn, w_up, w_down = weights
    middle = inputs + matmul(mixed, w_out)
    low, unused, unused2 = normalize(middle, gain_ffn)
    hidden = matmul(low, w_up)
    active = jax.nn.gelu(hidden, approximate=True).astype(jnp.bfloat16)
    output = middle + matmul(active, w_down)
    return (output.astype(jnp.bfloat16), middle, hidden.astype(jnp.bfloat16))


def gelu_both(hidden):
    scale = 0.7978845608028654
    square = hidden * hidden
    tanh = jnp.tanh(scale * hidden * (1.0 + 0.044715 * square))
    active = 0.5 * hidden * (1.0 + tanh)
    slope = 0.5 * (1.0 + tanh) + 0.5 * hidden * (1.0 - tanh * tanh) * scale * (
        1.0 + 3.0 * 0.044715 * square
    )
    return (active, slope)


def post_attention_back(grad_out, mixed, middle, hidden, weights):
    gain_attn, w_qkv, w_out, gain_ffn, w_up, w_down = weights
    low, normed, inverse = normalize(middle, gain_ffn)
    grad_low = grad_out.astype(jnp.bfloat16)
    active, slope = gelu_both(hidden.astype(jnp.float32))
    grad_down = left_grad(grad_low, active.astype(jnp.bfloat16))
    grad_hidden = (right_grad(grad_low, w_down) * slope).astype(jnp.bfloat16)
    grad_up = left_grad(low, grad_hidden)
    grad_norm, grad_gain = normalize_back(right_grad(grad_hidden, w_up), normed, inverse, gain_ffn)
    grad_middle = grad_out + grad_norm
    grad_branch = grad_middle.astype(jnp.bfloat16)
    grad_w_out = left_grad(grad_branch, mixed)
    grad_mixed = right_grad(grad_branch, w_out).astype(jnp.bfloat16)
    return (grad_middle, grad_mixed, grad_down, grad_up, grad_w_out, grad_gain)


def pre_attention_back(inputs, grad_queries, grad_own, grad_others, grad_middle, cosine, sine, weights):
    gain_attn, w_qkv, w_out, gain_ffn, w_up, w_down = weights
    low, normed, inverse = normalize(inputs, gain_attn)
    total = sum([member.astype(jnp.float32) for member in grad_others], grad_own.astype(jnp.float32))
    grad_joined = jnp.concatenate(
        [
            rotate(grad_queries.astype(jnp.float32) * DH ** (-0.5), cosine, -sine),
            rotate(total[0], cosine, -sine),
            total[1],
        ],
        1,
    ).astype(jnp.bfloat16)
    grad_w_qkv = left_grad(grad_joined, low)
    grad_norm, grad_gain = normalize_back(right_grad(grad_joined, w_qkv), normed, inverse, gain_attn)
    return (grad_middle + grad_norm, grad_w_qkv, grad_gain)


def blocked(value, outer, inner, swapped):
    rows, columns = value.shape
    if swapped:
        return value.reshape(inner, rows // inner, outer, columns // outer).transpose(2, 0, 1, 3)
    return value.reshape(outer, rows // outer, inner, columns // inner).transpose(0, 2, 1, 3)


def body(
    tokens, loss_mask, cotangent, embed, gain_attn, w_qkv, w_out, gain_ffn, w_up, w_down, w_pool
):
    plan = Plan(tokens.shape[0])
    rows, span = tokens.shape
    short = loss_mask.shape[1]
    members = plan.P
    vocab = embed.shape[0]
    params = (gain_attn, w_qkv, w_out, gain_ffn, w_up, w_down)
    first_weights = tuple((member[0] for member in params))
    second_weights = tuple((member[1] for member in params))

    my_tokens = plan.to_worker(tokens).reshape(rows * span)
    start_grad = plan.to_worker(cotangent * loss_mask.astype(jnp.bfloat16)[..., None]).reshape(-1, D)

    def places(length):
        block = jnp.arange(rows, dtype=jnp.int32)[:, None] * members + plan.h
        return (block * length + jnp.arange(length, dtype=jnp.int32)[None]).reshape(-1)

    first_angles, second_angles = angles(places(span)), angles(places(short))
    first_seen = visible(plan.h, members, span)
    second_seen = visible(plan.h, members, short)

    onehot = (my_tokens[:, None] == jnp.arange(vocab, dtype=jnp.int32)).astype(jnp.bfloat16)
    inputs = matmul(onehot, embed)

    def forward(value, angle, seen, weights):
        queries, own = pre_attention(value, weights[0], weights[1], *angle)
        others = plan.others(own)
        mixed, logsum = attention(queries, own, others, rows, seen)
        output, middle, hidden = post_attention(value, mixed, weights)
        return (output, (queries, own, others, mixed, logsum, middle, hidden))

    def backward(value, grad_out, kept, angle, seen, weights):
        queries, own, others, mixed, logsum, middle, hidden = kept
        grad_middle, grad_mixed, grad_down, grad_up, grad_w_out, grad_gain_ffn = post_attention_back(
            grad_out, mixed, middle, hidden, weights
        )
        grad_queries, pieces = attention_back(
            queries, own, others, rows, seen, mixed, logsum, grad_mixed
        )
        grad_others = [plan.shift(pieces[by], -by) for by in range(1, members)]
        grad_inputs, grad_qkv, grad_gain_attn = pre_attention_back(
            value, grad_queries, pieces[0], grad_others, grad_middle, *angle, weights
        )
        return (grad_inputs, (grad_qkv, grad_w_out, grad_up, grad_down), grad_gain_attn, grad_gain_ffn)

    first_low, first_kept = forward(inputs, first_angles, first_seen, first_weights)
    first_blocks = first_low.reshape(rows, span, D)
    full_out = plan.to_home(first_blocks)

    edge = plan.shift(first_blocks[:, span - 2 :], 1)
    late = jnp.concatenate([jnp.zeros_like(edge[:1]), edge[:-1]], 0)
    edge = jnp.where(plan.h == 0, late, edge)
    shifted = jnp.concatenate([edge, first_blocks[:, : span - 2]], 1)
    grouped = shifted.reshape(rows * short, 3 * D)
    pooled = matmul(grouped, w_pool)

    second_low, second_kept = forward(pooled, second_angles, second_seen, second_weights)
    short_out = plan.to_home(second_low.reshape(rows, short, D))

    grad_pooled, second_grads, gain_attn_1, gain_ffn_1 = backward(
        pooled, start_grad.astype(jnp.float32), second_kept, second_angles, second_seen, second_weights
    )
    grad_pooled_low = grad_pooled.astype(jnp.bfloat16)
    grad_pool = left_grad(grad_pooled_low, grouped)
    grad_shifted = right_grad(grad_pooled_low, w_pool).reshape(rows, span, D)
    carried = plan.shift(grad_shifted[:, :2], -1)
    early = jnp.concatenate([carried[1:], jnp.zeros_like(carried[:1])], 0)
    carried = jnp.where(plan.h == members - 1, early, carried)
    grad_first = jnp.concatenate([grad_shifted[:, 2:], carried], 1).reshape(rows * span, D)

    grad_inputs, first_grads, gain_attn_0, gain_ffn_0 = backward(
        inputs, grad_first, first_kept, first_angles, first_seen, first_weights
    )
    input_grad = plan.to_home(grad_inputs.astype(jnp.bfloat16).reshape(rows, span, D))
    grad_embed = left_grad(grad_inputs.astype(jnp.bfloat16), onehot)

    order = [("batch", bit) for bit in plan.bits("batch")] + [("seq", bit) for bit in plan.bits("seq")]

    def reduced(value, swapped):
        total = plan.reduce_scatter(blocked(value, plan.B, plan.S, swapped), order)
        return total.T if swapped else total

    def stacked(number, swapped):
        return jnp.stack([reduced(first_grads[number], swapped), reduced(second_grads[number], swapped)])

    gains = plan.all_sum(jnp.concatenate([gain_attn_0, gain_attn_1, gain_ffn_0, gain_ffn_1]))
    return (
        full_out,
        short_out,
        input_grad.astype(jnp.float32),
        reduced(grad_embed, True),
        gains[:2],
        stacked(0, True),
        stacked(1, True),
        gains[2:],
        stacked(2, False),
        stacked(3, True),
        reduced(grad_pool, True),
    )


def solution(mesh):
    in_specs = (
        P("batch", "seq"),
        P("batch", "seq"),
        P("batch", "seq", None),
        P(),
        P(),
        P(),
        P(),
        P(),
        P(),
        P(),
        P(),
    )
    out_specs = (
        P("batch", "seq", None),
        P("batch", "seq", None),
        P("batch", "seq", None),
        P("batch", "seq"),
        P(),
        P(None, "batch", "seq"),
        P(None, "batch", "seq"),
        P(),
        P(None, "batch", "seq"),
        P(None, "batch", "seq"),
        P("batch", "seq"),
    )
    return jax.shard_map(body, mesh=mesh, in_specs=in_specs, out_specs=out_specs, check_vma=False)
```

```python
import functools

import jax
import jax.numpy as jnp
from jax import lax
from jax.experimental import pallas as pl
from jax.experimental.pallas import tpu as pltpu
from jax.sharding import PartitionSpec as P

D = 512
H = 8
DH = 64

epsilon = 1e-05
masked_score = -1e30
AXES = ("seq", "batch")


VOCAB = 256
BF16 = jnp.bfloat16
F32 = jnp.float32
ANYWHERE = pl.BlockSpec(memory_space=pl.ANY)
ROOM = 56 * 1024 * 1024


def dot(left, right):
    return jnp.dot(left, right, preferred_element_type=F32)


def dot_nt(left, right):
    return lax.dot_general(left, right, (((1,), (1,)), ((), ())), preferred_element_type=F32)


def iota(shape, dim):
    return lax.broadcasted_iota(jnp.int32, shape, dim)


def picks(condition):
    return jnp.where(condition, 1.0, 0.0).astype(BF16)


def call(kernel, out_shape, grid, in_specs, out_specs, scratch=(), scalars=0, flops=0, after=()):
    held = scalars + len(in_specs)

    def inner(*refs):
        kernel(*refs[:held], *refs[held + len(after) :])

    made = pl.pallas_call(
        inner,
        out_shape=out_shape,
        grid_spec=pltpu.PrefetchScalarGridSpec(
            num_scalar_prefetch=scalars,
            grid=grid,
            in_specs=in_specs + [ANYWHERE] * len(after),
            out_specs=out_specs,
            scratch_shapes=scratch,
        ),
        compiler_params=pltpu.CompilerParams(vmem_limit_bytes=ROOM),
        cost_estimate=pl.CostEstimate(flops=flops, bytes_accessed=flops // 300, transcendentals=0),
    )
    return lambda *operands: made(*operands, *after)


def shape(dims, dtype):
    return jax.ShapeDtypeStruct(dims, dtype)


def fixed(block, index=None, buffers=1):
    place = index or (0,) * len(block)
    return pl.BlockSpec(block, lambda *unused: place, pipeline_mode=pl.Buffered(buffers))


def gain_row(ref, layer):
    return ref[...].astype(F32)[layer : layer + 1]


def normalize(inputs, gain):
    centred = inputs - jnp.mean(inputs, -1, keepdims=True)
    inverse = lax.rsqrt(jnp.mean(centred * centred, -1, keepdims=True) + epsilon)
    normed = centred * inverse
    return ((normed * gain).astype(BF16), normed, inverse)


def normalize_back(grad, normed, inverse, gain):
    scaled = grad * gain
    result = inverse * (
        scaled
        - jnp.mean(scaled, -1, keepdims=True)
        - normed * jnp.mean(scaled * normed, -1, keepdims=True)
    )
    return (result, jnp.sum(grad * normed, axis=0, keepdims=True))


def rotate(inputs, cosine, sine):
    width = inputs.shape[1]
    count = width // 128
    first = iota(inputs.shape, 1) % DH < DH // 2
    other = jnp.where(
        first, pltpu.roll(inputs, width - DH // 2, 1), pltpu.roll(inputs, DH // 2, 1)
    )
    return inputs * jnp.concatenate([cosine] * count, 1) + other * jnp.concatenate([sine] * count, 1)


def gelu_both(hidden):
    scale = 0.7978845608028654
    square = hidden * hidden
    tanh = jnp.tanh(scale * hidden * (1.0 + 0.044715 * square))
    half = 0.5 + 0.5 * tanh
    slope = half + (0.5 * scale) * hidden * (1.0 - tanh * tanh) * (1.0 + 0.134145 * square)
    return (hidden * half, slope)


def layout(blocks):
    starts, at = [], 0
    for deep, wide in blocks:
        starts.append(at)
        at += deep * -(-wide // 128)
    return starts, at


def slot_of(order, axis, apart):
    slot = 0
    for place, (name, bit) in enumerate(order):
        if name == axis:
            slot = slot + ((apart // bit) % 2) * (1 << (len(order) - 1 - place))
    return slot


def put(packed, slot, start, block):
    deep, wide = block.shape
    half = packed.shape[1]
    for tile in range(-(-wide // 128)):
        piece = block[:, tile * 128 : min(wide, (tile + 1) * 128)]
        packed[slot // half, slot % half, start + tile * deep : start + (tile + 1) * deep, : piece.shape[1]] = piece


def put_all(packed, order, me, start, made, deep, wide, swapped):
    rows, columns = made.shape
    for line in range(rows // deep):
        for column in range(columns // wide):
            batch, seq = (column, line) if swapped else (line, column)
            slot = slot_of(order, "batch", batch ^ me[1]) + slot_of(order, "seq", seq ^ me[2])
            put(packed, slot, start, made[line * deep : (line + 1) * deep, column * wide : (column + 1) * wide])


def hand_out(packed, stays, leaves, sems):
    copies = [pltpu.make_async_copy(packed.at[n], out, sems.at[n]) for n, out in enumerate((stays, leaves))]
    for copy in copies:
        copy.start()
    for copy in copies:
        copy.wait()


def packed_scratch(batches, seqs, rows):
    return [pltpu.VMEM((2, batches * seqs // 2, rows, 128), BF16), pltpu.SemaphoreType.DMA((2,))]


def packed_shapes(batches, seqs, rows):
    return (shape((batches * seqs // 2, rows, 128), BF16),) * 2


def embed_kernel(layer, tokens, embed, gain, w_qkv, cosine, sine, inputs, low, both):
    part = pl.program_id(0)

    @pl.when(part == 0)
    def first():
        onehot = picks(tokens[...] == iota((tokens.shape[0], embed.shape[0]), 1))
        value = dot(onehot, embed[...])
        inputs[...] = value.astype(BF16)
        low[...] = normalize(value, gain_row(gain, layer))[0]

    joined = dot(low[...], w_qkv[0])

    @pl.when(part == 0)
    def keys():
        both[0] = rotate(joined, cosine[...], sine[...]).astype(BF16)

    @pl.when(part == 1)
    def values():
        both[0] = joined.astype(BF16)


def embed_call(layer, tokens, embed, gain, w_qkv, cosine, sine, after=()):
    count = tokens.shape[0]
    return call(
        functools.partial(embed_kernel, layer),
        (shape((count, D), BF16), shape((count, D), BF16), shape((2, count, D), BF16)),
        grid=(2,),
        in_specs=[
            fixed(tokens.shape),
            fixed(embed.shape),
            fixed(gain.shape),
            pl.BlockSpec((1, D, D), lambda part: (layer, 0, part + 1)),
            fixed(cosine.shape),
            fixed(sine.shape),
        ],
        out_specs=(
            fixed((count, D)),
            fixed((count, D)),
            pl.BlockSpec((1, count, D), lambda part: (part, 0, 0)),
        ),
        flops=2 * count * D * (2 * D + embed.shape[0]),
        after=after,
    )(tokens, embed, gain, w_qkv, cosine, sine)


def query_kernel(low, w_qkv, cosine, sine, queries):
    joined = dot(low[...], w_qkv[0])
    queries[...] = (rotate(joined, cosine[...], sine[...]) * DH ** (-0.5)).astype(BF16)


def query_call(layer, low, w_qkv, cosine, sine, after=()):
    count = low.shape[0]
    return call(
        query_kernel,
        shape((count, D), BF16),
        grid=(1,),
        in_specs=[
            fixed((count, D)),
            fixed((1, D, D), (layer, 0, 0)),
            fixed(cosine.shape),
            fixed(sine.shape),
        ],
        out_specs=fixed((count, D)),
        flops=2 * count * D * D,
        after=after,
    )(low, w_qkv, cosine, sine)


def pool_kernel(layer, rows, members, me, first, edge, w_pool, gain, w_qkv, cosine, sine, grouped, pooled, low, both):
    span = first.shape[0] // rows
    count = pooled.shape[0]
    short = count // rows
    late = jnp.where(me[0] == 0, 1, 0)
    total = jnp.zeros((count, D), F32)
    for third in range(3):
        pick = picks(iota((short, span), 1) == 3 * iota((short, span), 0) + third - 2)
        piece = jnp.concatenate(
            [dot(pick, first[row * span : (row + 1) * span, :]) for row in range(rows)], 0
        )
        if third < 2:
            place = iota((count, 2 * rows), 0) == (iota((count, 2 * rows), 1) // 2 + late) * short
            place = picks(place & (iota((count, 2 * rows), 1) % 2 == third))
            piece = piece + dot(place, edge[...])
        piece = piece.astype(BF16)
        grouped[:, third * D : (third + 1) * D] = piece
        total = total + dot(piece, w_pool[third * D : (third + 1) * D, :])
    pooled[...] = total
    low[...] = normalize(total, gain_row(gain, layer))[0]
    both[0] = rotate(dot(low[...], w_qkv[0, :, D : 2 * D]), cosine[...], sine[...]).astype(BF16)
    both[1] = dot(low[...], w_qkv[0, :, 2 * D :]).astype(BF16)


def pool_call(layer, rows, members, me, first, edge, w_pool, gain, w_qkv, cosine, sine, after=()):
    count = cosine.shape[0]
    return call(
        functools.partial(pool_kernel, layer, rows, members),
        (
            shape((count, 3 * D), BF16),
            shape((count, D), F32),
            shape((count, D), BF16),
            shape((2, count, D), BF16),
        ),
        grid=(1,),
        scalars=1,
        in_specs=[
            fixed(first.shape),
            fixed(edge.shape),
            fixed(w_pool.shape),
            fixed(gain.shape),
            fixed((1, D, 3 * D), (layer, 0, 0)),
            fixed(cosine.shape),
            fixed(sine.shape),
        ],
        out_specs=(fixed((count, 3 * D)), fixed((count, D)), fixed((count, D)), fixed((2, count, D))),
        flops=2 * count * D * 5 * D,
        after=after,
    )(me, first, edge, w_pool, gain, w_qkv, cosine, sine)


GROUP = 256
HEADS = GROUP // DH


def fill_keys(rows, members, own, others, keys, values):
    span = own.shape[1] // rows
    for row in range(rows):
        for by, source in enumerate([own, *others]):
            start = (row * members + by) * span
            keys[start : start + span, :] = source[0, row * span : (row + 1) * span, :]
            values[start : start + span, :] = source[1, row * span : (row + 1) * span, :]


def fill_bias(member, members, span, bias):
    line = iota((span, members * span), 0)
    column = iota((span, members * span), 1)
    other = (member + column // span) % members < member
    seen = ((column < span) & (column <= line)) | ((column >= span) & other)
    bias[...] = jnp.where(seen, 0.0, masked_score)


def score(query, keys, bias, start, end):
    scores = dot_nt(query, keys[0:end, :])
    last = scores[:, start:] + bias[...]
    return jnp.concatenate([scores[:, :start], last], 1) if start else last


def attention_kernel(rows, members, me, queries, own, *refs):
    others = refs[: members - 1]
    mixed, logsum, keys, values, bias, total = refs[members - 1 :]
    span = queries.shape[0] // rows
    width = members * span
    fill_keys(rows, members, own, others, keys, values)
    fill_bias(me[0], members, span, bias)
    logsum[...] = jnp.zeros_like(logsum)

    def one_head(head, unused):
        lanes = iota((1, GROUP), 1) // DH == head
        mask = picks(lanes)
        for row in range(rows):
            block = slice(row * span, (row + 1) * span)
            start, end = row * width, (row + 1) * width
            scores = score(queries[block, :] * mask, keys, bias, start, end)
            highest = jnp.max(scores, -1, keepdims=True)
            expon = jnp.exp(scores - highest)
            totals = jnp.sum(expon, -1, keepdims=True)
            out = dot(expon.astype(BF16), values[0:end, :]) / totals
            total[block, :] = jnp.where(lanes, out, total[block, :])
            logsum[0, block, :] = jnp.where(
                iota((span, 128), 1) == head, highest + jnp.log(totals), logsum[0, block, :]
            )
        return unused

    lax.fori_loop(0, HEADS, one_head, 0)
    mixed[...] = total[...].astype(BF16)


def lane_group(ndim, block):
    return pl.BlockSpec(block, lambda group, *unused: (0,) * (ndim - 1) + (group,))


def attention_call(rows, members, me, queries, own, others, after=()):
    count = queries.shape[0]
    span = count // rows
    every = members * count
    pairs = rows * (rows + 1) // 2 * members * span * span
    return call(
        functools.partial(attention_kernel, rows, members),
        (shape((count, D), BF16), shape((D // GROUP, count, 128), F32)),
        grid=(D // GROUP,),
        scalars=1,
        in_specs=[lane_group(2, (count, GROUP))] + [lane_group(3, (2, count, GROUP))] * members,
        out_specs=(
            lane_group(2, (count, GROUP)),
            pl.BlockSpec((1, count, 128), lambda group, *unused: (group, 0, 0)),
        ),
        scratch=[
            pltpu.VMEM((every, GROUP), BF16),
            pltpu.VMEM((every, GROUP), BF16),
            pltpu.VMEM((span, members * span), F32),
            pltpu.VMEM((count, GROUP), F32),
        ],
        flops=16 * pairs * D,
        after=after,
    )(me, queries, own, *others)


def attention_back_kernel(rows, members, me, queries, own, *refs):
    others = refs[: members - 1]
    mixed, logsum, grad_mixed, grad_queries, *rest = refs[members - 1 :]
    pieces = rest[:members]
    keys, values, bias, turned, turned_grad, grad_keys, grad_values, total = rest[members:]
    span = queries.shape[0] // rows
    width = members * span
    fill_keys(rows, members, own, others, keys, values)
    fill_bias(me[0], members, span, bias)
    for row in range(rows):
        block = slice(row * span, (row + 1) * span)
        turned[row] = queries[block, :].T
        turned_grad[row] = grad_mixed[block, :].T

    def one_head(head, unused):
        lanes = iota((1, GROUP), 1) // DH == head
        mask = picks(lanes)
        mine = pl.ds(pl.multiple_of(head * DH, DH), DH)
        for row in reversed(range(rows)):
            block = slice(row * span, (row + 1) * span)
            start, end = row * width, (row + 1) * width
            grad = grad_mixed[block, :] * mask
            summed = jnp.sum(
                jnp.where(iota((span, 128), 1) == head, logsum[0, block, :], 0.0), -1, keepdims=True
            )
            probs = jnp.exp(score(queries[block, :] * mask, keys, bias, start, end) - summed)
            delta = jnp.sum(grad.astype(F32) * mixed[block, :].astype(F32), -1, keepdims=True)
            grad_scores = (probs * (dot_nt(grad, values[0:end, :]) - delta)).astype(BF16)
            out = dot(grad_scores, keys[0:end, :])
            total[block, :] = jnp.where(lanes, out, total[block, :])
            part_keys = dot(turned[row, mine, :], grad_scores)
            part_values = dot(turned_grad[row, mine, :], probs.astype(BF16))
            if row == rows - 1:
                grad_keys[mine, 0:end] = part_keys
                grad_values[mine, 0:end] = part_values
            else:
                grad_keys[mine, 0:end] += part_keys
                grad_values[mine, 0:end] += part_values
        return unused

    lax.fori_loop(0, HEADS, one_head, 0)
    grad_queries[...] = total[...].astype(BF16)
    for number, source in enumerate((grad_keys, grad_values)):
        made = source[...].astype(BF16).T
        for row in range(rows):
            for by, piece in enumerate(pieces):
                start = (row * members + by) * span
                piece[number, row * span : (row + 1) * span, :] = made[start : start + span, :]


def attention_back_call(rows, members, me, queries, own, others, mixed, logsum, grad_mixed, after=()):
    count = queries.shape[0]
    span = count // rows
    every = members * count
    pairs = rows * (rows + 1) // 2 * members * span * span
    made = call(
        functools.partial(attention_back_kernel, rows, members),
        (shape((count, D), BF16),) + (shape((2, count, D), BF16),) * members,
        grid=(D // GROUP,),
        scalars=1,
        in_specs=[lane_group(2, (count, GROUP))]
        + [lane_group(3, (2, count, GROUP))] * members
        + [
            lane_group(2, (count, GROUP)),
            pl.BlockSpec((1, count, 128), lambda group, *unused: (group, 0, 0)),
            lane_group(2, (count, GROUP)),
        ],
        out_specs=(lane_group(2, (count, GROUP)),) + (lane_group(3, (2, count, GROUP)),) * members,
        scratch=[
            pltpu.VMEM((every, GROUP), BF16),
            pltpu.VMEM((every, GROUP), BF16),
            pltpu.VMEM((span, members * span), F32),
            pltpu.VMEM((rows, GROUP, span), BF16),
            pltpu.VMEM((rows, GROUP, span), BF16),
            pltpu.VMEM((GROUP, every), F32),
            pltpu.VMEM((GROUP, every), F32),
            pltpu.VMEM((count, GROUP), F32),
        ],
        flops=40 * pairs * D,
        after=after,
    )(me, queries, own, *others, mixed, logsum, grad_mixed)
    return (made[0], made[1:])


CHUNK = 512


def ffn_kernel(layer, rows, inputs, mixed, w_out, gain, w_up, w_down, output, edges, middle, hidden, low, total):
    part = pl.program_id(0)

    @pl.when(part == 0)
    def first():
        value = inputs[...].astype(F32) + dot(mixed[...], w_out[0])
        middle[...] = value
        total[...] = value
        low[...] = normalize(value, gain_row(gain, layer))[0]

    made = dot(low[...], w_up[0])
    hidden[...] = made.astype(BF16)
    total[...] += dot(gelu_both(made)[0].astype(BF16), w_down[0])

    @pl.when(part == pl.num_programs(0) - 1)
    def last():
        made = total[...].astype(BF16)
        output[...] = made
        count = made.shape[0]
        span = count // rows
        line = iota((2 * rows, count), 0)
        pick = picks(iota((2 * rows, count), 1) == (line // 2 + 1) * span - 2 + line % 2)
        edges[...] = dot(pick, made).astype(BF16)


def ffn_call(layer, rows, inputs, mixed, w_out, gain, w_up, w_down, after=()):
    count = inputs.shape[0]
    units = w_up.shape[2]
    return call(
        functools.partial(ffn_kernel, layer, rows),
        (
            shape((count, D), BF16),
            shape((2 * rows, D), BF16),
            shape((count, D), F32),
            shape((count, units), BF16),
        ),
        grid=(units // CHUNK,),
        in_specs=[
            fixed((count, D)),
            fixed((count, D)),
            fixed((1, D, D), (layer, 0, 0)),
            fixed(gain.shape),
            pl.BlockSpec((1, D, CHUNK), lambda part: (layer, 0, part)),
            pl.BlockSpec((1, CHUNK, D), lambda part: (layer, part, 0)),
        ],
        out_specs=(
            fixed((count, D)),
            fixed((2 * rows, D)),
            fixed((count, D)),
            pl.BlockSpec((count, CHUNK), lambda part: (0, part)),
        ),
        scratch=[pltpu.VMEM((count, D), BF16), pltpu.VMEM((count, D), F32)],
        flops=2 * count * D * (D + 2 * units),
        after=after,
    )(inputs, mixed, w_out, gain, w_up, w_down)


def ffn_blocks(batches, seqs, units):
    return ((D // batches, units // seqs), (D // seqs, units // batches), (D // seqs, D // batches))


def ffn_back_kernel(
    layer, rows, members, batches, seqs, order, carries,
    me, grad_ref, carried, mixed, middle, hidden, w_out, gain, w_up, w_down,
    stays, leaves, grad_gain, grad_middle, grad_mixed,
    low, turned_low, grad, turned_grad, total, packed, sems,
):
    part = pl.program_id(0)
    blocks = ffn_blocks(batches, seqs, CHUNK * pl.num_programs(0))
    starts, unused = layout(blocks)

    @pl.when(part == 0)
    def first():
        value = grad_ref[...]
        if carries:
            count = value.shape[0]
            span = count // rows
            early = jnp.where(me[0] == members - 1, 1, 0)
            line = iota((count, 2 * rows), 1)
            place = iota((count, 2 * rows), 0) == (line // 2 + 1 - early) * span - 2 + line % 2
            value = (value.astype(F32) + dot(picks(place), carried[...])).astype(BF16)
        grad[...] = value
        turned_grad[...] = value.T
        made = normalize(middle[...], gain_row(gain, layer))[0]
        low[...] = made
        turned_low[...] = made.T

    active, slope = gelu_both(hidden[...].astype(F32))
    grad_hidden = (dot_nt(grad[...], w_down[0]) * slope).astype(BF16)
    made = dot(turned_grad[...], active.astype(BF16)).astype(BF16)
    deep, wide = blocks[1]
    for column in range(CHUNK // wide):
        batch = slot_of(order, "batch", (part * (CHUNK // wide) + column) ^ me[1])
        for seq in range(seqs):
            slot = batch + slot_of(order, "seq", seq ^ me[2])
            put(packed, slot, starts[1], made[seq * deep : (seq + 1) * deep, column * wide : (column + 1) * wide])
    made = dot(turned_low[...], grad_hidden).astype(BF16)
    deep, wide = blocks[0]
    for column in range(CHUNK // wide):
        seq = slot_of(order, "seq", (part * (CHUNK // wide) + column) ^ me[2])
        for batch in range(batches):
            slot = seq + slot_of(order, "batch", batch ^ me[1])
            put(packed, slot, starts[0], made[batch * deep : (batch + 1) * deep, column * wide : (column + 1) * wide])
    made = dot_nt(grad_hidden, w_up[0])

    @pl.when(part == 0)
    def begin():
        total[...] = made

    @pl.when(part > 0)
    def add():
        total[...] += made

    @pl.when(part == pl.num_programs(0) - 1)
    def last():
        row = gain_row(gain, layer)
        unused, normed, inverse = normalize(middle[...], row)
        back, gain_sum = normalize_back(total[...], normed, inverse, row)
        grad_gain[...] = gain_sum
        value = grad[...].astype(F32) + back
        grad_middle[...] = value
        branch = value.astype(BF16)
        grad_mixed[...] = dot_nt(branch, w_out[0]).astype(BF16)
        put_all(packed, order, me, starts[2], dot(branch.T, mixed[...]).astype(BF16), *blocks[2], True)
        hand_out(packed, stays, leaves, sems)


def ffn_back_call(
    layer, rows, members, batches, seqs, order, me,
    grad, carried, mixed, middle, hidden, w_out, gain, w_up, w_down, after=()):
    count = grad.shape[0]
    units = w_up.shape[2]
    carries = carried is not None
    if not carries:
        carried = jnp.zeros((2 * rows, D), BF16)
    packs = layout(ffn_blocks(batches, seqs, units))[1]
    return call(
        functools.partial(ffn_back_kernel, layer, rows, members, batches, seqs, order, carries),
        packed_shapes(batches, seqs, packs)
        + (shape((1, D), F32), shape((count, D), F32), shape((count, D), BF16)),
        grid=(units // CHUNK,),
        scalars=1,
        in_specs=[
            fixed((count, D)),
            fixed((2 * rows, D)),
            fixed((count, D)),
            fixed((count, D)),
            pl.BlockSpec((count, CHUNK), lambda part, me: (0, part)),
            fixed((1, D, D), (layer, 0, 0)),
            fixed(gain.shape),
            pl.BlockSpec((1, D, CHUNK), lambda part, me: (layer, 0, part)),
            pl.BlockSpec((1, CHUNK, D), lambda part, me: (layer, part, 0)),
        ],
        out_specs=(ANYWHERE, ANYWHERE, fixed((1, D)), fixed((count, D)), fixed((count, D))),
        scratch=[
            pltpu.VMEM((count, D), BF16),
            pltpu.VMEM((D, count), BF16),
            pltpu.VMEM((count, D), BF16),
            pltpu.VMEM((D, count), BF16),
            pltpu.VMEM((count, D), F32),
        ]
        + packed_scratch(batches, seqs, packs),
        flops=2 * count * D * (2 * D + 4 * units),
        after=after,
    )(me, grad, carried, mixed, middle, hidden, w_out, gain, w_up, w_down)


def joined_blocks(batches, seqs, other):
    return ((3 * D // seqs, D // batches), other)


def joined_back(layer, batches, seqs, order, me, inputs, grad_queries, sources, rest):
    grad_middle, cosine, sine, gain, w_qkv, grad_gain, turned, packed = rest
    row = gain_row(gain, layer)
    low, normed, inverse = normalize(inputs[...].astype(F32), row)
    back = 0.0
    for part in range(3):
        if part == 0:
            value = grad_queries[...].astype(F32) * DH ** (-0.5)
        else:
            value = sources[0][part - 1].astype(F32)
            for other in sources[1:]:
                value = value + other[part - 1].astype(F32)
        if part < 2:
            value = rotate(value, cosine[...], -sine[...])
        value = value.astype(BF16)
        turned[part * D : (part + 1) * D, :] = value.T
        back = back + dot_nt(value, w_qkv[0, :, part * D : (part + 1) * D])
    deep, wide = joined_blocks(batches, seqs, None)[0]

    def one_block(seq, unused):
        made = dot(turned[pl.ds(pl.multiple_of(seq * deep, deep), deep), :], low).astype(BF16)
        place = slot_of(order, "seq", seq ^ me[2])
        for batch in range(batches):
            slot = place + slot_of(order, "batch", batch ^ me[1])
            put(packed, slot, 0, made[:, batch * wide : (batch + 1) * wide])
        return unused

    lax.fori_loop(0, seqs, one_block, 0)
    value, gain_sum = normalize_back(back, normed, inverse, row)
    grad_gain[...] = gain_sum
    return grad_middle[...] + value


def embed_back_kernel(layer, members, batches, seqs, order, me, inputs, grad_queries, *refs):
    sources = refs[:members]
    (
        grad_middle, cosine, sine, gain, w_qkv, tokens,
        stays, leaves, grad_gain, grad_inputs, turned, packed, sems,
    ) = refs[members:]
    value = joined_back(
        layer, batches, seqs, order, me, inputs, grad_queries, sources,
        (grad_middle, cosine, sine, gain, w_qkv, grad_gain, turned, packed),
    ).astype(BF16)
    grad_inputs[...] = value
    blocks = joined_blocks(batches, seqs, (VOCAB // batches, D // seqs))
    onehot = picks(tokens[...] == iota((VOCAB, tokens.shape[1]), 0))
    put_all(packed, order, me, layout(blocks)[0][1], dot(onehot, value).astype(BF16), *blocks[1], False)
    hand_out(packed, stays, leaves, sems)


def embed_back_call(
    layer, batches, seqs, order, me, inputs, grad_queries, pieces, grad_middle, cosine, sine, gain, w_qkv, tokens, after=()):
    count = inputs.shape[0]
    members = len(pieces)
    packs = layout(joined_blocks(batches, seqs, (VOCAB // batches, D // seqs)))[1]
    return call(
        functools.partial(embed_back_kernel, layer, members, batches, seqs, order),
        packed_shapes(batches, seqs, packs) + (shape((1, D), F32), shape((count, D), BF16)),
        grid=(1,),
        scalars=1,
        in_specs=[fixed((count, D))] * 2
        + [fixed((2, count, D))] * members
        + [
            fixed((count, D)),
            fixed(cosine.shape),
            fixed(sine.shape),
            fixed(gain.shape),
            fixed((1, D, 3 * D), (layer, 0, 0)),
            fixed(tokens.shape),
        ],
        out_specs=(ANYWHERE, ANYWHERE, fixed((1, D)), fixed((count, D))),
        scratch=[pltpu.VMEM((3 * D, count), BF16)] + packed_scratch(batches, seqs, packs),
        flops=2 * count * D * (6 * D + VOCAB),
        after=after,
    )(me, inputs, grad_queries, *pieces, grad_middle, cosine, sine, gain, w_qkv, tokens)


def pool_back_kernel(layer, rows, members, batches, seqs, order, me, inputs, grad_queries, *refs):
    sources = refs[:members]
    (
        grad_middle, cosine, sine, gain, w_qkv, grouped, w_pool,
        stays, leaves, grad_gain, grad_first, edges, turned, packed, sems,
    ) = refs[members:]
    value = joined_back(
        layer, batches, seqs, order, me, inputs, grad_queries, sources,
        (grad_middle, cosine, sine, gain, w_qkv, grad_gain, turned, packed),
    ).astype(BF16)
    blocks = joined_blocks(batches, seqs, (D // seqs, 3 * D // batches))
    put_all(packed, order, me, layout(blocks)[0][1], dot(value.T, grouped[...]).astype(BF16), *blocks[1], True)
    count = value.shape[0]
    short = count // rows
    span = grad_first.shape[0] // rows
    parts = [dot_nt(value, w_pool[third * D : (third + 1) * D, :]).astype(BF16) for third in range(3)]
    line = iota((2 * rows, count), 0)
    found = 0.0
    for third in range(2):
        pick = (iota((2 * rows, count), 1) == (line // 2) * short) & (line % 2 == third)
        found = found + dot(picks(pick), parts[third])
    edges[...] = found.astype(BF16)
    for row in range(rows):
        total = 0.0
        for third in range(3):
            pick = picks(iota((span, short), 0) == 3 * iota((span, short), 1) + third - 2)
            total = total + dot(pick, parts[third][row * short : (row + 1) * short, :])
        grad_first[row * span : (row + 1) * span, :] = total.astype(BF16)
    hand_out(packed, stays, leaves, sems)


def pool_back_call(
    layer, rows, span, batches, seqs, order, me, inputs, grad_queries, pieces, grad_middle, cosine, sine,
    gain, w_qkv, grouped, w_pool, after=()):
    count = inputs.shape[0]
    members = len(pieces)
    packs = layout(joined_blocks(batches, seqs, (D // seqs, 3 * D // batches)))[1]
    return call(
        functools.partial(pool_back_kernel, layer, rows, members, batches, seqs, order),
        packed_shapes(batches, seqs, packs)
        + (shape((1, D), F32), shape((rows * span, D), BF16), shape((2 * rows, D), BF16)),
        grid=(1,),
        scalars=1,
        in_specs=[fixed((count, D))] * 2
        + [fixed((2, count, D))] * members
        + [
            fixed((count, D)),
            fixed(cosine.shape),
            fixed(sine.shape),
            fixed(gain.shape),
            fixed((1, D, 3 * D), (layer, 0, 0)),
            fixed(grouped.shape),
            fixed(w_pool.shape),
        ],
        out_specs=(ANYWHERE, ANYWHERE, fixed((1, D)), fixed((rows * span, D)), fixed((2 * rows, D))),
        scratch=[pltpu.VMEM((3 * D, count), BF16)] + packed_scratch(batches, seqs, packs),
        flops=2 * count * D * (12 * D),
        after=after,
    )(me, inputs, grad_queries, *pieces, grad_middle, cosine, sine, gain, w_qkv, grouped, w_pool)


def angles(positions):
    half_size = DH // 2
    freqs = 10000.0 ** (-jnp.arange(half_size).astype(jnp.float32) / half_size)
    phase = positions.astype(jnp.float32)[:, None] * freqs[None, :]
    cosine, sine = jnp.cos(phase), jnp.sin(phase)
    return (jnp.concatenate([cosine] * 4, 1), jnp.concatenate([-sine, sine] * 2, 1))


class Plan:
    def __init__(self, rows):
        self.S = lax.axis_size("seq")
        self.B = lax.axis_size("batch")
        self.R = rows
        self.P = self.S // rows
        self.s = lax.axis_index("seq")
        self.b = lax.axis_index("batch")
        self.z = self.s // self.P
        self.h = self.s % self.P // 2 * 2 + self.b % 2

    def device(self, pair, z, y, core):
        return (z * self.P + y) * self.B + 2 * pair + core

    def exchange(self, value):
        moves = []
        for apart in range(self.R):
            perm = []
            for pair in range(self.B // 2):
                for z in range(self.R):
                    for y in range(self.P):
                        for core in range(2):
                            other = self.device(pair, z ^ apart, y // 2 * 2 + core, y % 2)
                            perm.append((self.device(pair, z, y, core), other))
            piece = lax.dynamic_index_in_dim(value, self.z ^ apart, 0, keepdims=False)
            moves.append(lax.ppermute(piece, AXES, perm))
        got, bit = moves, 1
        while bit < self.R:
            flip = (self.z // bit) % 2 == 1
            got = [jnp.where(flip, got[n ^ bit], got[n]) for n in range(self.R)]
            bit *= 2
        return (jnp.stack(got), moves)

    def shift(self, value, by):
        perm = []
        for pair in range(self.B // 2):
            for z in range(self.R):
                for batch in range(2):
                    for member in range(self.P):
                        to = (member + by) % self.P
                        perm.append((
                            self.device(pair, z, member // 2 * 2 + batch, member % 2),
                            self.device(pair, z, to // 2 * 2 + batch, to % 2),
                        ))
        return lax.ppermute(value, AXES, perm)

    def others(self, value):
        return [self.shift(value, by) for by in range(1, self.P)]

    def swap(self, value, axis, bit):
        count = lax.axis_size(axis)
        return lax.ppermute(value, axis, [(n, n ^ bit) for n in range(count)])

    def bits(self, axis):
        count = lax.axis_size(axis)
        return [1 << n for n in range(count.bit_length() - 1)]

    def order(self, first):
        batch = [("batch", bit) for bit in self.bits("batch")]
        seq = [("seq", bit) for bit in self.bits("seq")]
        return batch + seq if first == "batch" else batch[:1] + seq[:1] + batch[1:] + seq[1:]

    def all_sum(self, value):
        for axis in ("batch", "seq"):
            for bit in self.bits(axis):
                value = value + self.swap(value, axis, bit)
        return value


class Halving:
    def __init__(self, plan, order, stays, leaves):
        self.plan, self.order = plan, order
        self.value, self.leaves = stays.astype(F32), leaves
        self.got = []

    def step(self, count=1):
        for axis, bit in self.order[len(self.got) : len(self.got) + count]:
            got = self.plan.swap(self.leaves, axis, bit)
            self.got.append(got)
            self.value = self.value + got.astype(F32)
            half = self.value.shape[0] // 2
            if half:
                self.leaves, self.value = self.value[half:].astype(BF16), self.value[:half]
        return self.got[-1]

    def end(self):
        self.step(len(self.order))
        return self.value[0]


def unpacked(total, blocks):
    starts, unused = layout(blocks)
    made = []
    for (deep, wide), start in zip(blocks, starts):
        tiles = [
            total[start + tile * deep : start + (tile + 1) * deep, : min(128, wide - tile * 128)]
            for tile in range(-(-wide // 128))
        ]
        made.append(jnp.concatenate(tiles, 1))
    return made


def body(
    tokens, loss_mask, cotangent, embed, gain_attn, w_qkv, w_out, gain_ffn, w_up, w_down, w_pool
):
    plan = Plan(tokens.shape[0])
    rows, span = tokens.shape
    short = loss_mask.shape[1]
    members, batches, seqs = plan.P, plan.B, plan.S
    units = w_up.shape[2]
    by_x, by_y = plan.order("batch"), plan.order("seq")
    me = jnp.stack([plan.h, plan.b, plan.s]).astype(jnp.int32)

    my_tokens = plan.exchange(tokens)[0]
    token_line, token_column = my_tokens.reshape(1, rows * span), my_tokens.reshape(rows * span, 1)

    def places(length):
        block = jnp.arange(rows, dtype=jnp.int32)[:, None] * members + plan.h
        return (block * length + jnp.arange(length, dtype=jnp.int32)[None]).reshape(-1)

    first_angles, second_angles = angles(places(span)), angles(places(short))

    inputs, low, own_0 = embed_call(0, token_column, embed, gain_attn, w_qkv, *first_angles)
    others_0 = plan.others(own_0)
    queries_0 = query_call(0, low, w_qkv, *first_angles)
    start_grad, start_moves = plan.exchange(cotangent * loss_mask.astype(BF16)[..., None])
    mixed_0, logsum_0 = attention_call(rows, members, me, queries_0, own_0, others_0)
    first_low, edges, middle_0, hidden_0 = ffn_call(
        0, rows, inputs, mixed_0, w_out, gain_ffn, w_up, w_down, after=start_moves
    )
    edge = plan.shift(edges, 1)
    full_out, full_moves = plan.exchange(first_low.reshape(rows, span, D))

    grouped, pooled, low, own_1 = pool_call(
        1, rows, members, me, first_low, edge, w_pool, gain_attn, w_qkv, *second_angles
    )
    others_1 = plan.others(own_1)
    queries_1 = query_call(1, low, w_qkv, *second_angles)
    mixed_1, logsum_1 = attention_call(rows, members, me, queries_1, own_1, others_1)
    second_low, unused, middle_1, hidden_1 = ffn_call(
        1, rows, pooled, mixed_1, w_out, gain_ffn, w_up, w_down, after=full_moves
    )
    short_out, short_moves = plan.exchange(second_low.reshape(rows, short, D))

    stays, leaves, gain_ffn_1, grad_middle, grad_mixed = ffn_back_call(
        1, rows, members, batches, seqs, by_x, me, start_grad.reshape(-1, D), None, mixed_1, middle_1, hidden_1,
        w_out, gain_ffn, w_up, w_down,
    )
    ffn_1 = Halving(plan, by_x, stays, leaves)
    after = [ffn_1.step()]
    grad_queries, pieces = attention_back_call(
        rows, members, me, queries_1, own_1, others_1, mixed_1, logsum_1, grad_mixed
    )
    pieces = [pieces[0]] + [plan.shift(pieces[by], -by) for by in range(1, members)]
    stays, leaves, gain_attn_1, grad_first, edges = pool_back_call(
        1, rows, span, batches, seqs, by_y, me, pooled, grad_queries, pieces, grad_middle, *second_angles,
        gain_attn, w_qkv, grouped, w_pool, after=after + short_moves,
    )
    pool_1 = Halving(plan, by_y, stays, leaves)
    carried = plan.shift(edges, -1)

    after = [ffn_1.step(), pool_1.step()]
    stays, leaves, gain_ffn_0, grad_middle, grad_mixed = ffn_back_call(
        0, rows, members, batches, seqs, by_x, me, grad_first, carried, mixed_0, middle_0, hidden_0,
        w_out, gain_ffn, w_up, w_down,
    )
    ffn_0 = Halving(plan, by_x, stays, leaves)
    grad_queries, pieces = attention_back_call(
        rows, members, me, queries_0, own_0, others_0, mixed_0, logsum_0, grad_mixed, after=after
    )
    pieces = [pieces[0]] + [plan.shift(pieces[by], -by) for by in range(1, members)]
    after = [ffn_1.step(), pool_1.step(), ffn_0.step()]
    stays, leaves, gain_attn_0, grad_inputs = embed_back_call(
        0, batches, seqs, by_y, me, inputs, grad_queries, pieces, grad_middle, *first_angles,
        gain_attn, w_qkv, token_line, after=after,
    )
    qkv_0 = Halving(plan, by_y, stays, leaves)
    input_grad = plan.exchange(grad_inputs.reshape(rows, span, D))[0]

    blocks = ffn_blocks(batches, seqs, units)
    up_1, down_1, out_1 = unpacked(ffn_1.end(), blocks)
    up_0, down_0, out_0 = unpacked(ffn_0.end(), blocks)
    blocks = joined_blocks(batches, seqs, (D // seqs, 3 * D // batches))
    qkv_1, pool = unpacked(pool_1.end(), blocks)
    blocks = joined_blocks(batches, seqs, (VOCAB // batches, D // seqs))
    qkv_0, embed_grad = unpacked(qkv_0.end(), blocks)
    gains = plan.all_sum(jnp.concatenate([gain_attn_0, gain_attn_1, gain_ffn_0, gain_ffn_1]))
    return (
        full_out,
        short_out,
        input_grad.astype(jnp.float32),
        embed_grad,
        gains[:2],
        jnp.stack([qkv_0.T, qkv_1.T]),
        jnp.stack([out_0.T, out_1.T]),
        gains[2:],
        jnp.stack([up_0, up_1]),
        jnp.stack([down_0.T, down_1.T]),
        pool.T,
    )


def solution(mesh):
    in_specs = (
        P("batch", "seq"),
        P("batch", "seq"),
        P("batch", "seq", None),
        P(),
        P(),
        P(),
        P(),
        P(),
        P(),
        P(),
        P(),
    )
    out_specs = (
        P("batch", "seq", None),
        P("batch", "seq", None),
        P("batch", "seq", None),
        P("batch", "seq"),
        P(),
        P(None, "batch", "seq"),
        P(None, "batch", "seq"),
        P(),
        P(None, "batch", "seq"),
        P(None, "batch", "seq"),
        P("batch", "seq"),
    )
    return jax.shard_map(body, mesh=mesh, in_specs=in_specs, out_specs=out_specs, check_vma=False)
```

```python
import functools

import jax
import jax.numpy as jnp
from jax import lax
from jax.experimental import pallas as pl
from jax.experimental.pallas import tpu as pltpu
from jax.sharding import PartitionSpec as P

D = 512
H = 8
DH = 64

epsilon = 1e-05
masked_score = -1e30
AXES = ("seq", "batch")


VOCAB = 256
BF16 = jnp.bfloat16
F32 = jnp.float32
ANYWHERE = pl.BlockSpec(memory_space=pl.ANY)
ROOM = 56 * 1024 * 1024


def dot(left, right):
    return jnp.dot(left, right, preferred_element_type=F32)


def dot_nt(left, right):
    return lax.dot_general(left, right, (((1,), (1,)), ((), ())), preferred_element_type=F32)


def iota(shape, dim):
    return lax.broadcasted_iota(jnp.int32, shape, dim)


def picks(condition):
    return jnp.where(condition, 1.0, 0.0).astype(BF16)


def call(kernel, out_shape, grid, in_specs, out_specs, scratch=(), scalars=0):
    return pl.pallas_call(
        kernel,
        out_shape=out_shape,
        grid_spec=pltpu.PrefetchScalarGridSpec(
            num_scalar_prefetch=scalars,
            grid=grid,
            in_specs=in_specs,
            out_specs=out_specs,
            scratch_shapes=scratch,
        ),
        compiler_params=pltpu.CompilerParams(vmem_limit_bytes=ROOM),
    )


def shape(dims, dtype):
    return jax.ShapeDtypeStruct(dims, dtype)


def fixed(block, index=None, buffers=1):
    place = index or (0,) * len(block)
    return pl.BlockSpec(block, lambda *unused: place, pipeline_mode=pl.Buffered(buffers))


def gain_row(ref, layer):
    return ref[...].astype(F32)[layer : layer + 1]


def normalize(inputs, gain):
    centred = inputs - jnp.mean(inputs, -1, keepdims=True)
    inverse = lax.rsqrt(jnp.mean(centred * centred, -1, keepdims=True) + epsilon)
    normed = centred * inverse
    return ((normed * gain).astype(BF16), normed, inverse)


def normalize_back(grad, normed, inverse, gain):
    scaled = grad * gain
    result = inverse * (
        scaled
        - jnp.mean(scaled, -1, keepdims=True)
        - normed * jnp.mean(scaled * normed, -1, keepdims=True)
    )
    return (result, jnp.sum(grad * normed, axis=0, keepdims=True))


def rotate(inputs, table, back=False):
    width = inputs.shape[1]
    turned = pltpu.roll(table, DH, 1)
    early = iota(table.shape, 1) < DH
    cosine, sine = jnp.where(early, table, turned), jnp.where(early, turned, table)
    if back:
        sine = -sine
    count = width // 128
    first = iota(inputs.shape, 1) % DH < DH // 2
    other = jnp.where(
        first, pltpu.roll(inputs, width - DH // 2, 1), pltpu.roll(inputs, DH // 2, 1)
    )
    return inputs * jnp.concatenate([cosine] * count, 1) + other * jnp.concatenate([sine] * count, 1)


def gelu_both(hidden):
    scale = 0.7978845608028654
    square = hidden * hidden
    tanh = jnp.tanh(scale * hidden * (1.0 + 0.044715 * square))
    half = 0.5 + 0.5 * tanh
    slope = half + (0.5 * scale) * hidden * (1.0 - tanh * tanh) * (1.0 + 0.134145 * square)
    return (hidden * half, slope)


def layout(blocks):
    starts, at = [], 0
    for deep, wide in blocks:
        starts.append(at)
        at += deep * -(-wide // 128)
    return starts, at


def unpacked(slot, blocks):
    made = []
    for (deep, wide), start in zip(blocks, layout(blocks)[0]):
        tiles = [
            slot[start + tile * deep : start + (tile + 1) * deep, : min(128, wide - tile * 128)]
            for tile in range(-(-wide // 128))
        ]
        made.append(tiles[0] if len(tiles) == 1 else jnp.concatenate(tiles, 1))
    return made


def slot_of(order, axis, place, own):
    if all(name != axis for name, bit in order):
        return place << len(order)
    slot, apart = 0, place ^ own
    for number, (name, bit) in enumerate(order):
        if name == axis:
            slot = slot + ((apart // bit) % 2) * (1 << (len(order) - 1 - number))
    return slot


class Packs:
    def __init__(self, batches, seqs, order, blocks):
        self.batches, self.seqs, self.order, self.blocks = batches, seqs, order, blocks
        self.starts, self.rows = layout(blocks)
        self.slots = batches * seqs
        self.whole = len(order) < 2 or batches * seqs != 1 << len(order)

    def put(self, packed, slot, start, block):
        deep, wide = block.shape
        for tile in range(-(-wide // 128)):
            piece = block[:, tile * 128 : min(wide, (tile + 1) * 128)]
            first = pl.multiple_of(slot * self.rows + (start + tile * deep), 16)
            packed[pl.ds(first, deep), : piece.shape[1]] = piece

    def put_block(self, packed, me, number, batch, seq, block):
        if self.order:
            slot = slot_of(self.order, "batch", batch, me[1]) + slot_of(self.order, "seq", seq, me[2])
        else:
            slot = batch * self.seqs + seq
        self.put(packed, slot, self.starts[number], block)

    def put_all(self, packed, me, number, made, swapped):
        deep, wide = self.blocks[number]
        for line in range(made.shape[0] // deep):
            for column in range(made.shape[1] // wide):
                batch, seq = (column, line) if swapped else (line, column)
                block = made[line * deep : (line + 1) * deep, column * wide : (column + 1) * wide]
                self.put_block(packed, me, number, batch, seq, block)

    def hand_out(self, packed, outs, sems):
        copies, at = [], 0
        for number, out in enumerate(outs):
            copies.append(pltpu.make_async_copy(packed.at[pl.ds(at, out.shape[0])], out, sems.at[number]))
            at += out.shape[0]
        for copy in copies:
            copy.start()
        for copy in copies:
            copy.wait()

    def send(self, packed, outs, moves, first, last):
        for slot in range(self.slots):
            at, out = slot * self.rows, outs[0]
            to = at
            if len(outs) == 2 and slot >= self.slots // 2:
                to, out = at - self.slots // 2 * self.rows, outs[1]
            rows = last - first
            moves.start(packed.at[pl.ds(at + first, rows)], out.at[pl.ds(to + first, rows)])

    def shapes(self, extra=0):
        if self.whole:
            return (shape((self.slots * self.rows, 128), BF16),)
        half = self.slots * self.rows // 2
        return (shape((half, 128), BF16), shape((half + extra, 128), BF16))

    def specs(self):
        return (ANYWHERE,) * len(self.shapes())

    def scratch(self, extra=0):
        return [pltpu.VMEM((self.slots * self.rows + extra, 128), BF16), pltpu.SemaphoreType.DMA((2,))]


def in_two(value):
    high = value.astype(BF16)
    return high, (value - high.astype(F32)).astype(BF16)


def halve_kernel(kept, got, sums, stays, leaves, made):
    size = kept.shape[0]
    half = size // 2
    stays[...] = (kept[:half, :].astype(F32) + got[:half, :].astype(F32)).astype(BF16)
    leaves[:half, :] = (kept[half:, :].astype(F32) + got[half:size, :].astype(F32)).astype(BF16)
    made[...] = add_sums(sums[...], got, size)
    high, low = in_two(made[...])
    leaves[half : half + high.shape[0], :] = high
    leaves[half + high.shape[0] :, :] = low


def add_sums(own, got, at):
    count = own.shape[0]
    high, low = in_two(own)
    own = high.astype(F32) + low.astype(F32)
    return own + (got[at : at + count, :].astype(F32) + got[at + count : at + 2 * count, :].astype(F32))


def halve_call(kept, got, sums):
    half = kept.shape[0] // 2
    operands = (kept, got, sums)
    outs = (
        shape((half, 128), BF16),
        shape((half + 2 * sums.shape[0], 128), BF16),
        shape(sums.shape, F32),
    )
    return call(
        halve_kernel,
        outs,
        grid=(1,),
        in_specs=[fixed(each.shape) for each in operands],
        out_specs=tuple(fixed(each.shape) for each in outs),
    )(*operands)


def spread_kernel(kept, got, sums, own, made, *leaves):
    size, rows = kept.shape[0], own.shape[0]
    made[...] = add_sums(sums[...], got, size)
    high, low = in_two(made[...])
    for slot in range(size // rows):
        lines = slice(slot * rows, (slot + 1) * rows)
        value = (kept[lines, :].astype(F32) + got[lines, :].astype(F32)).astype(BF16)
        if slot == 0:
            own[...] = value
        else:
            out = leaves[slot - 1]
            out[:rows, :] = value
            out[rows : rows + high.shape[0], :] = high
            out[rows + high.shape[0] :, :] = low


def spread_call(rows, kept, got, sums):
    operands = (kept, got, sums)
    outs = (shape((rows, 128), BF16), shape(sums.shape, F32))
    outs += (shape((rows + 2 * sums.shape[0], 128), BF16),) * (kept.shape[0] // rows - 1)
    made = call(
        spread_kernel,
        outs,
        grid=(1,),
        in_specs=[fixed(each.shape) for each in operands],
        out_specs=tuple(fixed(each.shape) for each in outs),
    )(*operands)
    return made[0], made[1], made[2:]


def pairwise(values):
    while len(values) > 1:
        values = [values[n] + values[n + 1] for n in range(0, len(values), 2)]
    return values[0]


def finish_kernel(layouts, counts, *refs):
    terms = []
    for count in counts:
        terms.append(sum([ref[...].astype(F32) for ref in refs[:count]]))
        refs = refs[count:]
    qkv_0, sums, *came = refs[:-8]
    qkv_out, out_out, up_out, down_out, pool_out, embed_out, gain_attn, gain_ffn = refs[-8:]
    for number in range(2):
        up_out[number], down_out[number], out_out[number] = unpacked(terms[number], layouts[0])
    qkv_out[1], pool_out[...] = unpacked(terms[2], layouts[1])
    at, count = qkv_0.shape[0], sums.shape[0]
    slot = pairwise([each[:at, :].astype(F32) for each in (qkv_0, *came)])
    qkv_out[0], embed_out[...] = unpacked(slot, layouts[2])
    high, low = in_two(sums[...])
    made = [high.astype(F32) + low.astype(F32)]
    for each in came:
        made.append(each[at : at + count, :].astype(F32) + each[at + count :, :].astype(F32))
    made = pairwise(made)
    tiles = D // 128
    for number, ref in enumerate((gain_attn, gain_attn, gain_ffn, gain_ffn)):
        for tile in range(tiles):
            place = number * tiles + tile
            ref[number % 2 : number % 2 + 1, tile * 128 : (tile + 1) * 128] = made[place : place + 1, :]


def finish_call(layouts, terms, *rest):
    (up, down, out), (qkv, pool), (unused, embed) = layouts
    dims = [(2,) + qkv, (2,) + out, (2,) + up, (2,) + down, pool, embed, (2, D), (2, D)]
    specs = []
    for number, group in enumerate(terms):
        specs += [fixed((layout(layouts[number // 2])[1], 128))] * len(group)
    return call(
        functools.partial(finish_kernel, layouts, [len(group) for group in terms]),
        tuple(shape(each, F32) for each in dims),
        grid=(1,),
        in_specs=specs + [fixed(each.shape) for each in rest],
        out_specs=tuple(fixed(each) for each in dims),
    )(*sum(terms, []), *rest)


def embed_kernel(layer, tokens, embed, gain, w_qkv, table, inputs, low, both):
    part = pl.program_id(0)

    @pl.when(part == 0)
    def first():
        onehot = picks(tokens[...] == iota((tokens.shape[0], embed.shape[0]), 1))
        value = dot(onehot, embed[...])
        inputs[...] = value.astype(BF16)
        low[...] = normalize(value, gain_row(gain, layer))[0]

    joined = dot(low[...], w_qkv[0])

    @pl.when(part == 0)
    def keys():
        both[0] = rotate(joined, table[...]).astype(BF16)

    @pl.when(part == 1)
    def values():
        both[0] = joined.astype(BF16)


def embed_call(layer, tokens, embed, gain, w_qkv, table):
    count = tokens.shape[0]
    return call(
        functools.partial(embed_kernel, layer),
        (shape((count, D), BF16), shape((count, D), BF16), shape((2, count, D), BF16)),
        grid=(2,),
        in_specs=[
            fixed(tokens.shape),
            fixed(embed.shape),
            fixed(gain.shape),
            pl.BlockSpec((1, D, D), lambda part: (layer, 0, part + 1)),
            fixed(table.shape),
        ],
        out_specs=(
            fixed((count, D)),
            fixed((count, D)),
            pl.BlockSpec((1, count, D), lambda part: (part, 0, 0)),
        ),
    )(tokens, embed, gain, w_qkv, table)


def pool_kernel(layer, rows, members, me, first, edge, w_pool, gain, w_qkv, table, grouped, pooled, low, both):
    span = first.shape[0] // rows
    count = pooled.shape[0]
    short = count // rows
    late = jnp.where(me[0] == 0, 1, 0)
    total = jnp.zeros((count, D), F32)
    for third in range(3):
        pick = picks(iota((short, span), 1) == 3 * iota((short, span), 0) + third - 2)
        piece = jnp.concatenate(
            [dot(pick, first[row * span : (row + 1) * span, :]) for row in range(rows)], 0
        )
        if third < 2:
            place = iota((count, 2 * rows), 0) == (iota((count, 2 * rows), 1) // 2 + late) * short
            place = picks(place & (iota((count, 2 * rows), 1) % 2 == third))
            piece = piece + dot(place, edge[...])
        piece = piece.astype(BF16)
        grouped[:, third * D : (third + 1) * D] = piece
        total = total + dot(piece, w_pool[third * D : (third + 1) * D, :])
    pooled[...] = total
    low[...] = normalize(total, gain_row(gain, layer))[0]
    both[0] = rotate(dot(low[...], w_qkv[0, :, D : 2 * D]), table[...]).astype(BF16)
    both[1] = dot(low[...], w_qkv[0, :, 2 * D :]).astype(BF16)


def pool_call(layer, rows, members, me, first, edge, w_pool, gain, w_qkv, table):
    count = table.shape[0]
    return call(
        functools.partial(pool_kernel, layer, rows, members),
        (
            shape((count, 3 * D), BF16),
            shape((count, D), F32),
            shape((count, D), BF16),
            shape((2, count, D), BF16),
        ),
        grid=(1,),
        scalars=1,
        in_specs=[
            fixed(first.shape),
            fixed(edge.shape),
            fixed(w_pool.shape),
            fixed(gain.shape),
            fixed((1, D, 3 * D), (layer, 0, 0)),
            fixed(table.shape),
        ],
        out_specs=(fixed((count, 3 * D)), fixed((count, D)), fixed((count, D)), fixed((2, count, D))),
    )(me, first, edge, w_pool, gain, w_qkv, table)


GROUP = 256
HEADS = GROUP // DH


def fill_keys(rows, members, own, others, keys, values):
    span = own.shape[1] // rows
    for row in range(rows):
        for by, source in enumerate([own, *others]):
            start = (row * members + by) * span
            keys[start : start + span, :] = source[0, row * span : (row + 1) * span, :]
            values[start : start + span, :] = source[1, row * span : (row + 1) * span, :]


def tiles_of(rows, members, span):
    step = min(rows, max(1, 256 // span))
    return [(first, min(rows, first + step)) for first in range(0, rows, step)]


def heads_at_once(rows, members, span):
    size = sum((last - first) * span * last * members * span * 4 for first, last in tiles_of(rows, members, span))
    return max(count for count in (1, 2, HEADS) if count == 1 or count * size <= 12 << 20)


def bias_shape(rows, members, span):
    first, last = tiles_of(rows, members, span)[0]
    return ((last - first) * span, (last - first) * members * span)


def turned_shape(rows, members, span):
    tiles = tiles_of(rows, members, span)
    return (len(tiles), GROUP, rows * span)


def fill_bias(member, members, span, bias):
    line, column = iota(bias.shape, 0), iota(bias.shape, 1)
    width = members * span
    by = column % width // span
    own = (by == 0) & (column % span <= line % span)
    same = own | ((by > 0) & ((member + by) % members < member))
    seen = (column // width < line // span) | ((column // width == line // span) & same)
    bias[...] = jnp.where(seen, 0.0, masked_score)


def score(query, keys, bias, start, end):
    scores = dot_nt(query, keys[0:end, :])
    last = scores[:, start:] + bias[...]
    return jnp.concatenate([scores[:, :start], last], 1) if start else last


def attention_part(rows, members, queries, own, *refs):
    others = refs[: members - 1]
    mixed, logsum, keys, values, bias, total = refs[members - 1 :]
    span = queries.shape[0] // rows
    width = members * span
    tiles = tiles_of(rows, members, span)
    fill_keys(rows, members, own, others, keys, values)
    logsum[...] = jnp.zeros_like(logsum)

    at_once = heads_at_once(rows, members, span)

    def some_heads(turn, unused):
        todo = []
        for number in range(at_once):
            head = turn * at_once + number
            lanes = iota((1, GROUP), 1) // DH == head
            mask = picks(lanes)
            for first, last in tiles:
                block = slice(first * span, last * span)
                todo.append((head, lanes, mask, block, first * width, last * width))
        scores = [
            score(queries[block, :] * mask, keys, bias, start, end)
            for head, lanes, mask, block, start, end in todo
        ]
        highest = [jnp.max(value, -1, keepdims=True) for value in scores]
        expon = [jnp.exp(value - most) for value, most in zip(scores, highest)]
        totals = [jnp.sum(value, -1, keepdims=True) for value in expon]
        outs = [
            dot(value.astype(BF16), values[0:end, :]) * (1.0 / whole)
            for value, whole, (head, lanes, mask, block, start, end) in zip(expon, totals, todo)
        ]
        for (head, lanes, mask, block, start, end), out, most, whole in zip(todo, outs, highest, totals):
            total[block, :] = jnp.where(lanes, out, total[block, :])
            here = iota((out.shape[0], 128), 1) == head
            logsum[0, block, :] = jnp.where(here, most + jnp.log(whole), logsum[0, block, :])
        return unused

    lax.fori_loop(0, HEADS // at_once, some_heads, 0)
    mixed[...] = total[...].astype(BF16)


def lane_group(ndim, block, base=0):
    return pl.BlockSpec(block, lambda group, *unused: (0,) * (ndim - 1) + (group + base,))


def lane_part(ref, group):
    lanes = pl.ds(group * GROUP, GROUP)
    return ref.at[:, lanes] if len(ref.shape) == 2 else ref.at[:, :, lanes]


def attention_scratch(rows, members, count):
    span = count // rows
    return [
        pltpu.VMEM((members * count, GROUP), BF16),
        pltpu.VMEM((members * count, GROUP), BF16),
        pltpu.VMEM(bias_shape(rows, members, span), F32),
        pltpu.VMEM((count, GROUP), F32),
    ]


def attention_back_scratch(rows, members, count):
    span = count // rows
    return [
        pltpu.VMEM(turned_shape(rows, members, span), BF16),
        pltpu.VMEM(turned_shape(rows, members, span), BF16),
        pltpu.VMEM((GROUP, members * count), F32),
        pltpu.VMEM((GROUP, members * count), F32),
    ]


def attention_back_kernel(rows, members, me, queries, own, *refs):
    fill_bias(me[0], members, queries.shape[0] // rows, refs[-6])
    attention_back_part(rows, members, queries, own, *refs)


def attention_back_part(rows, members, queries, own, *refs):
    others = refs[: members - 1]
    mixed, logsum, grad_mixed, grad_queries, *rest = refs[members - 1 :]
    pieces = rest[:members]
    keys, values, bias, total, turned, turned_grad, grad_keys, grad_values = rest[members:]
    span = queries.shape[0] // rows
    width = members * span
    fill_keys(rows, members, own, others, keys, values)
    tiles = tiles_of(rows, members, span)
    for tile, (first, last) in enumerate(tiles):
        lines = (rows - first) * span
        turned[tile, :, 0:lines] = queries[first * span :, :].T
        turned_grad[tile, :, 0:lines] = grad_mixed[first * span :, :].T

    at_once = heads_at_once(rows, members, span)

    def some_heads(turn, unused):
        todo = []
        for number in range(at_once):
            head = turn * at_once + number
            lanes = iota((1, GROUP), 1) // DH == head
            for tile, (first, last) in enumerate(tiles):
                block = slice(first * span, last * span)
                todo.append((head, lanes, picks(lanes), tile, block, first * width, last * width))
        grads = [grad_mixed[block, :] * mask for head, lanes, mask, tile, block, start, end in todo]
        scores = [
            score(queries[block, :] * mask, keys, bias, start, end)
            for head, lanes, mask, tile, block, start, end in todo
        ]
        grad_probs = [dot_nt(grad, values[0 : each[-1], :]) for grad, each in zip(grads, todo)]
        sums = [
            jnp.sum(
                jnp.where(iota((block.stop - block.start, 128), 1) == head, logsum[0, block, :], 0.0),
                -1,
                keepdims=True,
            )
            for head, lanes, mask, tile, block, start, end in todo
        ]
        deltas = [
            jnp.sum(grad.astype(F32) * mixed[each[4], :].astype(F32), -1, keepdims=True)
            for grad, each in zip(grads, todo)
        ]
        probs = [jnp.exp(value - whole) for value, whole in zip(scores, sums)]
        grad_scores = [
            (prob * (grad - delta)).astype(BF16) for prob, grad, delta in zip(probs, grad_probs, deltas)
        ]
        for each, grad in zip(todo, grad_scores):
            head, lanes, mask, tile, block, start, end = each
            total[block, :] = jnp.where(lanes, dot(grad, keys[0:end, :]), total[block, :])
        count = len(tiles)
        for number in range(at_once):
            mine = pl.ds(pl.multiple_of((turn * at_once + number) * DH, DH), DH)
            for tile, (first, last) in enumerate(tiles):
                columns = slice(first * width, last * width)
                lines = (rows - first) * span
                for source, made, into in (
                    (turned, grad_scores, grad_keys),
                    (turned_grad, probs, grad_values),
                ):
                    later = made[number * count + tile : (number + 1) * count]
                    stack = jnp.concatenate([value[:, columns].astype(BF16) for value in later], 0)
                    into[mine, columns] = dot(source[tile, mine, 0:lines], stack)
        return unused

    lax.fori_loop(0, HEADS // at_once, some_heads, 0)
    grad_queries[...] = total[...].astype(BF16)
    for number, source in enumerate((grad_keys, grad_values)):
        made = source[...].astype(BF16).T
        for row in range(rows):
            for by, piece in enumerate(pieces):
                start = (row * members + by) * span
                piece[number, row * span : (row + 1) * span, :] = made[start : start + span, :]


def attention_back_call(rows, members, me, queries, own, others, mixed, logsum, grad_mixed, groups):
    count = queries.shape[0]
    base, wide = groups[0], len(groups) * GROUP
    made = call(
        functools.partial(attention_back_kernel, rows, members),
        (shape((count, wide), BF16),) + (shape((2, count, wide), BF16),) * members,
        grid=(len(groups),),
        scalars=1,
        in_specs=[lane_group(2, (count, GROUP), base)]
        + [lane_group(3, (2, count, GROUP), base)] * members
        + [
            lane_group(2, (count, GROUP), base),
            pl.BlockSpec((1, count, 128), lambda group, *unused: (group + base, 0, 0)),
            lane_group(2, (count, GROUP), base),
        ],
        out_specs=(lane_group(2, (count, GROUP)),) + (lane_group(3, (2, count, GROUP)),) * members,
        scratch=attention_scratch(rows, members, count) + attention_back_scratch(rows, members, count),
    )(me, queries, own, *others, mixed, logsum, grad_mixed)
    return (made[0], made[1:])


CHUNK = 512


class Moves:
    def __init__(self, sems, first=0):
        self.sems, self.taken, self.open = sems, first, []

    def start(self, source, target):
        copy = pltpu.make_async_copy(source, target, self.sems.at[self.taken])
        copy.start()
        self.open.append(copy)
        self.taken += 1
        return copy

    def end(self):
        for copy in self.open:
            copy.wait()
        self.open = []


class Weights:
    def __init__(self, sems, layer, sources, held):
        self.sems, self.layer, self.sources, self.held = sems, layer, sources, held
        self.chunks = held[1].shape[1] // CHUNK
        self.copies = 1 + 2 * self.chunks

    def pair(self, name, part=0):
        (w_out, w_up, w_down), (out, up, down) = self.sources, self.held
        if name == "out":
            return w_out.at[self.layer], out
        lines = pl.ds(pl.multiple_of(part * CHUNK, CHUNK), CHUNK)
        if name == "up":
            return w_up.at[self.layer, :, lines], up.at[:, lines]
        return w_down.at[self.layer, lines, :], down.at[lines, :]

    def copy(self, name, part=0):
        place = {"out": 0, "up": 1, "down": 2}[name] + 2 * part
        return pltpu.make_async_copy(*self.pair(name, part), self.sems.at[place])

    def start(self):
        self.copy("out").start()
        for part in range(self.chunks):
            self.copy("up", part).start()
            self.copy("down", part).start()

    def wait(self, name, part=0):
        self.copy(name, part).wait()

    def get(self, name, part=0):
        return self.pair(name, part)[1][...]


def weight_scratch(units):
    return [pltpu.VMEM((D, D), BF16), pltpu.VMEM((D, units), BF16), pltpu.VMEM((units, D), BF16)]


def edge_rows(made, rows):
    count = made.shape[0]
    span = count // rows
    line = iota((2 * rows, count), 0)
    pick = picks(iota((2 * rows, count), 1) == (line // 2 + 1) * span - 2 + line % 2)
    return dot(pick, made).astype(BF16)


def make_queries(low, w_qkv, table):
    joined = dot(low[...], w_qkv[0])
    return (rotate(joined, table[...]) * DH ** (-0.5)).astype(BF16)


def attend(rows, members, me, queries, own, others, mixed, logsum, scratch):
    fill_bias(me[0], members, queries.shape[0] // rows, scratch[2])
    for group in range(D // GROUP):
        sources = [lane_part(each, group) for each in (queries, own, *others, mixed)]
        attention_part(rows, members, *sources, logsum.at[pl.ds(group, 1)], *scratch)


def forward_kernel(layer, rows, members, me, inputs, low, own, *refs):
    others = refs[: members - 1]
    (
        table, gain, w_qkv, w_out, w_up, w_down,
        output, edges, queries_out, mixed_out, logsum_out, middle_out, hidden_out,
        queries, mixed, logsum, middle, hidden, low_now, sum_now, *scratch,
    ) = refs[members - 1 :]
    held, attention, sems = scratch[:3], scratch[3:7], scratch[7]
    weights = Weights(sems, layer, (w_out, w_up, w_down), held)
    moves = Moves(sems, weights.copies)
    weights.start()
    queries[...] = make_queries(low, w_qkv, table)
    moves.start(queries, queries_out)
    attend(rows, members, me, queries, own, others, mixed, logsum, attention)
    moves.start(mixed, mixed_out)
    moves.start(logsum, logsum_out)
    weights.wait("out")
    total = inputs[...].astype(F32) + dot(mixed[...], weights.get("out"))
    middle[...] = total
    moves.start(middle, middle_out)
    normed = normalize(total, gain_row(gain, layer))[0]
    low_now[...] = normed
    sum_now[...] = total

    def one_part(part, unused):
        weights.wait("up", part)
        made = dot(low_now[...], weights.get("up", part))
        lanes = pl.ds(pl.multiple_of(part * CHUNK, CHUNK), CHUNK)
        hidden[:, lanes] = made.astype(BF16)
        weights.wait("down", part)
        sum_now[...] += dot(gelu_both(made)[0].astype(BF16), weights.get("down", part))
        return unused

    lax.fori_loop(0, weights.chunks, one_part, 0)
    moves.start(hidden, hidden_out)
    made = sum_now[...].astype(BF16)
    output[...] = made
    edges[...] = edge_rows(made, rows)
    moves.end()


def forward_call(layer, rows, members, me, inputs, low, own, others, table, gain, w_qkv, w_out, w_up, w_down):
    count = inputs.shape[0]
    units = w_up.shape[2]
    handed = [
        ((count, D), BF16), ((count, D), BF16), ((D // GROUP, count, 128), F32),
        ((count, D), F32), ((count, units), BF16),
    ]
    return call(
        functools.partial(forward_kernel, layer, rows, members),
        (shape((count, D), BF16), shape((2 * rows, D), BF16)) + tuple(shape(*each) for each in handed),
        grid=(1,),
        scalars=1,
        in_specs=[fixed((count, D))] * 2
        + [fixed((2, count, D))] * members
        + [fixed(table.shape), fixed(gain.shape), fixed((1, D, D), (layer, 0, 0))]
        + [ANYWHERE] * 3,
        out_specs=(fixed((count, D)), fixed((2 * rows, D))) + (ANYWHERE,) * len(handed),
        scratch=[pltpu.VMEM(*each) for each in handed]
        + [pltpu.VMEM((count, D), BF16), pltpu.VMEM((count, D), F32)]
        + weight_scratch(units)
        + attention_scratch(rows, members, count)
        + [pltpu.SemaphoreType.DMA((6 + 2 * (units // CHUNK),))],
    )(me, inputs, low, own, *others, table, gain, w_qkv, w_out, w_up, w_down)


def ffn_blocks(batches, seqs, units):
    return ((D // batches, units // seqs), (D // seqs, units // batches), (D // seqs, D // batches))


def ffn_back(layer, packs, me, middle, mixed, parts, weights, gain, packed, outs, moves, scratch, unroll):
    grad, turned_low, turned_grad, total = scratch
    row = gain_row(gain, layer)
    turned_low[...] = normalize(middle[...], row)[0].T
    turned_grad[...] = grad[...].T
    total[...] = jnp.zeros_like(total)

    def one_part(part, unused):
        active, slope = parts(part)
        grad_hidden = (dot_nt(grad[...], weights.get("down", part)) * slope).astype(BF16)
        made = dot(turned_grad[...], active.astype(BF16)).astype(BF16)
        deep, wide = packs.blocks[1]
        for column in range(CHUNK // wide):
            for seq in range(packs.seqs):
                block = made[seq * deep : (seq + 1) * deep, column * wide : (column + 1) * wide]
                packs.put_block(packed, me, 1, part * (CHUNK // wide) + column, seq, block)
        made = dot(turned_low[...], grad_hidden).astype(BF16)
        deep, wide = packs.blocks[0]
        for column in range(CHUNK // wide):
            for batch in range(packs.batches):
                block = made[batch * deep : (batch + 1) * deep, column * wide : (column + 1) * wide]
                packs.put_block(packed, me, 0, batch, part * (CHUNK // wide) + column, block)
        total[...] += dot_nt(grad_hidden, weights.get("up", part))
        return unused

    lax.fori_loop(0, weights.chunks, one_part, 0, unroll=unroll)
    packs.send(packed, outs, moves, 0, packs.starts[2])
    unused, normed, inverse = normalize(middle[...], row)
    back, gain_sum = normalize_back(total[...], normed, inverse, row)
    grad_middle = grad[...].astype(F32) + back
    branch = grad_middle.astype(BF16)
    packs.put_all(packed, me, 2, dot(branch.T, mixed[...]).astype(BF16), True)
    packs.send(packed, outs, moves, packs.starts[2], packs.rows)
    return grad_middle, dot_nt(branch, weights.get("out")).astype(BF16), gain_sum


def ffn_back_scratch(count):
    return [
        pltpu.VMEM((count, D), BF16),
        pltpu.VMEM((D, count), BF16),
        pltpu.VMEM((D, count), BF16),
        pltpu.VMEM((count, D), F32),
    ]


def ffn_back_kernel(
    layer, rows, members, packs, me, grad_ref, carried, middle_ref, mixed_ref, hidden_ref, gain,
    w_out, w_up, w_down, *refs,
):
    outs = refs[: len(packs.shapes())]
    (
        grad_gain, grad_middle, grad_mixed,
        middle, mixed, hidden, out, up, down, grad, turned_low, turned_grad, total, packed, sems,
    ) = refs[len(outs) :]
    weights = Weights(sems, layer, (w_out, w_up, w_down), (out, up, down))
    moves = Moves(sems, weights.copies + weights.chunks)
    came = moves.start(middle_ref, middle)

    def hidden_copy(part):
        lanes = pl.ds(pl.multiple_of(part * CHUNK, CHUNK), CHUNK)
        return pltpu.make_async_copy(
            hidden_ref.at[:, lanes], hidden.at[:, lanes], sems.at[weights.copies + part]
        )

    for part in range(weights.chunks):
        weights.copy("down", part).start()
        hidden_copy(part).start()
        weights.copy("up", part).start()
    weights.copy("out").start()
    late = moves.start(mixed_ref, mixed)
    moves.open = []
    value = grad_ref[...]
    count = value.shape[0]
    span = count // rows
    early = jnp.where(me[0] == members - 1, 1, 0)
    line = iota((count, 2 * rows), 1)
    place = iota((count, 2 * rows), 0) == (line // 2 + 1 - early) * span - 2 + line % 2
    grad[...] = (value.astype(F32) + dot(picks(place), carried[...])).astype(BF16)

    def parts(part):
        hidden_copy(part).wait()
        weights.wait("down", part)
        weights.wait("up", part)
        lanes = pl.ds(pl.multiple_of(part * CHUNK, CHUNK), CHUNK)
        return gelu_both(hidden[:, lanes].astype(F32))

    came.wait()
    late.wait()
    weights.wait("out")
    made = ffn_back(
        layer, packs, me, middle, mixed, parts, weights, gain, packed, outs, moves,
        (grad, turned_low, turned_grad, total), 1,
    )
    grad_middle[...], grad_mixed[...], grad_gain[...] = made
    moves.end()


def ffn_back_call(
    layer, rows, members, batches, seqs, order, me, grad, carried, middle, mixed, hidden, gain, w_out, w_up, w_down
):
    count = grad.shape[0]
    units = w_up.shape[2]
    packs = Packs(batches, seqs, order, ffn_blocks(batches, seqs, units))
    return call(
        functools.partial(ffn_back_kernel, layer, rows, members, packs),
        packs.shapes() + (shape((1, D), F32), shape((count, D), F32), shape((count, D), BF16)),
        grid=(1,),
        scalars=1,
        in_specs=[fixed((count, D)), fixed((2 * rows, D)), ANYWHERE, ANYWHERE, ANYWHERE, fixed(gain.shape)]
        + [ANYWHERE] * 3,
        out_specs=packs.specs() + (fixed((1, D)), fixed((count, D)), fixed((count, D))),
        scratch=[pltpu.VMEM((count, D), F32), pltpu.VMEM((count, D), BF16), pltpu.VMEM((count, units), BF16)]
        + weight_scratch(units)
        + ffn_back_scratch(count)
        + [packs.scratch()[0], pltpu.SemaphoreType.DMA((3 + 3 * (units // CHUNK) + 2 * packs.slots,))],
    )(me, grad, carried, middle, mixed, hidden, gain, w_out, w_up, w_down)


def middle_kernel(layer, rows, members, packs, me, inputs, low, own, *refs):
    others = refs[: members - 1]
    (
        grad_ref, table, gain, w_qkv, w_out, w_up, w_down,
        output, *refs,
    ) = refs[members - 1 :]
    outs = refs[: len(packs.shapes())]
    grad_gain, grad_middle, grad_queries, *refs = refs[len(outs) :]
    pieces = refs[:members]
    queries, mixed, logsum, middle, active, slope, grad_mixed, packed, *scratch = refs[members:]
    held, attention, back, ffn, sems = scratch[:3], scratch[3:7], scratch[7:11], scratch[11:15], scratch[15]
    parts = range(w_up.shape[2] // CHUNK)
    weights = Weights(sems, layer, (w_out, w_up, w_down), held)
    moves = Moves(sems, weights.copies)
    weights.start()
    queries[...] = make_queries(low, w_qkv, table)
    attend(rows, members, me, queries, own, others, mixed, logsum, attention)
    weights.wait("out")
    total = inputs[...].astype(F32) + dot(mixed[...], weights.get("out"))
    middle[...] = total
    normed = normalize(total, gain_row(gain, layer))[0]
    for part in parts:
        lanes = pl.ds(part * CHUNK, CHUNK)
        weights.wait("up", part)
        one, other = gelu_both(dot(normed, weights.get("up", part)))
        active[:, lanes], slope[:, lanes] = one.astype(BF16), other
        weights.wait("down", part)
        total = total + dot(active[:, lanes], weights.get("down", part))
    output[...] = total.astype(BF16)
    ffn[0][...] = grad_ref[...]

    def part_of(part):
        lanes = pl.ds(pl.multiple_of(part * CHUNK, CHUNK), CHUNK)
        return active[:, lanes], slope[:, lanes]

    made = ffn_back(
        layer, packs, me, middle, mixed, part_of, weights, gain, packed, outs, moves, ffn, True
    )
    grad_middle[...], grad_mixed[...], grad_gain[...] = made
    for group in range(D // GROUP):
        sources = [lane_part(each, group) for each in (queries, own, *others, mixed)]
        targets = [lane_part(each, group) for each in (grad_mixed, grad_queries, *pieces)]
        attention_back_part(
            rows, members, *sources, logsum.at[pl.ds(group, 1)], *targets, *attention, *back
        )
    moves.end()


def middle_call(
    layer, rows, members, batches, seqs, order, me, inputs, low, own, others, grad, table, gain,
    w_qkv, w_out, w_up, w_down,
):
    count = inputs.shape[0]
    units = w_up.shape[2]
    packs = Packs(batches, seqs, order, ffn_blocks(batches, seqs, units))
    made = call(
        functools.partial(middle_kernel, layer, rows, members, packs),
        (shape((count, D), BF16),)
        + packs.shapes()
        + (shape((1, D), F32), shape((count, D), F32), shape((count, D), BF16))
        + (shape((2, count, D), BF16),) * members,
        grid=(1,),
        scalars=1,
        in_specs=[fixed((count, D))] * 2
        + [fixed((2, count, D))] * members
        + [fixed((count, D)), fixed(table.shape), fixed(gain.shape)]
        + [fixed((1, D, D), (layer, 0, 0))]
        + [ANYWHERE] * 3,
        out_specs=(fixed((count, D)),)
        + packs.specs()
        + (fixed((1, D)), fixed((count, D)), fixed((count, D)))
        + (fixed((2, count, D)),) * members,
        scratch=[
            pltpu.VMEM((count, D), BF16),
            pltpu.VMEM((count, D), BF16),
            pltpu.VMEM((D // GROUP, count, 128), F32),
            pltpu.VMEM((count, D), F32),
            pltpu.VMEM((count, units), BF16),
            pltpu.VMEM((count, units), F32),
            pltpu.VMEM((count, D), BF16),
            packs.scratch()[0],
        ]
        + weight_scratch(units)
        + attention_scratch(rows, members, count)
        + attention_back_scratch(rows, members, count)
        + ffn_back_scratch(count)
        + [pltpu.SemaphoreType.DMA((1 + 2 * (units // CHUNK) + 2 * packs.slots,))],
    )(me, inputs, low, own, *others, grad, table, gain, w_qkv, w_out, w_up, w_down)
    cut = 4 + len(packs.shapes())
    return (*made[:cut], made[cut:])


def joined_blocks(batches, seqs, other):
    return ((3 * D // seqs, D // batches), other)


def joined_back(layer, packs, me, inputs, grad_queries, sources, rest):
    grad_middle, table, gain, w_qkv, grad_gain, turned, packed = rest
    row = gain_row(gain, layer)
    low, normed, inverse = normalize(inputs[...].astype(F32), row)
    back = 0.0
    for part in range(3):
        if part == 0:
            value = [lanes[...].astype(F32) * DH ** (-0.5) for lanes in grad_queries]
        else:
            value = [sum([source[part - 1].astype(F32) for source in lanes]) for lanes in sources]
        value = jnp.concatenate(value, 1)
        if part < 2:
            value = rotate(value, table[...], True)
        value = value.astype(BF16)
        turned[part * D : (part + 1) * D, :] = value.T
        back = back + dot_nt(value, w_qkv[0, :, part * D : (part + 1) * D])
    deep, wide = packs.blocks[0]

    def one_block(seq, unused):
        made = dot(turned[pl.ds(pl.multiple_of(seq * deep, deep), deep), :], low).astype(BF16)
        for batch in range(packs.batches):
            packs.put_block(packed, me, 0, batch, seq, made[:, batch * wide : (batch + 1) * wide])
        return unused

    lax.fori_loop(0, packs.seqs, one_block, 0)
    value, gain_sum = normalize_back(back, normed, inverse, row)
    grad_gain[...] = gain_sum
    return grad_middle[...] + value


def split_sources(refs, members, cuts):
    rest = refs[cuts:]
    sources = [rest[cut * members : (cut + 1) * members] for cut in range(cuts)]
    return (refs[:cuts], sources, rest[cuts * members :])


def source_specs(count, members, cuts):
    wide = D // cuts
    return [fixed((count, wide))] * cuts + [fixed((2, count, wide))] * (members * cuts)


def embed_back_kernel(layer, members, cuts, packs, me, inputs, *refs):
    grad_queries, sources, refs = split_sources(refs, members, cuts)
    (
        grad_middle, table, gain, w_qkv, tokens, gain_attn_1, gain_ffn_0, gain_ffn_1,
        stays, leaves, sums, grad_inputs, gain_attn_0, turned, packed, sems,
    ) = refs
    value = joined_back(
        layer, packs, me, inputs, grad_queries, sources,
        (grad_middle, table, gain, w_qkv, gain_attn_0, turned, packed),
    ).astype(BF16)
    grad_inputs[...] = value
    onehot = picks(tokens[...] == iota((VOCAB, tokens.shape[1]), 0))
    packs.put_all(packed, me, 1, dot(onehot, value).astype(BF16), False)
    tiles = D // 128
    for number, ref in enumerate((gain_attn_0, gain_attn_1, gain_ffn_0, gain_ffn_1)):
        for tile in range(tiles):
            place = number * tiles + tile
            sums[place : place + 1, :] = ref[:, tile * 128 : (tile + 1) * 128]
    at = packs.slots * packs.rows
    for number, piece in enumerate(in_two(sums[...])):
        packed[at + number * 4 * tiles : at + (number + 1) * 4 * tiles, :] = piece
    packs.hand_out(packed, (stays, leaves), sems)


def embed_back_call(
    layer, batches, seqs, order, me, inputs, grad_queries, sources, grad_middle, table, gain, w_qkv,
    tokens, *gains,
):
    count = inputs.shape[0]
    cuts, members = len(sources), len(sources[0])
    packs = Packs(batches, seqs, order, joined_blocks(batches, seqs, (VOCAB // batches, D // seqs)))
    summed = 4 * D // 128
    return call(
        functools.partial(embed_back_kernel, layer, members, cuts, packs),
        packs.shapes(2 * summed) + (shape((summed, 128), F32), shape((count, D), BF16)),
        grid=(1,),
        scalars=1,
        in_specs=[fixed((count, D))]
        + source_specs(count, members, cuts)
        + [
            fixed((count, D)),
            fixed(table.shape),
            fixed(gain.shape),
            fixed((1, D, 3 * D), (layer, 0, 0)),
            fixed(tokens.shape),
        ]
        + [fixed((1, D))] * 3,
        out_specs=packs.specs() + (fixed((summed, 128)), fixed((count, D))),
        scratch=[pltpu.VMEM((1, D), F32), pltpu.VMEM((3 * D, count), BF16)] + packs.scratch(2 * summed),
    )(me, inputs, *grad_queries, *sum(sources, []), grad_middle, table, gain, w_qkv, tokens, *gains)


def pool_back_kernel(layer, rows, members, cuts, packs, me, inputs, *refs):
    grad_queries, sources, refs = split_sources(refs, members, cuts)
    grad_middle, table, gain, w_qkv, grouped, w_pool, *refs = refs
    outs = refs[: len(packs.shapes())]
    grad_gain, grad_first, edges, turned, packed, sems = refs[len(outs) :]
    value = joined_back(
        layer, packs, me, inputs, grad_queries, sources,
        (grad_middle, table, gain, w_qkv, grad_gain, turned, packed),
    ).astype(BF16)
    packs.put_all(packed, me, 1, dot(value.T, grouped[...]).astype(BF16), True)
    count = value.shape[0]
    short = count // rows
    span = grad_first.shape[0] // rows
    parts = [dot_nt(value, w_pool[third * D : (third + 1) * D, :]).astype(BF16) for third in range(3)]
    line = iota((2 * rows, count), 0)
    found = 0.0
    for third in range(2):
        pick = (iota((2 * rows, count), 1) == (line // 2) * short) & (line % 2 == third)
        found = found + dot(picks(pick), parts[third])
    edges[...] = found.astype(BF16)
    for row in range(rows):
        total = 0.0
        for third in range(3):
            pick = picks(iota((span, short), 0) == 3 * iota((span, short), 1) + third - 2)
            total = total + dot(pick, parts[third][row * short : (row + 1) * short, :])
        grad_first[row * span : (row + 1) * span, :] = total.astype(BF16)
    packs.hand_out(packed, outs, sems)


def pool_back_call(
    layer, rows, span, batches, seqs, order, me, inputs, grad_queries, sources, grad_middle, table,
    gain, w_qkv, grouped, w_pool,
):
    count = inputs.shape[0]
    cuts, members = len(sources), len(sources[0])
    packs = Packs(batches, seqs, order, joined_blocks(batches, seqs, (D // seqs, 3 * D // batches)))
    return call(
        functools.partial(pool_back_kernel, layer, rows, members, cuts, packs),
        packs.shapes() + (shape((1, D), F32), shape((rows * span, D), BF16), shape((2 * rows, D), BF16)),
        grid=(1,),
        scalars=1,
        in_specs=[fixed((count, D))]
        + source_specs(count, members, cuts)
        + [
            fixed((count, D)),
            fixed(table.shape),
            fixed(gain.shape),
            fixed((1, D, 3 * D), (layer, 0, 0)),
            fixed(grouped.shape),
            fixed(w_pool.shape),
        ],
        out_specs=packs.specs() + (fixed((1, D)), fixed((rows * span, D)), fixed((2 * rows, D))),
        scratch=[pltpu.VMEM((3 * D, count), BF16)] + packs.scratch(),
    )(me, inputs, *grad_queries, *sum(sources, []), grad_middle, table, gain, w_qkv, grouped, w_pool)


def angles(positions):
    half_size = DH // 2
    freqs = 10000.0 ** (-jnp.arange(half_size).astype(jnp.float32) / half_size)
    phase = positions.astype(jnp.float32)[:, None] * jnp.tile(freqs, 4)[None, :]
    lane = jnp.arange(4 * half_size)[None, :]
    sine = jnp.sin(phase) * jnp.where(lane < 3 * half_size, -1.0, 1.0)
    return jnp.where(lane < 2 * half_size, jnp.cos(phase), sine)


class Plan:
    def __init__(self, rows):
        self.S = lax.axis_size("seq")
        self.B = lax.axis_size("batch")
        self.R = rows
        self.P = self.S // rows
        self.s = lax.axis_index("seq")
        self.b = lax.axis_index("batch")
        self.z = self.s // self.P
        self.h = self.s % self.P // 2 * 2 + self.b % 2

    def device(self, pair, z, y, core):
        return (z * self.P + y) * self.B + 2 * pair + core

    def exchange(self, value):
        moves = []
        for apart in range(self.R):
            perm = []
            for pair in range(self.B // 2):
                for z in range(self.R):
                    for y in range(self.P):
                        for core in range(2):
                            other = self.device(pair, z ^ apart, y // 2 * 2 + core, y % 2)
                            perm.append((self.device(pair, z, y, core), other))
            piece = lax.dynamic_index_in_dim(value, self.z ^ apart, 0, keepdims=False)
            moves.append(lax.ppermute(piece, AXES, perm))
        got, bit = moves, 1
        while bit < self.R:
            flip = (self.z // bit) % 2 == 1
            got = [jnp.where(flip, got[n ^ bit], got[n]) for n in range(self.R)]
            bit *= 2
        return (jnp.stack(got), moves)

    def shift(self, value, by):
        perm = []
        for pair in range(self.B // 2):
            for z in range(self.R):
                for batch in range(2):
                    for member in range(self.P):
                        to = (member + by) % self.P
                        perm.append((
                            self.device(pair, z, member // 2 * 2 + batch, member % 2),
                            self.device(pair, z, to // 2 * 2 + batch, to % 2),
                        ))
        return lax.ppermute(value, AXES, perm)

    def others(self, value):
        return [self.shift(value, by) for by in range(1, self.P)]

    def swap(self, value, axis, bit):
        count = lax.axis_size(axis)
        return lax.ppermute(value, axis, [(n, n ^ bit) for n in range(count)])

    def bits(self, axis):
        count = lax.axis_size(axis)
        return [1 << n for n in range(count.bit_length() - 1)]

    def order(self, *axes):
        return [(axis, bit) for axis in axes for bit in self.bits(axis)]


def behind(value, *others):
    return lax.optimization_barrier((value, others))[0]


class Halving:
    def __init__(self, plan, order, stays, leaves=None):
        self.plan, self.order = plan, order
        self.terms, self.count, self.leaves = [(stays, 0, stays.shape[0])], stays.shape[0], []
        if leaves is not None:
            self.leaves = [(leaves, 0, leaves.shape[0])]

    def sum(self, start, stop):
        made = 0.0
        for array, first, last in self.terms:
            if first <= start and stop <= last:
                made = made + array[start - first : stop - first].astype(F32)
        return made

    def add(self, cuts=1):
        self.count //= 2
        size = self.count // cuts
        self.leaves = []
        for cut in reversed(range(cuts)):
            made = self.sum(self.count + cut * size, self.count + (cut + 1) * size).astype(BF16)
            self.leaves.append((made, cut * size, (cut + 1) * size))
        return [made for made, start, stop in self.leaves]

    def send(self):
        (axis, bit), self.order = self.order[0], self.order[1:]
        got = [self.plan.swap(made, axis, bit) for made, start, stop in self.leaves]
        self.terms += [(each, start, stop) for each, (made, start, stop) in zip(got, self.leaves)]
        return got

    def wait(self, *others):
        array, start, stop = self.terms[0]
        self.terms[0] = (behind(array, *others), start, stop)

    def rest(self):
        return [array for array, start, stop in self.terms if start == 0]


def body(
    tokens, loss_mask, cotangent, embed, gain_attn, w_qkv, w_out, gain_ffn, w_up, w_down, w_pool
):
    plan = Plan(tokens.shape[0])
    rows, span = tokens.shape
    short = loss_mask.shape[1]
    members, batches, seqs = plan.P, plan.B, plan.S
    units = w_up.shape[2]
    groups = D // GROUP
    every, along = plan.order("batch", "seq"), plan.order("seq")
    me = jnp.stack([plan.h, plan.b, plan.s]).astype(jnp.int32)

    token_line = plan.exchange(tokens)[0].reshape(1, rows * span)
    token_column = token_line.reshape(rows * span, 1)

    def places(length):
        block = jnp.arange(rows, dtype=jnp.int32)[:, None] * members + plan.h
        return (block * length + jnp.arange(length, dtype=jnp.int32)[None]).reshape(-1)

    first_angles, second_angles = angles(places(span)), angles(places(short))

    ffn_layout = ffn_blocks(batches, seqs, units)
    pool_layout = joined_blocks(batches, seqs, (D // seqs, 3 * D // batches))
    embed_layout = joined_blocks(batches, seqs, (VOCAB // batches, D // seqs))

    def scatter(value, axis):
        return lax.psum_scatter(value, axis, scatter_dimension=0, tiled=True)

    inputs, low, own_0 = embed_call(0, token_column, embed, gain_attn, w_qkv, first_angles)
    others_0 = plan.others(own_0)
    start_grad, start_moves = plan.exchange(cotangent * loss_mask.astype(BF16)[..., None])
    first_low, edges, queries_0, mixed_0, logsum_0, middle_0, hidden_0 = forward_call(
        0, rows, members, me, inputs, low, own_0, others_0, first_angles, gain_ffn, w_qkv, w_out, w_up, w_down
    )
    edge = plan.shift(edges, 1)

    grouped, pooled, low, own_1 = pool_call(
        1, rows, members, me, behind(first_low, *start_moves), edge, w_pool, gain_attn, w_qkv, second_angles
    )
    others_1 = plan.others(own_1)
    second_low, packed, gain_ffn_1, grad_middle, grad_queries, pieces = middle_call(
        1, rows, members, batches, seqs, along, me, pooled, low, own_1, others_1, start_grad.reshape(-1, D),
        second_angles, gain_ffn, w_qkv, w_out, w_up, w_down,
    )
    ffn_1 = Halving(plan, along, scatter(packed, "batch"))
    others = [plan.shift(pieces[by], -by) for by in range(1, members)]
    outs, out_moves = plan.exchange(
        jnp.concatenate([first_low.reshape(rows, span, D), second_low.reshape(rows, short, D)], 1)
    )
    near, far = out_moves[: rows // 2], out_moves[rows // 2 :]
    packed, gain_attn_1, grad_first, edges = pool_back_call(
        1, rows, span, batches, seqs, along, me, pooled, [grad_queries], [[pieces[0]] + others],
        grad_middle, second_angles, gain_attn, w_qkv, grouped, w_pool,
    )
    pool_1 = Halving(plan, along, scatter(packed, "batch"))
    carried = plan.shift(edges, -1)

    stays, leaves, gain_ffn_0, grad_middle, grad_mixed = ffn_back_call(
        0, rows, members, batches, seqs, every, me, behind(grad_first, *near), carried, middle_0, mixed_0,
        hidden_0, gain_ffn, w_out, w_up, w_down,
    )
    ffn_0 = Halving(plan, every, stays, leaves)
    got = ffn_0.send()
    leaving = ffn_1.add()
    got += ffn_1.send()
    got += far[::2]
    grad_mixed = behind(grad_mixed, *leaving)
    grad_queries, sources = [], []
    for group in range(groups):
        grad, pieces = attention_back_call(
            rows, members, me, queries_0, own_0, others_0, mixed_0, logsum_0, grad_mixed, [group]
        )
        grad_queries.append(grad)
        sources.append([pieces[0]] + [plan.shift(pieces[by], -by) for by in range(1, members)])
        ffn_0.wait(grad, *got)
        ffn_1.wait(grad, *got)
        if group == 0:
            leaving = ffn_0.add(2) + ffn_1.add()
            late = ffn_0.send()
            got = [late.pop(0)] + ffn_1.send() + far[1::2]
            grad_mixed = behind(grad_mixed, *leaving)
        else:
            leaving = ffn_1.add()
            got = late + ffn_1.send()
            leaving += ffn_0.add(2)
            got.append(ffn_0.send()[0])
    stays, leaves, sums, grad_inputs = embed_back_call(
        0, batches, seqs, every, me, inputs, [behind(grad, *leaving) for grad in grad_queries], sources,
        grad_middle, first_angles, gain_attn, w_qkv, token_line, gain_attn_1, gain_ffn_0, gain_ffn_1,
    )

    leaves = behind(leaves, *got)
    for step, (axis, bit) in enumerate(every):
        came = plan.swap(leaves, axis, bit)
        if step == 1:
            input_grad = plan.exchange(behind(grad_inputs, leaves).reshape(rows, span, D))[0]
        for chain in (pool_1, ffn_1, ffn_0) if step else (pool_1,):
            if chain.order:
                chain.wait(leaves)
                chain.add()
                chain.send()
        if step < len(every) - 1:
            stays, leaves, sums = halve_call(stays, came, sums)
    made = finish_call(
        (ffn_layout, pool_layout, embed_layout),
        [ffn_0.rest(), ffn_1.rest(), pool_1.rest()],
        stays, sums, came,
    )
    qkv_grad, out_grad, up_grad, down_grad, pool_grad, embed_grad, gain_attn_grad, gain_ffn_grad = made
    return (
        outs[:, :span],
        outs[:, span:],
        input_grad.astype(F32),
        embed_grad,
        gain_attn_grad,
        jnp.swapaxes(qkv_grad, 1, 2),
        jnp.swapaxes(out_grad, 1, 2),
        gain_ffn_grad,
        up_grad,
        jnp.swapaxes(down_grad, 1, 2),
        pool_grad.T,
    )


def solution(mesh):
    in_specs = (
        P("batch", "seq"),
        P("batch", "seq"),
        P("batch", "seq", None),
        P(),
        P(),
        P(),
        P(),
        P(),
        P(),
        P(),
        P(),
    )
    out_specs = (
        P("batch", "seq", None),
        P("batch", "seq", None),
        P("batch", "seq", None),
        P("batch", "seq"),
        P(),
        P(None, "batch", "seq"),
        P(None, "batch", "seq"),
        P(),
        P(None, "batch", "seq"),
        P(None, "batch", "seq"),
        P("batch", "seq"),
    )
    return jax.shard_map(body, mesh=mesh, in_specs=in_specs, out_specs=out_specs, check_vma=False)
```

```python
import functools

import jax
import jax.numpy as jnp
from jax import lax
from jax.experimental import pallas as pl
from jax.experimental.pallas import tpu as pltpu
from jax.sharding import PartitionSpec as P

D = 512
H = 8
DH = 64

epsilon = 1e-05
masked_score = -1e30
AXES = ("seq", "batch")


VOCAB = 256
BF16 = jnp.bfloat16
F32 = jnp.float32
ANYWHERE = pl.BlockSpec(memory_space=pl.ANY)
ROOM = 56 * 1024 * 1024


def dot(left, right):
    return jnp.dot(left, right, preferred_element_type=F32)


def dot_nt(left, right):
    return lax.dot_general(left, right, (((1,), (1,)), ((), ())), preferred_element_type=F32)


def iota(shape, dim):
    return lax.broadcasted_iota(jnp.int32, shape, dim)


def picks(condition):
    return jnp.where(condition, 1.0, 0.0).astype(BF16)


def call(kernel, out_shape, grid, in_specs, out_specs, scratch=(), scalars=0):
    return pl.pallas_call(
        kernel,
        out_shape=out_shape,
        grid_spec=pltpu.PrefetchScalarGridSpec(
            num_scalar_prefetch=scalars,
            grid=grid,
            in_specs=in_specs,
            out_specs=out_specs,
            scratch_shapes=scratch,
        ),
        compiler_params=pltpu.CompilerParams(vmem_limit_bytes=ROOM),
    )


def shape(dims, dtype):
    return jax.ShapeDtypeStruct(dims, dtype)


def fixed(block, index=None, buffers=1):
    place = index or (0,) * len(block)
    return pl.BlockSpec(block, lambda *unused: place, pipeline_mode=pl.Buffered(buffers))


def gain_row(ref, layer):
    return ref[...].astype(F32)[layer : layer + 1]


def normalize(inputs, gain):
    centred = inputs - jnp.mean(inputs, -1, keepdims=True)
    inverse = lax.rsqrt(jnp.mean(centred * centred, -1, keepdims=True) + epsilon)
    normed = centred * inverse
    return ((normed * gain).astype(BF16), normed, inverse)


def normalize_back(grad, normed, inverse, gain):
    scaled = grad * gain
    result = inverse * (
        scaled
        - jnp.mean(scaled, -1, keepdims=True)
        - normed * jnp.mean(scaled * normed, -1, keepdims=True)
    )
    return (result, jnp.sum(grad * normed, axis=0, keepdims=True))


def rotate(inputs, table, back=False):
    width = inputs.shape[1]
    turned = pltpu.roll(table, DH, 1)
    early = iota(table.shape, 1) < DH
    cosine, sine = jnp.where(early, table, turned), jnp.where(early, turned, table)
    if back:
        sine = -sine
    count = width // 128
    first = iota(inputs.shape, 1) % DH < DH // 2
    other = jnp.where(
        first, pltpu.roll(inputs, width - DH // 2, 1), pltpu.roll(inputs, DH // 2, 1)
    )
    return inputs * jnp.concatenate([cosine] * count, 1) + other * jnp.concatenate([sine] * count, 1)


def gelu_both(hidden):
    scale = 0.7978845608028654
    square = hidden * hidden
    tanh = jnp.tanh(scale * hidden * (1.0 + 0.044715 * square))
    half = 0.5 + 0.5 * tanh
    slope = half + (0.5 * scale) * hidden * (1.0 - tanh * tanh) * (1.0 + 0.134145 * square)
    return (hidden * half, slope)


def layout(blocks):
    starts, at = [], 0
    for deep, wide in blocks:
        starts.append(at)
        at += deep * -(-wide // 128)
    return starts, at


def unpacked(slot, blocks):
    made = []
    for (deep, wide), start in zip(blocks, layout(blocks)[0]):
        tiles = [
            slot[start + tile * deep : start + (tile + 1) * deep, : min(128, wide - tile * 128)]
            for tile in range(-(-wide // 128))
        ]
        made.append(tiles[0] if len(tiles) == 1 else jnp.concatenate(tiles, 1))
    return made


def slot_of(order, axis, place, own):
    if all(name != axis for name, bit in order):
        return place << len(order)
    slot, apart = 0, place ^ own
    for number, (name, bit) in enumerate(order):
        if name == axis:
            slot = slot + ((apart // bit) % 2) * (1 << (len(order) - 1 - number))
    return slot


class Packs:
    def __init__(self, batches, seqs, order, blocks):
        self.batches, self.seqs, self.order, self.blocks = batches, seqs, order, blocks
        self.starts, self.rows = layout(blocks)
        self.slots = batches * seqs
        self.whole = len(order) < 2 or batches * seqs != 1 << len(order)

    def put(self, packed, slot, start, block):
        deep, wide = block.shape
        for tile in range(-(-wide // 128)):
            piece = block[:, tile * 128 : min(wide, (tile + 1) * 128)]
            first = pl.multiple_of(slot * self.rows + (start + tile * deep), 16)
            packed[pl.ds(first, deep), : piece.shape[1]] = piece

    def put_block(self, packed, me, number, batch, seq, block):
        if self.order:
            slot = slot_of(self.order, "batch", batch, me[1]) + slot_of(self.order, "seq", seq, me[2])
        else:
            slot = batch * self.seqs + seq
        self.put(packed, slot, self.starts[number], block)

    def put_all(self, packed, me, number, made, swapped):
        deep, wide = self.blocks[number]
        for line in range(made.shape[0] // deep):
            for column in range(made.shape[1] // wide):
                batch, seq = (column, line) if swapped else (line, column)
                block = made[line * deep : (line + 1) * deep, column * wide : (column + 1) * wide]
                self.put_block(packed, me, number, batch, seq, block)

    def send(self, packed, outs, moves, first, last):
        for slot in range(self.slots):
            at, out = slot * self.rows, outs[0]
            to = at
            if len(outs) == 2 and slot >= self.slots // 2:
                to, out = at - self.slots // 2 * self.rows, outs[1]
            rows = last - first
            moves.start(packed.at[pl.ds(at + first, rows)], out.at[pl.ds(to + first, rows)])

    def shapes(self, extra=0):
        if self.whole:
            return (shape((self.slots * self.rows, 128), BF16),)
        half = self.slots * self.rows // 2
        return (shape((half, 128), BF16), shape((half + extra, 128), BF16))

    def specs(self):
        return (ANYWHERE,) * len(self.shapes())

    def scratch(self, extra=0):
        return [pltpu.VMEM((self.slots * self.rows + extra, 128), BF16), pltpu.SemaphoreType.DMA((2,))]


def in_two(value):
    high = value.astype(BF16)
    return high, (value - high.astype(F32)).astype(BF16)


def halve_kernel(kept, got, sums, stays, leaves, made):
    size = kept.shape[0]
    half = size // 2
    stays[...] = (kept[:half, :].astype(F32) + got[:half, :].astype(F32)).astype(BF16)
    leaves[:half, :] = (kept[half:, :].astype(F32) + got[half:size, :].astype(F32)).astype(BF16)
    made[...] = add_sums(sums[...], got, size)
    high, low = in_two(made[...])
    leaves[half : half + high.shape[0], :] = high
    leaves[half + high.shape[0] :, :] = low


def add_sums(own, got, at):
    count = own.shape[0]
    high, low = in_two(own)
    own = high.astype(F32) + low.astype(F32)
    return own + (got[at : at + count, :].astype(F32) + got[at + count : at + 2 * count, :].astype(F32))


def halve_call(kept, got, sums):
    half = kept.shape[0] // 2
    operands = (kept, got, sums)
    outs = (
        shape((half, 128), BF16),
        shape((half + 2 * sums.shape[0], 128), BF16),
        shape(sums.shape, F32),
    )
    return call(
        halve_kernel,
        outs,
        grid=(1,),
        in_specs=[fixed(each.shape) for each in operands],
        out_specs=tuple(fixed(each.shape) for each in outs),
    )(*operands)


def spread_kernel(kept, got, sums, own, made, *leaves):
    size, rows = kept.shape[0], own.shape[0]
    made[...] = add_sums(sums[...], got, size)
    high, low = in_two(made[...])
    for slot in range(size // rows):
        lines = slice(slot * rows, (slot + 1) * rows)
        value = (kept[lines, :].astype(F32) + got[lines, :].astype(F32)).astype(BF16)
        if slot == 0:
            own[...] = value
        else:
            out = leaves[slot - 1]
            out[:rows, :] = value
            out[rows : rows + high.shape[0], :] = high
            out[rows + high.shape[0] :, :] = low


def spread_call(rows, kept, got, sums):
    operands = (kept, got, sums)
    outs = (shape((rows, 128), BF16), shape(sums.shape, F32))
    outs += (shape((rows + 2 * sums.shape[0], 128), BF16),) * (kept.shape[0] // rows - 1)
    made = call(
        spread_kernel,
        outs,
        grid=(1,),
        in_specs=[fixed(each.shape) for each in operands],
        out_specs=tuple(fixed(each.shape) for each in outs),
    )(*operands)
    return made[0], made[1], made[2:]


def pairwise(values):
    while len(values) > 1:
        values = [values[n] + values[n + 1] for n in range(0, len(values), 2)]
    return values[0]


def finish_kernel(layouts, counts, *refs):
    terms = []
    for count in counts:
        terms.append(sum([ref[...].astype(F32) for ref in refs[:count]]))
        refs = refs[count:]
    qkv_0, sums, *came = refs[:-8]
    qkv_out, out_out, up_out, down_out, pool_out, embed_out, gain_attn, gain_ffn = refs[-8:]
    for number in range(2):
        up_out[number], down_out[number], out_out[number] = unpacked(terms[number], layouts[0])
    qkv_out[1], pool_out[...] = unpacked(terms[2], layouts[1])
    at, count = qkv_0.shape[0], sums.shape[0]
    slot = pairwise([each[:at, :].astype(F32) for each in (qkv_0, *came)])
    qkv_out[0], embed_out[...] = unpacked(slot, layouts[2])
    high, low = in_two(sums[...])
    made = [high.astype(F32) + low.astype(F32)]
    for each in came:
        made.append(each[at : at + count, :].astype(F32) + each[at + count :, :].astype(F32))
    made = pairwise(made)
    tiles = D // 128
    for number, ref in enumerate((gain_attn, gain_attn, gain_ffn, gain_ffn)):
        for tile in range(tiles):
            place = number * tiles + tile
            ref[number % 2 : number % 2 + 1, tile * 128 : (tile + 1) * 128] = made[place : place + 1, :]


def finish_call(layouts, terms, *rest):
    (up, down, out), (qkv, pool), (unused, embed) = layouts
    dims = [(2,) + qkv, (2,) + out, (2,) + up, (2,) + down, pool, embed, (2, D), (2, D)]
    specs = []
    for number, group in enumerate(terms):
        specs += [fixed((layout(layouts[number // 2])[1], 128))] * len(group)
    return call(
        functools.partial(finish_kernel, layouts, [len(group) for group in terms]),
        tuple(shape(each, F32) for each in dims),
        grid=(1,),
        in_specs=specs + [fixed(each.shape) for each in rest],
        out_specs=tuple(fixed(each) for each in dims),
    )(*sum(terms, []), *rest)


def embed_kernel(layer, tokens, embed, gain, w_qkv, table, inputs, low, both):
    part = pl.program_id(0)

    @pl.when(part == 0)
    def first():
        onehot = picks(tokens[...] == iota((embed.shape[0], tokens.shape[1]), 0))
        value = lax.dot_general(onehot, embed[...], (((0,), (0,)), ((), ())), preferred_element_type=F32)
        inputs[...] = value.astype(BF16)
        low[...] = normalize(value, gain_row(gain, layer))[0]

    joined = dot(low[...], w_qkv[0])

    @pl.when(part == 0)
    def keys():
        both[0] = rotate(joined, table[...]).astype(BF16)

    @pl.when(part == 1)
    def values():
        both[0] = joined.astype(BF16)


def embed_call(layer, tokens, embed, gain, w_qkv, table):
    count = tokens.shape[1]
    return call(
        functools.partial(embed_kernel, layer),
        (shape((count, D), BF16), shape((count, D), BF16), shape((2, count, D), BF16)),
        grid=(2,),
        in_specs=[
            fixed(tokens.shape),
            fixed(embed.shape),
            fixed(gain.shape),
            pl.BlockSpec((1, D, D), lambda part: (layer, 0, part + 1)),
            fixed(table.shape),
        ],
        out_specs=(
            fixed((count, D)),
            fixed((count, D)),
            pl.BlockSpec((1, count, D), lambda part: (part, 0, 0)),
        ),
    )(tokens, embed, gain, w_qkv, table)


def pool_kernel(layer, rows, members, me, first, edge, w_pool, gain, w_qkv, table, grouped, pooled, low, both):
    span = first.shape[0] // rows
    count = pooled.shape[0]
    short = count // rows
    late = jnp.where(me[0] == 0, 1, 0)
    total = jnp.zeros((count, D), F32)
    for third in range(3):
        pick = picks(iota((short, span), 1) == 3 * iota((short, span), 0) + third - 2)
        piece = jnp.concatenate(
            [dot(pick, first[row * span : (row + 1) * span, :]) for row in range(rows)], 0
        )
        if third < 2:
            place = iota((count, 2 * rows), 0) == (iota((count, 2 * rows), 1) // 2 + late) * short
            place = picks(place & (iota((count, 2 * rows), 1) % 2 == third))
            piece = piece + dot(place, edge[...])
        piece = piece.astype(BF16)
        grouped[:, third * D : (third + 1) * D] = piece
        total = total + dot(piece, w_pool[third * D : (third + 1) * D, :])
    pooled[...] = total
    low[...] = normalize(total, gain_row(gain, layer))[0]
    both[0] = rotate(dot(low[...], w_qkv[0, :, D : 2 * D]), table[...]).astype(BF16)
    both[1] = dot(low[...], w_qkv[0, :, 2 * D :]).astype(BF16)


def pool_call(layer, rows, members, me, first, edge, w_pool, gain, w_qkv, table):
    count = table.shape[0]
    return call(
        functools.partial(pool_kernel, layer, rows, members),
        (
            shape((count, 3 * D), BF16),
            shape((count, D), F32),
            shape((count, D), BF16),
            shape((2, count, D), BF16),
        ),
        grid=(1,),
        scalars=1,
        in_specs=[
            fixed(first.shape),
            fixed(edge.shape),
            fixed(w_pool.shape),
            fixed(gain.shape),
            fixed((1, D, 3 * D), (layer, 0, 0)),
            fixed(table.shape),
        ],
        out_specs=(fixed((count, 3 * D)), fixed((count, D)), fixed((count, D)), fixed((2, count, D))),
    )(me, first, edge, w_pool, gain, w_qkv, table)


GROUP = 256
HEADS = GROUP // DH


def fill_keys(rows, members, own, others, keys, values):
    span = own.shape[1] // rows
    for row in range(rows):
        for by, source in enumerate([own, *others]):
            start = (row * members + by) * span
            keys[start : start + span, :] = source[0, row * span : (row + 1) * span, :]
            values[start : start + span, :] = source[1, row * span : (row + 1) * span, :]


def tiles_of(rows, members, span):
    step = min(rows, max(1, 256 // span))
    return [(first, min(rows, first + step)) for first in range(0, rows, step)]


def heads_at_once(rows, members, span):
    size = sum((last - first) * span * last * members * span * 4 for first, last in tiles_of(rows, members, span))
    return max(count for count in (1, 2, HEADS) if count == 1 or count * size <= 12 << 20)


def bias_shape(rows, members, span):
    first, last = tiles_of(rows, members, span)[0]
    return ((last - first) * span, (last - first) * members * span)


def turned_shape(rows, members, span):
    tiles = tiles_of(rows, members, span)
    return (len(tiles), GROUP, rows * span)


def fill_bias(member, members, span, bias):
    line, column = iota(bias.shape, 0), iota(bias.shape, 1)
    width = members * span
    by = column % width // span
    own = (by == 0) & (column % span <= line % span)
    same = own | ((by > 0) & ((member + by) % members < member))
    seen = (column // width < line // span) | ((column // width == line // span) & same)
    bias[...] = jnp.where(seen, 0.0, masked_score)


def stacked(block, masks):
    return jnp.concatenate([block * mask for mask in masks], 0)


def score(stack, keys, bias, start, end):
    scores = dot_nt(stack, keys[0:end, :])
    last = scores[:, start:] + jnp.concatenate([bias[...]] * (stack.shape[0] // bias.shape[0]), 0)
    return jnp.concatenate([scores[:, :start], last], 1) if start else last


def unstacked(stack, lanes, held):
    count = held.shape[0]
    for number, mine in enumerate(lanes):
        held = jnp.where(mine, stack[number * count : (number + 1) * count, :], held)
    return held


def attention_part(rows, members, queries, own, *refs):
    others = refs[: members - 1]
    mixed, logsum, keys, values, bias, total = refs[members - 1 :]
    span = queries.shape[0] // rows
    width = members * span
    tiles = tiles_of(rows, members, span)
    fill_keys(rows, members, own, others, keys, values)
    logsum[...] = jnp.zeros_like(logsum)

    at_once = heads_at_once(rows, members, span)

    def some_heads(turn, unused):
        heads = [turn * at_once + number for number in range(at_once)]
        lanes = [iota((1, GROUP), 1) // DH == head for head in heads]
        masks = [picks(mine) for mine in lanes]
        blocks = [slice(first * span, last * span) for first, last in tiles]
        scores = [
            score(stacked(queries[block, :], masks), keys, bias, first * width, last * width)
            for block, (first, last) in zip(blocks, tiles)
        ]
        highest = [jnp.max(value, -1, keepdims=True) for value in scores]
        expon = [jnp.exp(value - most) for value, most in zip(scores, highest)]
        totals = [jnp.sum(value, -1, keepdims=True) for value in expon]
        outs = [
            dot(value.astype(BF16), values[0 : last * width, :]) * (1.0 / whole)
            for value, whole, (first, last) in zip(expon, totals, tiles)
        ]
        for block, out, most, whole in zip(blocks, outs, highest, totals):
            total[block, :] = unstacked(out, lanes, total[block, :])
            logs = jnp.broadcast_to(most + jnp.log(whole), (out.shape[0], 128))
            places = [iota((1, 128), 1) == head for head in heads]
            logsum[0, block, :] = unstacked(logs, places, logsum[0, block, :])
        return unused

    lax.fori_loop(0, HEADS // at_once, some_heads, 0)
    mixed[...] = total[...].astype(BF16)


def lane_group(ndim, block, base=0):
    return pl.BlockSpec(block, lambda group, *unused: (0,) * (ndim - 1) + (group + base,))


def lane_part(ref, group):
    lanes = pl.ds(group * GROUP, GROUP)
    return ref.at[:, lanes] if len(ref.shape) == 2 else ref.at[:, :, lanes]


def attention_scratch(rows, members, count):
    span = count // rows
    return [
        pltpu.VMEM((members * count, GROUP), BF16),
        pltpu.VMEM((members * count, GROUP), BF16),
        pltpu.VMEM(bias_shape(rows, members, span), F32),
        pltpu.VMEM((count, GROUP), F32),
    ]


def attention_back_scratch(rows, members, count):
    span = count // rows
    return [
        pltpu.VMEM(turned_shape(rows, members, span), BF16),
        pltpu.VMEM(turned_shape(rows, members, span), BF16),
        pltpu.VMEM((GROUP, members * count), F32),
        pltpu.VMEM((GROUP, members * count), F32),
    ]


def attention_back_kernel(rows, members, me, queries, own, *refs):
    fill_bias(me[0], members, queries.shape[0] // rows, refs[-6])
    attention_back_part(rows, members, queries, own, *refs)


def attention_back_part(rows, members, queries, own, *refs):
    others = refs[: members - 1]
    mixed, logsum, grad_mixed, grad_queries, *rest = refs[members - 1 :]
    pieces = rest[:members]
    keys, values, bias, total, turned, turned_grad, grad_keys, grad_values = rest[members:]
    span = queries.shape[0] // rows
    width = members * span
    fill_keys(rows, members, own, others, keys, values)
    tiles = tiles_of(rows, members, span)
    for tile, (first, last) in enumerate(tiles):
        lines = (rows - first) * span
        turned[tile, :, 0:lines] = queries[first * span :, :].T
        turned_grad[tile, :, 0:lines] = grad_mixed[first * span :, :].T

    at_once = heads_at_once(rows, members, span)

    def some_heads(turn, unused):
        heads = [turn * at_once + number for number in range(at_once)]
        lanes = [iota((1, GROUP), 1) // DH == head for head in heads]
        masks = [picks(mine) for mine in lanes]
        blocks = [slice(first * span, last * span) for first, last in tiles]
        grads = [stacked(grad_mixed[block, :], masks) for block in blocks]
        scores = [
            score(stacked(queries[block, :], masks), keys, bias, first * width, last * width)
            for block, (first, last) in zip(blocks, tiles)
        ]
        grad_probs = [dot_nt(grad, values[0 : last * width, :]) for grad, (first, last) in zip(grads, tiles)]
        sums, deltas = [], []
        for block, grad in zip(blocks, grads):
            logs = logsum[0, block, :]
            sums.append(
                jnp.concatenate(
                    [
                        jnp.sum(jnp.where(iota(logs.shape, 1) == head, logs, 0.0), -1, keepdims=True)
                        for head in heads
                    ],
                    0,
                )
            )
            product = grad.astype(F32) * jnp.concatenate([mixed[block, :].astype(F32)] * at_once, 0)
            deltas.append(jnp.sum(product, -1, keepdims=True))
        probs = [jnp.exp(value - whole) for value, whole in zip(scores, sums)]
        grad_scores = [
            (prob * (grad - delta)).astype(BF16) for prob, grad, delta in zip(probs, grad_probs, deltas)
        ]
        for block, grad, (first, last) in zip(blocks, grad_scores, tiles):
            total[block, :] = unstacked(dot(grad, keys[0 : last * width, :]), lanes, total[block, :])
        probs = [prob.astype(BF16) for prob in probs]
        for number in range(at_once):
            mine = pl.ds(pl.multiple_of((turn * at_once + number) * DH, DH), DH)
            for tile, (first, last) in enumerate(tiles):
                columns = slice(first * width, last * width)
                lines = (rows - first) * span
                for source, made, into in (
                    (turned, grad_scores, grad_keys),
                    (turned_grad, probs, grad_values),
                ):
                    later = []
                    for each in made[tile:]:
                        size = each.shape[0] // at_once
                        later.append(each[number * size : (number + 1) * size, columns])
                    into[mine, columns] = dot(source[tile, mine, 0:lines], jnp.concatenate(later, 0))
        return unused

    lax.fori_loop(0, HEADS // at_once, some_heads, 0)
    grad_queries[...] = total[...].astype(BF16)
    for number, source in enumerate((grad_keys, grad_values)):
        made = source[...].astype(BF16).T
        for row in range(rows):
            for by, piece in enumerate(pieces):
                start = (row * members + by) * span
                piece[number, row * span : (row + 1) * span, :] = made[start : start + span, :]


def attention_back_call(rows, members, me, queries, own, others, mixed, logsum, grad_mixed, groups):
    count = queries.shape[0]
    base, wide = groups[0], len(groups) * GROUP
    made = call(
        functools.partial(attention_back_kernel, rows, members),
        (shape((count, wide), BF16),) + (shape((2, count, wide), BF16),) * members,
        grid=(len(groups),),
        scalars=1,
        in_specs=[lane_group(2, (count, GROUP), base)]
        + [lane_group(3, (2, count, GROUP), base)] * members
        + [
            lane_group(2, (count, GROUP), base),
            pl.BlockSpec((1, count, 128), lambda group, *unused: (group + base, 0, 0)),
            lane_group(2, (count, GROUP), base),
        ],
        out_specs=(lane_group(2, (count, GROUP)),) + (lane_group(3, (2, count, GROUP)),) * members,
        scratch=attention_scratch(rows, members, count) + attention_back_scratch(rows, members, count),
    )(me, queries, own, *others, mixed, logsum, grad_mixed)
    return (made[0], made[1:])


CHUNK = 512


class Moves:
    def __init__(self, sems, first=0):
        self.sems, self.taken, self.open = sems, first, []

    def start(self, source, target):
        copy = pltpu.make_async_copy(source, target, self.sems.at[self.taken])
        copy.start()
        self.open.append(copy)
        self.taken += 1
        return copy

    def end(self):
        for copy in self.open:
            copy.wait()
        self.open = []


class Weights:
    def __init__(self, sems, layer, sources, held):
        self.sems, self.layer, self.sources, self.held = sems, layer, sources, held
        self.chunks = held[1].shape[1] // CHUNK
        self.copies = 1 + 2 * self.chunks

    def pair(self, name, part=0):
        (w_out, w_up, w_down), (out, up, down) = self.sources, self.held
        if name == "out":
            return w_out.at[self.layer], out
        lines = pl.ds(pl.multiple_of(part * CHUNK, CHUNK), CHUNK)
        if name == "up":
            return w_up.at[self.layer, :, lines], up.at[:, lines]
        return w_down.at[self.layer, lines, :], down.at[lines, :]

    def copy(self, name, part=0):
        place = {"out": 0, "up": 1, "down": 2}[name] + 2 * part
        return pltpu.make_async_copy(*self.pair(name, part), self.sems.at[place])

    def start(self):
        self.copy("out").start()
        for part in range(self.chunks):
            self.copy("up", part).start()
            self.copy("down", part).start()

    def wait(self, name, part=0):
        self.copy(name, part).wait()

    def get(self, name, part=0):
        return self.pair(name, part)[1][...]


def weight_scratch(units):
    return [pltpu.VMEM((D, D), BF16), pltpu.VMEM((D, units), BF16), pltpu.VMEM((units, D), BF16)]


def edge_rows(made, rows):
    count = made.shape[0]
    span = count // rows
    line = iota((2 * rows, count), 0)
    pick = picks(iota((2 * rows, count), 1) == (line // 2 + 1) * span - 2 + line % 2)
    return dot(pick, made).astype(BF16)


def make_queries(low, w_qkv, table):
    joined = dot(low[...], w_qkv[0])
    return (rotate(joined, table[...]) * DH ** (-0.5)).astype(BF16)


def attend(rows, members, me, queries, own, others, mixed, logsum, scratch):
    fill_bias(me[0], members, queries.shape[0] // rows, scratch[2])
    for group in range(D // GROUP):
        sources = [lane_part(each, group) for each in (queries, own, *others, mixed)]
        attention_part(rows, members, *sources, logsum.at[pl.ds(group, 1)], *scratch)


def forward_kernel(layer, rows, members, me, inputs, low, own, *refs):
    others = refs[: members - 1]
    (
        table, gain, w_qkv, w_out, w_up, w_down,
        output, edges, queries_out, mixed_out, logsum_out, middle_out, hidden_out,
        queries, mixed, logsum, middle, hidden, low_now, sum_now, *scratch,
    ) = refs[members - 1 :]
    held, attention, sems = scratch[:3], scratch[3:7], scratch[7]
    weights = Weights(sems, layer, (w_out, w_up, w_down), held)
    moves = Moves(sems, weights.copies)
    weights.start()
    queries[...] = make_queries(low, w_qkv, table)
    moves.start(queries, queries_out)
    attend(rows, members, me, queries, own, others, mixed, logsum, attention)
    moves.start(mixed, mixed_out)
    moves.start(logsum, logsum_out)
    weights.wait("out")
    total = inputs[...].astype(F32) + dot(mixed[...], weights.get("out"))
    middle[...] = total
    moves.start(middle, middle_out)
    normed = normalize(total, gain_row(gain, layer))[0]
    low_now[...] = normed
    sum_now[...] = total

    def one_part(part, unused):
        weights.wait("up", part)
        made = dot(low_now[...], weights.get("up", part))
        lanes = pl.ds(pl.multiple_of(part * CHUNK, CHUNK), CHUNK)
        hidden[:, lanes] = made.astype(BF16)
        weights.wait("down", part)
        sum_now[...] += dot(gelu_both(made)[0].astype(BF16), weights.get("down", part))
        return unused

    lax.fori_loop(0, weights.chunks, one_part, 0)
    moves.start(hidden, hidden_out)
    made = sum_now[...].astype(BF16)
    output[...] = made
    edges[...] = edge_rows(made, rows)
    moves.end()


def forward_call(layer, rows, members, me, inputs, low, own, others, table, gain, w_qkv, w_out, w_up, w_down):
    count = inputs.shape[0]
    units = w_up.shape[2]
    handed = [
        ((count, D), BF16), ((count, D), BF16), ((D // GROUP, count, 128), F32),
        ((count, D), F32), ((count, units), BF16),
    ]
    return call(
        functools.partial(forward_kernel, layer, rows, members),
        (shape((count, D), BF16), shape((2 * rows, D), BF16)) + tuple(shape(*each) for each in handed),
        grid=(1,),
        scalars=1,
        in_specs=[fixed((count, D))] * 2
        + [fixed((2, count, D))] * members
        + [fixed(table.shape), fixed(gain.shape), fixed((1, D, D), (layer, 0, 0))]
        + [ANYWHERE] * 3,
        out_specs=(fixed((count, D)), fixed((2 * rows, D))) + (ANYWHERE,) * len(handed),
        scratch=[pltpu.VMEM(*each) for each in handed]
        + [pltpu.VMEM((count, D), BF16), pltpu.VMEM((count, D), F32)]
        + weight_scratch(units)
        + attention_scratch(rows, members, count)
        + [pltpu.SemaphoreType.DMA((6 + 2 * (units // CHUNK),))],
    )(me, inputs, low, own, *others, table, gain, w_qkv, w_out, w_up, w_down)


def ffn_blocks(batches, seqs, units):
    return ((D // batches, units // seqs), (D // seqs, units // batches), (D // seqs, D // batches))


def ffn_back(layer, packs, me, middle, mixed, parts, weights, gain, packed, outs, moves, scratch, unroll):
    grad, turned_low, turned_grad, total = scratch
    row = gain_row(gain, layer)
    low, normed, inverse = normalize(middle[...], row)
    turned_low[...] = low.T
    middle[...] = normed
    turned_grad[...] = grad[...].T
    total[...] = jnp.zeros_like(total)

    def one_part(part, unused):
        active, slope = parts(part)
        grad_hidden = (dot_nt(grad[...], weights.get("down", part)) * slope).astype(BF16)
        made = dot(turned_grad[...], active.astype(BF16)).astype(BF16)
        deep, wide = packs.blocks[1]
        for column in range(CHUNK // wide):
            for seq in range(packs.seqs):
                block = made[seq * deep : (seq + 1) * deep, column * wide : (column + 1) * wide]
                packs.put_block(packed, me, 1, part * (CHUNK // wide) + column, seq, block)
        made = dot(turned_low[...], grad_hidden).astype(BF16)
        deep, wide = packs.blocks[0]
        for column in range(CHUNK // wide):
            for batch in range(packs.batches):
                block = made[batch * deep : (batch + 1) * deep, column * wide : (column + 1) * wide]
                packs.put_block(packed, me, 0, batch, part * (CHUNK // wide) + column, block)
        total[...] += dot_nt(grad_hidden, weights.get("up", part))
        return unused

    lax.fori_loop(0, weights.chunks, one_part, 0, unroll=unroll)
    packs.send(packed, outs, moves, 0, packs.starts[2])
    back, gain_sum = normalize_back(total[...], middle[...], inverse, row)
    grad_middle = grad[...].astype(F32) + back
    branch = grad_middle.astype(BF16)
    packs.put_all(packed, me, 2, dot(branch.T, mixed[...]).astype(BF16), True)
    packs.send(packed, outs, moves, packs.starts[2], packs.rows)
    return grad_middle, dot_nt(branch, weights.get("out")).astype(BF16), gain_sum


def ffn_back_scratch(count):
    return [
        pltpu.VMEM((count, D), BF16),
        pltpu.VMEM((D, count), BF16),
        pltpu.VMEM((D, count), BF16),
        pltpu.VMEM((count, D), F32),
    ]


def ffn_back_kernel(
    layer, rows, members, packs, me, grad_ref, carried, middle_ref, mixed_ref, hidden_ref, gain,
    w_out, w_up, w_down, *refs,
):
    outs = refs[: len(packs.shapes())]
    (
        grad_gain, grad_middle, grad_mixed,
        middle, mixed, hidden, out, up, down, grad, turned_low, turned_grad, total, packed, sems,
    ) = refs[len(outs) :]
    weights = Weights(sems, layer, (w_out, w_up, w_down), (out, up, down))
    moves = Moves(sems, weights.copies + weights.chunks)
    came = moves.start(middle_ref, middle)

    def hidden_copy(part):
        lanes = pl.ds(pl.multiple_of(part * CHUNK, CHUNK), CHUNK)
        return pltpu.make_async_copy(
            hidden_ref.at[:, lanes], hidden.at[:, lanes], sems.at[weights.copies + part]
        )

    for part in range(weights.chunks):
        weights.copy("down", part).start()
        hidden_copy(part).start()
        weights.copy("up", part).start()
    weights.copy("out").start()
    late = moves.start(mixed_ref, mixed)
    moves.open = []
    value = grad_ref[...]
    count = value.shape[0]
    span = count // rows
    early = jnp.where(me[0] == members - 1, 1, 0)
    line = iota((count, 2 * rows), 1)
    place = iota((count, 2 * rows), 0) == (line // 2 + 1 - early) * span - 2 + line % 2
    grad[...] = (value.astype(F32) + dot(picks(place), carried[...])).astype(BF16)

    def parts(part):
        hidden_copy(part).wait()
        weights.wait("down", part)
        weights.wait("up", part)
        lanes = pl.ds(pl.multiple_of(part * CHUNK, CHUNK), CHUNK)
        return gelu_both(hidden[:, lanes].astype(F32))

    came.wait()
    late.wait()
    weights.wait("out")
    made = ffn_back(
        layer, packs, me, middle, mixed, parts, weights, gain, packed, outs, moves,
        (grad, turned_low, turned_grad, total), 1,
    )
    grad_middle[...], grad_mixed[...], grad_gain[...] = made
    moves.end()


def ffn_back_call(
    layer, rows, members, batches, seqs, order, me, grad, carried, middle, mixed, hidden, gain, w_out, w_up, w_down
):
    count = grad.shape[0]
    units = w_up.shape[2]
    packs = Packs(batches, seqs, order, ffn_blocks(batches, seqs, units))
    return call(
        functools.partial(ffn_back_kernel, layer, rows, members, packs),
        packs.shapes() + (shape((1, D), F32), shape((count, D), F32), shape((count, D), BF16)),
        grid=(1,),
        scalars=1,
        in_specs=[fixed((count, D)), fixed((2 * rows, D)), ANYWHERE, ANYWHERE, ANYWHERE, fixed(gain.shape)]
        + [ANYWHERE] * 3,
        out_specs=packs.specs() + (fixed((1, D)), fixed((count, D)), fixed((count, D))),
        scratch=[pltpu.VMEM((count, D), F32), pltpu.VMEM((count, D), BF16), pltpu.VMEM((count, units), BF16)]
        + weight_scratch(units)
        + ffn_back_scratch(count)
        + [packs.scratch()[0], pltpu.SemaphoreType.DMA((3 + 3 * (units // CHUNK) + 2 * packs.slots,))],
    )(me, grad, carried, middle, mixed, hidden, gain, w_out, w_up, w_down)


def middle_kernel(layer, rows, members, packs, me, inputs, low, own, *refs):
    others = refs[: members - 1]
    (
        grad_ref, table, gain, w_qkv, w_out, w_up, w_down,
        output, *refs,
    ) = refs[members - 1 :]
    outs = refs[: len(packs.shapes())]
    grad_gain, grad_middle, grad_queries, *refs = refs[len(outs) :]
    pieces = refs[:members]
    queries, mixed, logsum, middle, active, slope, grad_mixed, packed, *scratch = refs[members:]
    held, attention, back, ffn, sems = scratch[:3], scratch[3:7], scratch[7:11], scratch[11:15], scratch[15]
    parts = range(w_up.shape[2] // CHUNK)
    weights = Weights(sems, layer, (w_out, w_up, w_down), held)
    moves = Moves(sems, weights.copies)
    weights.start()
    queries[...] = make_queries(low, w_qkv, table)
    attend(rows, members, me, queries, own, others, mixed, logsum, attention)
    weights.wait("out")
    total = inputs[...].astype(F32) + dot(mixed[...], weights.get("out"))
    middle[...] = total
    normed = normalize(total, gain_row(gain, layer))[0]
    for part in parts:
        lanes = pl.ds(part * CHUNK, CHUNK)
        weights.wait("up", part)
        one, other = gelu_both(dot(normed, weights.get("up", part)))
        active[:, lanes], slope[:, lanes] = one.astype(BF16), other
        weights.wait("down", part)
        total = total + dot(active[:, lanes], weights.get("down", part))
    output[...] = total.astype(BF16)
    ffn[0][...] = grad_ref[...]

    def part_of(part):
        lanes = pl.ds(pl.multiple_of(part * CHUNK, CHUNK), CHUNK)
        return active[:, lanes], slope[:, lanes]

    made = ffn_back(
        layer, packs, me, middle, mixed, part_of, weights, gain, packed, outs, moves, ffn, True
    )
    grad_middle[...], grad_mixed[...], grad_gain[...] = made
    for group in range(D // GROUP):
        sources = [lane_part(each, group) for each in (queries, own, *others, mixed)]
        targets = [lane_part(each, group) for each in (grad_mixed, grad_queries, *pieces)]
        attention_back_part(
            rows, members, *sources, logsum.at[pl.ds(group, 1)], *targets, *attention, *back
        )
    moves.end()


def middle_call(
    layer, rows, members, batches, seqs, order, me, inputs, low, own, others, grad, table, gain,
    w_qkv, w_out, w_up, w_down,
):
    count = inputs.shape[0]
    units = w_up.shape[2]
    packs = Packs(batches, seqs, order, ffn_blocks(batches, seqs, units))
    made = call(
        functools.partial(middle_kernel, layer, rows, members, packs),
        (shape((count, D), BF16),)
        + packs.shapes()
        + (shape((1, D), F32), shape((count, D), F32), shape((count, D), BF16))
        + (shape((2, count, D), BF16),) * members,
        grid=(1,),
        scalars=1,
        in_specs=[fixed((count, D))] * 2
        + [fixed((2, count, D))] * members
        + [fixed((count, D)), fixed(table.shape), fixed(gain.shape)]
        + [fixed((1, D, D), (layer, 0, 0))]
        + [ANYWHERE] * 3,
        out_specs=(fixed((count, D)),)
        + packs.specs()
        + (fixed((1, D)), fixed((count, D)), fixed((count, D)))
        + (fixed((2, count, D)),) * members,
        scratch=[
            pltpu.VMEM((count, D), BF16),
            pltpu.VMEM((count, D), BF16),
            pltpu.VMEM((D // GROUP, count, 128), F32),
            pltpu.VMEM((count, D), F32),
            pltpu.VMEM((count, units), BF16),
            pltpu.VMEM((count, units), F32),
            pltpu.VMEM((count, D), BF16),
            packs.scratch()[0],
        ]
        + weight_scratch(units)
        + attention_scratch(rows, members, count)
        + attention_back_scratch(rows, members, count)
        + ffn_back_scratch(count)
        + [pltpu.SemaphoreType.DMA((1 + 2 * (units // CHUNK) + 2 * packs.slots,))],
    )(me, inputs, low, own, *others, grad, table, gain, w_qkv, w_out, w_up, w_down)
    cut = 4 + len(packs.shapes())
    return (*made[:cut], made[cut:])


def joined_blocks(batches, seqs, other):
    return ((3 * D // seqs, D // batches), other)


def joined_back(layer, packs, me, inputs, grad_queries, sources, rest):
    grad_middle, came, table, gain, w_qkv, grad_gain, turned, packed, outs, moves = rest
    row = gain_row(gain, layer)
    low, normed, inverse = normalize(inputs[...].astype(F32), row)
    joined = []
    for part in range(3):
        if part == 0:
            value = [lanes[...].astype(F32) * DH ** (-0.5) for lanes in grad_queries]
        else:
            value = [sum([source[part - 1].astype(F32) for source in lanes]) for lanes in sources]
        value = jnp.concatenate(value, 1)
        if part < 2:
            value = rotate(value, table[...], True)
        joined.append(value.astype(BF16))
        turned[part * D : (part + 1) * D, :] = joined[part].T
    deep, wide = packs.blocks[0]

    def one_block(seq, unused):
        made = dot(turned[pl.ds(pl.multiple_of(seq * deep, deep), deep), :], low).astype(BF16)
        for batch in range(packs.batches):
            packs.put_block(packed, me, 0, batch, seq, made[:, batch * wide : (batch + 1) * wide])
        return unused

    lax.fori_loop(0, packs.seqs, one_block, 0)
    packs.send(packed, outs, moves, 0, packs.starts[1])
    back = 0.0
    for copy in came:
        copy.wait()
    for part in range(3):
        back = back + dot_nt(joined[part], w_qkv[:, part * D : (part + 1) * D])
    value, gain_sum = normalize_back(back, normed, inverse, row)
    grad_gain[...] = gain_sum
    return grad_middle[...] + value


def split_sources(refs, members, cuts):
    rest = refs[cuts:]
    sources = [rest[cut * members : (cut + 1) * members] for cut in range(cuts)]
    return (refs[:cuts], sources, rest[cuts * members :])


def source_specs(count, members, cuts):
    wide = D // cuts
    return [fixed((count, wide))] * cuts + [fixed((2, count, wide))] * (members * cuts)


def embed_back_kernel(layer, members, cuts, packs, me, inputs, *refs):
    grad_queries, sources, refs = split_sources(refs, members, cuts)
    (
        middle_in, table, gain, w_in, tokens, gain_attn_1, gain_ffn_0, gain_ffn_1,
        stays, leaves, sums, grad_inputs, gain_attn_0, turned, grad_middle, w_qkv, packed, sems,
    ) = refs
    moves = Moves(sems)
    came = [moves.start(w_in.at[layer], w_qkv), moves.start(middle_in, grad_middle)]
    moves.open = []
    value = joined_back(
        layer, packs, me, inputs, grad_queries, sources,
        (grad_middle, came, table, gain, w_qkv, gain_attn_0, turned, packed, (stays, leaves), moves),
    ).astype(BF16)
    grad_inputs[...] = value
    onehot = picks(tokens[...] == iota((VOCAB, tokens.shape[1]), 0))
    packs.put_all(packed, me, 1, dot(onehot, value).astype(BF16), False)
    packs.send(packed, (stays, leaves), moves, packs.starts[1], packs.rows)
    tiles = D // 128
    for number, ref in enumerate((gain_attn_0, gain_attn_1, gain_ffn_0, gain_ffn_1)):
        for tile in range(tiles):
            place = number * tiles + tile
            sums[place : place + 1, :] = ref[:, tile * 128 : (tile + 1) * 128]
    at, extra = packs.slots * packs.rows, 8 * tiles
    for number, piece in enumerate(in_two(sums[...])):
        packed[at + number * 4 * tiles : at + (number + 1) * 4 * tiles, :] = piece
    moves.start(packed.at[pl.ds(at, extra)], leaves.at[pl.ds(at // 2, extra)])
    moves.end()


def embed_back_call(
    layer, batches, seqs, order, me, inputs, grad_queries, sources, grad_middle, table, gain, w_qkv,
    tokens, *gains,
):
    count = inputs.shape[0]
    cuts, members = len(sources), len(sources[0])
    packs = Packs(batches, seqs, order, joined_blocks(batches, seqs, (VOCAB // batches, D // seqs)))
    summed = 4 * D // 128
    return call(
        functools.partial(embed_back_kernel, layer, members, cuts, packs),
        packs.shapes(2 * summed) + (shape((summed, 128), F32), shape((count, D), BF16)),
        grid=(1,),
        scalars=1,
        in_specs=[fixed((count, D))]
        + source_specs(count, members, cuts)
        + [ANYWHERE, fixed(table.shape), fixed(gain.shape), ANYWHERE, fixed(tokens.shape)]
        + [fixed((1, D))] * 3,
        out_specs=packs.specs() + (fixed((summed, 128)), fixed((count, D))),
        scratch=[
            pltpu.VMEM((1, D), F32),
            pltpu.VMEM((3 * D, count), BF16),
            pltpu.VMEM((count, D), F32),
            pltpu.VMEM((D, 3 * D), BF16),
            packs.scratch(2 * summed)[0],
            pltpu.SemaphoreType.DMA((3 + 2 * packs.slots,)),
        ],
    )(me, inputs, *grad_queries, *sum(sources, []), grad_middle, table, gain, w_qkv, tokens, *gains)


def pool_back_kernel(layer, rows, members, cuts, packs, me, inputs, *refs):
    grad_queries, sources, refs = split_sources(refs, members, cuts)
    middle_in, table, gain, w_in, grouped_in, pool_in, *refs = refs
    outs = refs[: len(packs.shapes())]
    grad_gain, grad_first, edges, turned, grad_middle, w_qkv, grouped, w_pool, packed, sems = refs[len(outs) :]
    moves = Moves(sems)
    came = [moves.start(w_in.at[layer], w_qkv), moves.start(middle_in, grad_middle)]
    late = [moves.start(grouped_in, grouped), moves.start(pool_in, w_pool)]
    moves.open = []
    value = joined_back(
        layer, packs, me, inputs, grad_queries, sources,
        (grad_middle, came, table, gain, w_qkv, grad_gain, turned, packed, outs, moves),
    ).astype(BF16)
    for copy in late:
        copy.wait()
    packs.put_all(packed, me, 1, dot(value.T, grouped[...]).astype(BF16), True)
    packs.send(packed, outs, moves, packs.starts[1], packs.rows)
    count = value.shape[0]
    short = count // rows
    span = grad_first.shape[0] // rows
    parts = [dot_nt(value, w_pool[third * D : (third + 1) * D, :]).astype(BF16) for third in range(3)]
    line = iota((2 * rows, count), 0)
    found = 0.0
    for third in range(2):
        pick = (iota((2 * rows, count), 1) == (line // 2) * short) & (line % 2 == third)
        found = found + dot(picks(pick), parts[third])
    edges[...] = found.astype(BF16)
    for row in range(rows):
        total = 0.0
        for third in range(3):
            pick = picks(iota((span, short), 0) == 3 * iota((span, short), 1) + third - 2)
            total = total + dot(pick, parts[third][row * short : (row + 1) * short, :])
        grad_first[row * span : (row + 1) * span, :] = total.astype(BF16)
    moves.end()


def pool_back_call(
    layer, rows, span, batches, seqs, order, me, inputs, grad_queries, sources, grad_middle, table,
    gain, w_qkv, grouped, w_pool,
):
    count = inputs.shape[0]
    cuts, members = len(sources), len(sources[0])
    packs = Packs(batches, seqs, order, joined_blocks(batches, seqs, (D // seqs, 3 * D // batches)))
    return call(
        functools.partial(pool_back_kernel, layer, rows, members, cuts, packs),
        packs.shapes() + (shape((1, D), F32), shape((rows * span, D), BF16), shape((2 * rows, D), BF16)),
        grid=(1,),
        scalars=1,
        in_specs=[fixed((count, D))]
        + source_specs(count, members, cuts)
        + [ANYWHERE, fixed(table.shape), fixed(gain.shape), ANYWHERE, ANYWHERE, ANYWHERE],
        out_specs=packs.specs() + (fixed((1, D)), fixed((rows * span, D)), fixed((2 * rows, D))),
        scratch=[
            pltpu.VMEM((3 * D, count), BF16),
            pltpu.VMEM((count, D), F32),
            pltpu.VMEM((D, 3 * D), BF16),
            pltpu.VMEM(grouped.shape, BF16),
            pltpu.VMEM(w_pool.shape, BF16),
            packs.scratch()[0],
            pltpu.SemaphoreType.DMA((4 + 2 * packs.slots,)),
        ],
    )(me, inputs, *grad_queries, *sum(sources, []), grad_middle, table, gain, w_qkv, grouped, w_pool)


def angles(positions):
    half_size = DH // 2
    freqs = 10000.0 ** (-jnp.arange(half_size).astype(jnp.float32) / half_size)
    phase = positions.astype(jnp.float32)[:, None] * jnp.tile(freqs, 4)[None, :]
    lane = jnp.arange(4 * half_size)[None, :]
    sine = jnp.sin(phase) * jnp.where(lane < 3 * half_size, -1.0, 1.0)
    return jnp.where(lane < 2 * half_size, jnp.cos(phase), sine)


class Plan:
    def __init__(self, rows):
        self.S = lax.axis_size("seq")
        self.B = lax.axis_size("batch")
        self.R = rows
        self.P = self.S // rows
        self.s = lax.axis_index("seq")
        self.b = lax.axis_index("batch")
        self.z = self.s // self.P
        self.h = self.s % self.P // 2 * 2 + self.b % 2

    def device(self, pair, z, y, core):
        return (z * self.P + y) * self.B + 2 * pair + core

    def exchange(self, value):
        moves = []
        for apart in range(self.R):
            perm = []
            for pair in range(self.B // 2):
                for z in range(self.R):
                    for y in range(self.P):
                        for core in range(2):
                            other = self.device(pair, z ^ apart, y // 2 * 2 + core, y % 2)
                            perm.append((self.device(pair, z, y, core), other))
            piece = lax.dynamic_index_in_dim(value, self.z ^ apart, 0, keepdims=False)
            moves.append(lax.ppermute(piece, AXES, perm))
        got, bit = moves, 1
        while bit < self.R:
            flip = (self.z // bit) % 2 == 1
            got = [jnp.where(flip, got[n ^ bit], got[n]) for n in range(self.R)]
            bit *= 2
        return (jnp.stack(got), moves)

    def shift(self, value, by):
        perm = []
        for pair in range(self.B // 2):
            for z in range(self.R):
                for batch in range(2):
                    for member in range(self.P):
                        to = (member + by) % self.P
                        perm.append((
                            self.device(pair, z, member // 2 * 2 + batch, member % 2),
                            self.device(pair, z, to // 2 * 2 + batch, to % 2),
                        ))
        return lax.ppermute(value, AXES, perm)

    def others(self, value):
        return [self.shift(value, by) for by in range(1, self.P)]

    def swap(self, value, axis, bit):
        count = lax.axis_size(axis)
        return lax.ppermute(value, axis, [(n, n ^ bit) for n in range(count)])

    def bits(self, axis):
        count = lax.axis_size(axis)
        return [1 << n for n in range(count.bit_length() - 1)]

    def order(self, *axes):
        return [(axis, bit) for axis in axes for bit in self.bits(axis)]


def behind(value, *others):
    return lax.optimization_barrier((value, others))[0]


class Halving:
    def __init__(self, plan, order, stays, leaves=None):
        self.plan, self.order = plan, order
        self.terms, self.count, self.leaves = [(stays, 0, stays.shape[0])], stays.shape[0], []
        if leaves is not None:
            self.leaves = [(leaves, 0, leaves.shape[0])]

    def sum(self, start, stop):
        made = 0.0
        for array, first, last in self.terms:
            if first <= start and stop <= last:
                made = made + array[start - first : stop - first].astype(F32)
        return made

    def add(self, cuts=1):
        self.count //= 2
        size = self.count // cuts
        self.leaves = []
        for cut in reversed(range(cuts)):
            made = self.sum(self.count + cut * size, self.count + (cut + 1) * size).astype(BF16)
            self.leaves.append((made, cut * size, (cut + 1) * size))
        return [made for made, start, stop in self.leaves]

    def send(self):
        (axis, bit), self.order = self.order[0], self.order[1:]
        got = [self.plan.swap(made, axis, bit) for made, start, stop in self.leaves]
        self.terms += [(each, start, stop) for each, (made, start, stop) in zip(got, self.leaves)]
        return got

    def wait(self, *others):
        array, start, stop = self.terms[0]
        self.terms[0] = (behind(array, *others), start, stop)

    def rest(self):
        return [array for array, start, stop in self.terms if start == 0]


def body(
    tokens, loss_mask, cotangent, embed, gain_attn, w_qkv, w_out, gain_ffn, w_up, w_down, w_pool
):
    plan = Plan(tokens.shape[0])
    rows, span = tokens.shape
    short = loss_mask.shape[1]
    members, batches, seqs = plan.P, plan.B, plan.S
    units = w_up.shape[2]
    groups = D // GROUP
    every, along = plan.order("batch", "seq"), plan.order("seq")
    crossed = every[:1] + along[:1] + every[1:-len(along)] + along[1:]
    me = jnp.stack([plan.h, plan.b, plan.s]).astype(jnp.int32)

    token_line = plan.exchange(tokens)[0].reshape(1, rows * span)

    def places(length):
        block = jnp.arange(rows, dtype=jnp.int32)[:, None] * members + plan.h
        return (block * length + jnp.arange(length, dtype=jnp.int32)[None]).reshape(-1)

    first_angles, second_angles = angles(places(span)), angles(places(short))

    ffn_layout = ffn_blocks(batches, seqs, units)
    pool_layout = joined_blocks(batches, seqs, (D // seqs, 3 * D // batches))
    embed_layout = joined_blocks(batches, seqs, (VOCAB // batches, D // seqs))

    def scatter(value, axis):
        return lax.psum_scatter(value, axis, scatter_dimension=0, tiled=True)

    inputs, low, own_0 = embed_call(0, token_line, embed, gain_attn, w_qkv, first_angles)
    others_0 = plan.others(own_0)
    start_grad, start_moves = plan.exchange(cotangent * loss_mask.astype(BF16)[..., None])
    first_low, edges, queries_0, mixed_0, logsum_0, middle_0, hidden_0 = forward_call(
        0, rows, members, me, inputs, low, own_0, others_0, first_angles, gain_ffn, w_qkv, w_out, w_up, w_down
    )
    edge = plan.shift(edges, 1)

    grouped, pooled, low, own_1 = pool_call(
        1, rows, members, me, behind(first_low, *start_moves), edge, w_pool, gain_attn, w_qkv, second_angles
    )
    others_1 = plan.others(own_1)
    second_low, packed, gain_ffn_1, grad_middle, grad_queries, pieces = middle_call(
        1, rows, members, batches, seqs, along, me, pooled, low, own_1, others_1, start_grad.reshape(-1, D),
        second_angles, gain_ffn, w_qkv, w_out, w_up, w_down,
    )
    ffn_1 = Halving(plan, along, scatter(packed, "batch"))
    others = [plan.shift(pieces[by], -by) for by in range(1, members)]
    outs, out_moves = plan.exchange(
        jnp.concatenate([first_low.reshape(rows, span, D), second_low.reshape(rows, short, D)], 1)
    )
    near, far = out_moves[: rows // 2], out_moves[rows // 2 :]
    packed, gain_attn_1, grad_first, edges = pool_back_call(
        1, rows, span, batches, seqs, along, me, pooled, [grad_queries], [[pieces[0]] + others],
        grad_middle, second_angles, gain_attn, w_qkv, grouped, w_pool,
    )
    pool_1 = Halving(plan, along, scatter(packed, "batch"))
    carried = plan.shift(edges, -1)

    stays, leaves, gain_ffn_0, grad_middle, grad_mixed = ffn_back_call(
        0, rows, members, batches, seqs, crossed, me, behind(grad_first, *near), carried, middle_0, mixed_0,
        hidden_0, gain_ffn, w_out, w_up, w_down,
    )
    ffn_0 = Halving(plan, crossed, stays, leaves)
    got = ffn_0.send()
    leaving = ffn_1.add()
    got += ffn_1.send()
    got += far[::2]
    grad_mixed = behind(grad_mixed, *leaving)
    grad_queries, sources = [], []
    for group in range(groups):
        grad, pieces = attention_back_call(
            rows, members, me, queries_0, own_0, others_0, mixed_0, logsum_0, grad_mixed, [group]
        )
        grad_queries.append(grad)
        sources.append([pieces[0]] + [plan.shift(pieces[by], -by) for by in range(1, members)])
        ffn_0.wait(grad, *got)
        ffn_1.wait(grad, *got)
        if group == 0:
            leaving = ffn_0.add(2) + ffn_1.add()
            late = ffn_0.send()
            got = [late.pop(0)] + ffn_1.send() + far[1::2]
            grad_mixed = behind(grad_mixed, *leaving)
        else:
            leaving = ffn_1.add()
            got = late + ffn_1.send()
            leaving += ffn_0.add(2)
            got.append(ffn_0.send()[0])
    stays, leaves, sums, grad_inputs = embed_back_call(
        0, batches, seqs, every, me, inputs, [behind(grad, *leaving) for grad in grad_queries], sources,
        grad_middle, first_angles, gain_attn, w_qkv, token_line, gain_attn_1, gain_ffn_0, gain_ffn_1,
    )

    leaves = behind(leaves, *got)
    for step, (axis, bit) in enumerate(every):
        came = plan.swap(leaves, axis, bit)
        if step == 1:
            input_grad = plan.exchange(behind(grad_inputs, leaves).reshape(rows, span, D))[0]
        for chain in (pool_1, ffn_1, ffn_0) if step else (pool_1,):
            if chain.order:
                chain.wait(leaves)
                chain.add()
                chain.send()
        if step < len(every) - 1:
            stays, leaves, sums = halve_call(stays, came, sums)
    made = finish_call(
        (ffn_layout, pool_layout, embed_layout),
        [ffn_0.rest(), ffn_1.rest(), pool_1.rest()],
        stays, sums, came,
    )
    qkv_grad, out_grad, up_grad, down_grad, pool_grad, embed_grad, gain_attn_grad, gain_ffn_grad = made
    return (
        outs[:, :span],
        outs[:, span:],
        input_grad.astype(F32),
        embed_grad,
        gain_attn_grad,
        jnp.swapaxes(qkv_grad, 1, 2),
        jnp.swapaxes(out_grad, 1, 2),
        gain_ffn_grad,
        up_grad,
        jnp.swapaxes(down_grad, 1, 2),
        pool_grad.T,
    )


def solution(mesh):
    in_specs = (
        P("batch", "seq"),
        P("batch", "seq"),
        P("batch", "seq", None),
        P(),
        P(),
        P(),
        P(),
        P(),
        P(),
        P(),
        P(),
    )
    out_specs = (
        P("batch", "seq", None),
        P("batch", "seq", None),
        P("batch", "seq", None),
        P("batch", "seq"),
        P(),
        P(None, "batch", "seq"),
        P(None, "batch", "seq"),
        P(),
        P(None, "batch", "seq"),
        P(None, "batch", "seq"),
        P("batch", "seq"),
    )
    return jax.shard_map(body, mesh=mesh, in_specs=in_specs, out_specs=out_specs, check_vma=False)
```

```python
import functools

import jax
import jax.numpy as jnp
from jax import lax
from jax.experimental import pallas as pl
from jax.experimental.pallas import tpu as pltpu
from jax.sharding import PartitionSpec as P

D = 512
H = 8
DH = 64

epsilon = 1e-05
masked_score = -1e30
AXES = ("seq", "batch")


VOCAB = 256
BF16 = jnp.bfloat16
F32 = jnp.float32
ANYWHERE = pl.BlockSpec(memory_space=pl.ANY)
ROOM = 56 * 1024 * 1024


def dot(left, right):
    return jnp.dot(left, right, preferred_element_type=F32)


def dot_nt(left, right):
    return lax.dot_general(left, right, (((1,), (1,)), ((), ())), preferred_element_type=F32)


def iota(shape, dim):
    return lax.broadcasted_iota(jnp.int32, shape, dim)


def picks(condition):
    return jnp.where(condition, 1.0, 0.0).astype(BF16)


def call(kernel, out_shape, grid, in_specs, out_specs, scratch=(), scalars=0):
    return pl.pallas_call(
        kernel,
        out_shape=out_shape,
        grid_spec=pltpu.PrefetchScalarGridSpec(
            num_scalar_prefetch=scalars,
            grid=grid,
            in_specs=in_specs,
            out_specs=out_specs,
            scratch_shapes=scratch,
        ),
        compiler_params=pltpu.CompilerParams(vmem_limit_bytes=ROOM),
    )


def shape(dims, dtype):
    return jax.ShapeDtypeStruct(dims, dtype)


def fixed(block, index=None, buffers=1):
    place = index or (0,) * len(block)
    return pl.BlockSpec(block, lambda *unused: place, pipeline_mode=pl.Buffered(buffers))


def gain_row(ref, layer):
    return ref[...].astype(F32)[layer : layer + 1]


def normalize(inputs, gain):
    centred = inputs - jnp.mean(inputs, -1, keepdims=True)
    inverse = lax.rsqrt(jnp.mean(centred * centred, -1, keepdims=True) + epsilon)
    normed = centred * inverse
    return ((normed * gain).astype(BF16), normed, inverse)


def normalize_back(grad, normed, inverse, gain):
    scaled = grad * gain
    result = inverse * (
        scaled
        - jnp.mean(scaled, -1, keepdims=True)
        - normed * jnp.mean(scaled * normed, -1, keepdims=True)
    )
    return (result, jnp.sum(grad * normed, axis=0, keepdims=True))


def rotate(inputs, table, back=False):
    width = inputs.shape[1]
    turned = pltpu.roll(table, DH, 1)
    early = iota(table.shape, 1) < DH
    cosine, sine = jnp.where(early, table, turned), jnp.where(early, turned, table)
    if back:
        sine = -sine
    count = width // 128
    first = iota(inputs.shape, 1) % DH < DH // 2
    other = jnp.where(
        first, pltpu.roll(inputs, width - DH // 2, 1), pltpu.roll(inputs, DH // 2, 1)
    )
    return inputs * jnp.concatenate([cosine] * count, 1) + other * jnp.concatenate([sine] * count, 1)


def gelu_both(hidden):
    scale = 0.7978845608028654
    square = hidden * hidden
    tanh = jnp.tanh(scale * hidden * (1.0 + 0.044715 * square))
    half = 0.5 + 0.5 * tanh
    slope = half + (0.5 * scale) * hidden * (1.0 - tanh * tanh) * (1.0 + 0.134145 * square)
    return (hidden * half, slope)


def layout(blocks):
    starts, at = [], 0
    for deep, wide in blocks:
        starts.append(at)
        at += deep * -(-wide // 128)
    return starts, at


def unpacked(slot, blocks):
    made = []
    for (deep, wide), start in zip(blocks, layout(blocks)[0]):
        tiles = [
            slot[start + tile * deep : start + (tile + 1) * deep, : min(128, wide - tile * 128)]
            for tile in range(-(-wide // 128))
        ]
        made.append(tiles[0] if len(tiles) == 1 else jnp.concatenate(tiles, 1))
    return made


def slot_of(order, axis, place, own):
    if all(name != axis for name, bit in order):
        return place << len(order)
    slot, apart = 0, place ^ own
    for number, (name, bit) in enumerate(order):
        if name == axis:
            slot = slot + ((apart // bit) % 2) * (1 << (len(order) - 1 - number))
    return slot


class Packs:
    def __init__(self, batches, seqs, order, blocks):
        self.batches, self.seqs, self.order, self.blocks = batches, seqs, order, blocks
        self.starts, self.rows = layout(blocks)
        self.slots = batches * seqs
        self.whole = len(order) < 2 or batches * seqs != 1 << len(order)

    def put(self, packed, slot, start, block):
        deep, wide = block.shape
        for tile in range(-(-wide // 128)):
            piece = block[:, tile * 128 : min(wide, (tile + 1) * 128)]
            first = pl.multiple_of(slot * self.rows + (start + tile * deep), 16)
            packed[pl.ds(first, deep), : piece.shape[1]] = piece

    def put_block(self, packed, me, number, batch, seq, block):
        if self.order:
            slot = slot_of(self.order, "batch", batch, me[1]) + slot_of(self.order, "seq", seq, me[2])
        else:
            slot = batch * self.seqs + seq
        self.put(packed, slot, self.starts[number], block)

    def put_all(self, packed, me, number, made, swapped):
        deep, wide = self.blocks[number]
        for line in range(made.shape[0] // deep):
            for column in range(made.shape[1] // wide):
                batch, seq = (column, line) if swapped else (line, column)
                block = made[line * deep : (line + 1) * deep, column * wide : (column + 1) * wide]
                self.put_block(packed, me, number, batch, seq, block)

    def send(self, packed, outs, moves, first, last):
        for slot in range(self.slots):
            at, out = slot * self.rows, outs[0]
            to = at
            if len(outs) == 2 and slot >= self.slots // 2:
                to, out = at - self.slots // 2 * self.rows, outs[1]
            rows = last - first
            moves.start(packed.at[pl.ds(at + first, rows)], out.at[pl.ds(to + first, rows)])

    def shapes(self, extra=0):
        if self.whole:
            return (shape((self.slots * self.rows, 128), BF16),)
        half = self.slots * self.rows // 2
        return (shape((half, 128), BF16), shape((half + extra, 128), BF16))

    def specs(self):
        return (ANYWHERE,) * len(self.shapes())

    def scratch(self, extra=0):
        return [pltpu.VMEM((self.slots * self.rows + extra, 128), BF16), pltpu.SemaphoreType.DMA((2,))]


def in_two(value):
    high = value.astype(BF16)
    return high, (value - high.astype(F32)).astype(BF16)


def halve_kernel(kept, got, sums, stays, leaves, made):
    size = kept.shape[0]
    half = size // 2
    stays[...] = (kept[:half, :].astype(F32) + got[:half, :].astype(F32)).astype(BF16)
    leaves[:half, :] = (kept[half:, :].astype(F32) + got[half:size, :].astype(F32)).astype(BF16)
    made[...] = add_sums(sums[...], got, size)
    high, low = in_two(made[...])
    leaves[half : half + high.shape[0], :] = high
    leaves[half + high.shape[0] :, :] = low


def add_sums(own, got, at):
    count = own.shape[0]
    high, low = in_two(own)
    own = high.astype(F32) + low.astype(F32)
    return own + (got[at : at + count, :].astype(F32) + got[at + count : at + 2 * count, :].astype(F32))


def halve_call(kept, got, sums):
    half = kept.shape[0] // 2
    operands = (kept, got, sums)
    outs = (
        shape((half, 128), BF16),
        shape((half + 2 * sums.shape[0], 128), BF16),
        shape(sums.shape, F32),
    )
    return call(
        halve_kernel,
        outs,
        grid=(1,),
        in_specs=[fixed(each.shape) for each in operands],
        out_specs=tuple(fixed(each.shape) for each in outs),
    )(*operands)


def spread_kernel(kept, got, sums, own, made, *leaves):
    size, rows = kept.shape[0], own.shape[0]
    made[...] = add_sums(sums[...], got, size)
    high, low = in_two(made[...])
    for slot in range(size // rows):
        lines = slice(slot * rows, (slot + 1) * rows)
        value = (kept[lines, :].astype(F32) + got[lines, :].astype(F32)).astype(BF16)
        if slot == 0:
            own[...] = value
        else:
            out = leaves[slot - 1]
            out[:rows, :] = value
            out[rows : rows + high.shape[0], :] = high
            out[rows + high.shape[0] :, :] = low


def spread_call(rows, kept, got, sums):
    operands = (kept, got, sums)
    outs = (shape((rows, 128), BF16), shape(sums.shape, F32))
    outs += (shape((rows + 2 * sums.shape[0], 128), BF16),) * (kept.shape[0] // rows - 1)
    made = call(
        spread_kernel,
        outs,
        grid=(1,),
        in_specs=[fixed(each.shape) for each in operands],
        out_specs=tuple(fixed(each.shape) for each in outs),
    )(*operands)
    return made[0], made[1], made[2:]


def pairwise(values):
    while len(values) > 1:
        values = [values[n] + values[n + 1] for n in range(0, len(values), 2)]
    return values[0]


def finish_kernel(layouts, counts, *refs):
    terms = []
    for count in counts:
        terms.append(sum([ref[...].astype(F32) for ref in refs[:count]]))
        refs = refs[count:]
    qkv_0, sums, *came = refs[:-8]
    qkv_out, out_out, up_out, down_out, pool_out, embed_out, gain_attn, gain_ffn = refs[-8:]
    for number in range(2):
        up_out[number], down_out[number], out_out[number] = unpacked(terms[number], layouts[0])
    qkv_out[1], pool_out[...] = unpacked(terms[2], layouts[1])
    at, count = qkv_0.shape[0], sums.shape[0]
    slot = pairwise([each[:at, :].astype(F32) for each in (qkv_0, *came)])
    qkv_out[0], embed_out[...] = unpacked(slot, layouts[2])
    high, low = in_two(sums[...])
    made = [high.astype(F32) + low.astype(F32)]
    for each in came:
        made.append(each[at : at + count, :].astype(F32) + each[at + count :, :].astype(F32))
    made = pairwise(made)
    tiles = D // 128
    for number, ref in enumerate((gain_attn, gain_attn, gain_ffn, gain_ffn)):
        for tile in range(tiles):
            place = number * tiles + tile
            ref[number % 2 : number % 2 + 1, tile * 128 : (tile + 1) * 128] = made[place : place + 1, :]


def finish_call(layouts, terms, *rest):
    (up, down, out), (qkv, pool), (unused, embed) = layouts
    dims = [(2,) + qkv, (2,) + out, (2,) + up, (2,) + down, pool, embed, (2, D), (2, D)]
    specs = []
    for number, group in enumerate(terms):
        specs += [fixed((layout(layouts[number // 2])[1], 128))] * len(group)
    return call(
        functools.partial(finish_kernel, layouts, [len(group) for group in terms]),
        tuple(shape(each, F32) for each in dims),
        grid=(1,),
        in_specs=specs + [fixed(each.shape) for each in rest],
        out_specs=tuple(fixed(each) for each in dims),
    )(*sum(terms, []), *rest)


def embed_kernel(layer, tokens, embed, gain, w_qkv, table, inputs, low, both):
    part = pl.program_id(0)

    @pl.when(part == 0)
    def first():
        onehot = picks(tokens[...] == iota((embed.shape[0], tokens.shape[1]), 0))
        value = lax.dot_general(onehot, embed[...], (((0,), (0,)), ((), ())), preferred_element_type=F32)
        inputs[...] = value.astype(BF16)
        low[...] = normalize(value, gain_row(gain, layer))[0]

    joined = dot(low[...], w_qkv[0])

    @pl.when(part == 0)
    def keys():
        both[0] = rotate(joined, table[...]).astype(BF16)

    @pl.when(part == 1)
    def values():
        both[0] = joined.astype(BF16)


def embed_call(layer, tokens, embed, gain, w_qkv, table):
    count = tokens.shape[1]
    return call(
        functools.partial(embed_kernel, layer),
        (shape((count, D), BF16), shape((count, D), BF16), shape((2, count, D), BF16)),
        grid=(2,),
        in_specs=[
            fixed(tokens.shape),
            fixed(embed.shape),
            fixed(gain.shape),
            pl.BlockSpec((1, D, D), lambda part: (layer, 0, part + 1)),
            fixed(table.shape),
        ],
        out_specs=(
            fixed((count, D)),
            fixed((count, D)),
            pl.BlockSpec((1, count, D), lambda part: (part, 0, 0)),
        ),
    )(tokens, embed, gain, w_qkv, table)


def pool_kernel(layer, rows, members, me, first, edge, w_pool, gain, w_qkv, table, grouped, pooled, low, both):
    span = first.shape[0] // rows
    count = pooled.shape[0]
    short = count // rows
    late = jnp.where(me[0] == 0, 1, 0)
    total = jnp.zeros((count, D), F32)
    for third in range(3):
        pick = picks(iota((short, span), 1) == 3 * iota((short, span), 0) + third - 2)
        piece = jnp.concatenate(
            [dot(pick, first[row * span : (row + 1) * span, :]) for row in range(rows)], 0
        )
        if third < 2:
            place = iota((count, 2 * rows), 0) == (iota((count, 2 * rows), 1) // 2 + late) * short
            place = picks(place & (iota((count, 2 * rows), 1) % 2 == third))
            piece = piece + dot(place, edge[...])
        piece = piece.astype(BF16)
        grouped[:, third * D : (third + 1) * D] = piece
        total = total + dot(piece, w_pool[third * D : (third + 1) * D, :])
    pooled[...] = total
    low[...] = normalize(total, gain_row(gain, layer))[0]
    both[0] = rotate(dot(low[...], w_qkv[0, :, D : 2 * D]), table[...]).astype(BF16)
    both[1] = dot(low[...], w_qkv[0, :, 2 * D :]).astype(BF16)


def pool_call(layer, rows, members, me, first, edge, w_pool, gain, w_qkv, table):
    count = table.shape[0]
    return call(
        functools.partial(pool_kernel, layer, rows, members),
        (
            shape((count, 3 * D), BF16),
            shape((count, D), F32),
            shape((count, D), BF16),
            shape((2, count, D), BF16),
        ),
        grid=(1,),
        scalars=1,
        in_specs=[
            fixed(first.shape),
            fixed(edge.shape),
            fixed(w_pool.shape),
            fixed(gain.shape),
            fixed((1, D, 3 * D), (layer, 0, 0)),
            fixed(table.shape),
        ],
        out_specs=(fixed((count, 3 * D)), fixed((count, D)), fixed((count, D)), fixed((2, count, D))),
    )(me, first, edge, w_pool, gain, w_qkv, table)


GROUP = 256
HEADS = GROUP // DH


def fill_keys(rows, members, own, others, keys, values):
    span = own.shape[1] // rows
    for row in range(rows):
        for by, source in enumerate([own, *others]):
            start = (row * members + by) * span
            keys[start : start + span, :] = source[0, row * span : (row + 1) * span, :]
            values[start : start + span, :] = source[1, row * span : (row + 1) * span, :]


def tiles_of(rows, members, span):
    step = min(rows, max(1, 256 // span))
    return [(first, min(rows, first + step)) for first in range(0, rows, step)]


def heads_at_once(rows, members, span):
    size = sum((last - first) * span * last * members * span * 4 for first, last in tiles_of(rows, members, span))
    return max(count for count in (1, 2, HEADS) if count == 1 or count * size <= 12 << 20)


def bias_shape(rows, members, span):
    first, last = tiles_of(rows, members, span)[0]
    return ((last - first) * span, (last - first) * members * span)


def turned_shape(rows, members, span):
    tiles = tiles_of(rows, members, span)
    return (len(tiles), GROUP, rows * span)


def fill_bias(member, members, span, bias):
    line, column = iota(bias.shape, 0), iota(bias.shape, 1)
    width = members * span
    by = column % width // span
    own = (by == 0) & (column % span <= line % span)
    same = own | ((by > 0) & ((member + by) % members < member))
    seen = (column // width < line // span) | ((column // width == line // span) & same)
    bias[...] = jnp.where(seen, 0.0, masked_score)


def stacked(block, masks):
    return jnp.concatenate([block * mask for mask in masks], 0)


def score(stack, keys, bias, start, end):
    scores = dot_nt(stack, keys[0:end, :])
    last = scores[:, start:] + jnp.concatenate([bias[...]] * (stack.shape[0] // bias.shape[0]), 0)
    return jnp.concatenate([scores[:, :start], last], 1) if start else last


def unstacked(stack, lanes, held):
    count = held.shape[0]
    for number, mine in enumerate(lanes):
        held = jnp.where(mine, stack[number * count : (number + 1) * count, :], held)
    return held


def attention_part(rows, members, queries, own, *refs):
    others = refs[: members - 1]
    mixed, logsum, keys, values, bias, total = refs[members - 1 :]
    span = queries.shape[0] // rows
    width = members * span
    tiles = tiles_of(rows, members, span)
    fill_keys(rows, members, own, others, keys, values)
    logsum[...] = jnp.zeros_like(logsum)

    at_once = heads_at_once(rows, members, span)

    def some_heads(turn, unused):
        heads = [turn * at_once + number for number in range(at_once)]
        lanes = [iota((1, GROUP), 1) // DH == head for head in heads]
        masks = [picks(mine) for mine in lanes]
        blocks = [slice(first * span, last * span) for first, last in tiles]
        scores = [
            score(stacked(queries[block, :], masks), keys, bias, first * width, last * width)
            for block, (first, last) in zip(blocks, tiles)
        ]
        highest = [jnp.max(value, -1, keepdims=True) for value in scores]
        expon = [jnp.exp(value - most) for value, most in zip(scores, highest)]
        totals = [jnp.sum(value, -1, keepdims=True) for value in expon]
        outs = [
            dot(value.astype(BF16), values[0 : last * width, :]) * (1.0 / whole)
            for value, whole, (first, last) in zip(expon, totals, tiles)
        ]
        for block, out, most, whole in zip(blocks, outs, highest, totals):
            total[block, :] = unstacked(out, lanes, total[block, :])
            logs = jnp.broadcast_to(most + jnp.log(whole), (out.shape[0], 128))
            places = [iota((1, 128), 1) == head for head in heads]
            logsum[0, block, :] = unstacked(logs, places, logsum[0, block, :])
        return unused

    lax.fori_loop(0, HEADS // at_once, some_heads, 0)
    mixed[...] = total[...].astype(BF16)


def lane_group(ndim, block, base=0):
    return pl.BlockSpec(block, lambda group, *unused: (0,) * (ndim - 1) + (group + base,))


def lane_part(ref, group):
    lanes = pl.ds(group * GROUP, GROUP)
    return ref.at[:, lanes] if len(ref.shape) == 2 else ref.at[:, :, lanes]


def attention_scratch(rows, members, count):
    span = count // rows
    return [
        pltpu.VMEM((members * count, GROUP), BF16),
        pltpu.VMEM((members * count, GROUP), BF16),
        pltpu.VMEM(bias_shape(rows, members, span), F32),
        pltpu.VMEM((count, GROUP), F32),
    ]


def attention_back_scratch(rows, members, count):
    span = count // rows
    return [
        pltpu.VMEM(turned_shape(rows, members, span), BF16),
        pltpu.VMEM(turned_shape(rows, members, span), BF16),
        pltpu.VMEM((GROUP, members * count), F32),
        pltpu.VMEM((GROUP, members * count), F32),
    ]


def attention_back_kernel(rows, members, me, queries, own, *refs):
    fill_bias(me[0], members, queries.shape[0] // rows, refs[-6])
    attention_back_part(rows, members, queries, own, *refs)


def attention_back_part(rows, members, queries, own, *refs):
    others = refs[: members - 1]
    mixed, logsum, grad_mixed, grad_queries, *rest = refs[members - 1 :]
    pieces = rest[:members]
    keys, values, bias, total, turned, turned_grad, grad_keys, grad_values = rest[members:]
    span = queries.shape[0] // rows
    width = members * span
    fill_keys(rows, members, own, others, keys, values)
    tiles = tiles_of(rows, members, span)
    for tile, (first, last) in enumerate(tiles):
        lines = (rows - first) * span
        turned[tile, :, 0:lines] = queries[first * span :, :].T
        turned_grad[tile, :, 0:lines] = grad_mixed[first * span :, :].T

    at_once = heads_at_once(rows, members, span)

    def some_heads(turn, unused):
        heads = [turn * at_once + number for number in range(at_once)]
        lanes = [iota((1, GROUP), 1) // DH == head for head in heads]
        masks = [picks(mine) for mine in lanes]
        blocks = [slice(first * span, last * span) for first, last in tiles]
        grads = [stacked(grad_mixed[block, :], masks) for block in blocks]
        scores = [
            score(stacked(queries[block, :], masks), keys, bias, first * width, last * width)
            for block, (first, last) in zip(blocks, tiles)
        ]
        grad_probs = [dot_nt(grad, values[0 : last * width, :]) for grad, (first, last) in zip(grads, tiles)]
        sums, deltas = [], []
        for block, grad in zip(blocks, grads):
            logs = logsum[0, block, :]
            sums.append(
                jnp.concatenate(
                    [
                        jnp.sum(jnp.where(iota(logs.shape, 1) == head, logs, 0.0), -1, keepdims=True)
                        for head in heads
                    ],
                    0,
                )
            )
            product = grad.astype(F32) * jnp.concatenate([mixed[block, :].astype(F32)] * at_once, 0)
            deltas.append(jnp.sum(product, -1, keepdims=True))
        probs = [jnp.exp(value - whole) for value, whole in zip(scores, sums)]
        grad_scores = [
            (prob * (grad - delta)).astype(BF16) for prob, grad, delta in zip(probs, grad_probs, deltas)
        ]
        for block, grad, (first, last) in zip(blocks, grad_scores, tiles):
            total[block, :] = unstacked(dot(grad, keys[0 : last * width, :]), lanes, total[block, :])
        probs = [prob.astype(BF16) for prob in probs]
        for number in range(at_once):
            mine = pl.ds(pl.multiple_of((turn * at_once + number) * DH, DH), DH)
            for tile, (first, last) in enumerate(tiles):
                columns = slice(first * width, last * width)
                lines = (rows - first) * span
                for source, made, into in (
                    (turned, grad_scores, grad_keys),
                    (turned_grad, probs, grad_values),
                ):
                    later = []
                    for each in made[tile:]:
                        size = each.shape[0] // at_once
                        later.append(each[number * size : (number + 1) * size, columns])
                    into[mine, columns] = dot(source[tile, mine, 0:lines], jnp.concatenate(later, 0))
        return unused

    lax.fori_loop(0, HEADS // at_once, some_heads, 0)
    grad_queries[...] = total[...].astype(BF16)
    for number, source in enumerate((grad_keys, grad_values)):
        made = source[...].astype(BF16).T
        for row in range(rows):
            for by, piece in enumerate(pieces):
                start = (row * members + by) * span
                piece[number, row * span : (row + 1) * span, :] = made[start : start + span, :]


def attention_back_call(rows, members, me, queries, own, others, mixed, logsum, grad_mixed, groups):
    count = queries.shape[0]
    base, wide = groups[0], len(groups) * GROUP
    made = call(
        functools.partial(attention_back_kernel, rows, members),
        (shape((count, wide), BF16),) + (shape((2, count, wide), BF16),) * members,
        grid=(len(groups),),
        scalars=1,
        in_specs=[lane_group(2, (count, GROUP), base)]
        + [lane_group(3, (2, count, GROUP), base)] * members
        + [
            lane_group(2, (count, GROUP), base),
            pl.BlockSpec((1, count, 128), lambda group, *unused: (group + base, 0, 0)),
            lane_group(2, (count, GROUP), base),
        ],
        out_specs=(lane_group(2, (count, GROUP)),) + (lane_group(3, (2, count, GROUP)),) * members,
        scratch=attention_scratch(rows, members, count) + attention_back_scratch(rows, members, count),
    )(me, queries, own, *others, mixed, logsum, grad_mixed)
    return (made[0], made[1:])


CHUNK = 512


class Moves:
    def __init__(self, sems, first=0):
        self.sems, self.taken, self.open = sems, first, []

    def start(self, source, target):
        copy = pltpu.make_async_copy(source, target, self.sems.at[self.taken])
        copy.start()
        self.open.append(copy)
        self.taken += 1
        return copy

    def end(self):
        for copy in self.open:
            copy.wait()
        self.open = []


class Weights:
    def __init__(self, sems, layer, sources, held):
        self.sems, self.layer, self.sources, self.held = sems, layer, sources, held
        self.chunks = held[1].shape[1] // CHUNK
        self.copies = 1 + 2 * self.chunks

    def pair(self, name, part=0):
        (w_out, w_up, w_down), (out, up, down) = self.sources, self.held
        if name == "out":
            return w_out.at[self.layer], out
        lines = pl.ds(pl.multiple_of(part * CHUNK, CHUNK), CHUNK)
        if name == "up":
            return w_up.at[self.layer, :, lines], up.at[:, lines]
        return w_down.at[self.layer, lines, :], down.at[lines, :]

    def copy(self, name, part=0):
        place = {"out": 0, "up": 1, "down": 2}[name] + 2 * part
        return pltpu.make_async_copy(*self.pair(name, part), self.sems.at[place])

    def start(self):
        self.copy("out").start()
        for part in range(self.chunks):
            self.copy("up", part).start()
            self.copy("down", part).start()

    def wait(self, name, part=0):
        self.copy(name, part).wait()

    def get(self, name, part=0):
        return self.pair(name, part)[1][...]


def weight_scratch(units):
    return [pltpu.VMEM((D, D), BF16), pltpu.VMEM((D, units), BF16), pltpu.VMEM((units, D), BF16)]


def edge_rows(made, rows):
    count = made.shape[0]
    span = count // rows
    line = iota((2 * rows, count), 0)
    pick = picks(iota((2 * rows, count), 1) == (line // 2 + 1) * span - 2 + line % 2)
    return dot(pick, made).astype(BF16)


def make_queries(low, w_qkv, table):
    joined = dot(low[...], w_qkv[0])
    return (rotate(joined, table[...]) * DH ** (-0.5)).astype(BF16)


def attend(rows, members, me, queries, own, others, mixed, logsum, scratch):
    fill_bias(me[0], members, queries.shape[0] // rows, scratch[2])
    for group in range(D // GROUP):
        sources = [lane_part(each, group) for each in (queries, own, *others, mixed)]
        attention_part(rows, members, *sources, logsum.at[pl.ds(group, 1)], *scratch)


def forward_kernel(layer, rows, members, me, inputs, low, own, *refs):
    others = refs[: members - 1]
    (
        table, gain, w_qkv, w_out, w_up, w_down,
        output, edges, queries_out, mixed_out, logsum_out, middle_out, hidden_out,
        queries, mixed, logsum, middle, hidden, low_now, sum_now, *scratch,
    ) = refs[members - 1 :]
    held, attention, sems = scratch[:3], scratch[3:7], scratch[7]
    weights = Weights(sems, layer, (w_out, w_up, w_down), held)
    moves = Moves(sems, weights.copies)
    weights.start()
    queries[...] = make_queries(low, w_qkv, table)
    moves.start(queries, queries_out)
    attend(rows, members, me, queries, own, others, mixed, logsum, attention)
    moves.start(mixed, mixed_out)
    moves.start(logsum, logsum_out)
    weights.wait("out")
    total = inputs[...].astype(F32) + dot(mixed[...], weights.get("out"))
    middle[...] = total
    moves.start(middle, middle_out)
    normed = normalize(total, gain_row(gain, layer))[0]
    low_now[...] = normed
    sum_now[...] = total

    def one_part(part, unused):
        weights.wait("up", part)
        made = dot(low_now[...], weights.get("up", part))
        lanes = pl.ds(pl.multiple_of(part * CHUNK, CHUNK), CHUNK)
        hidden[:, lanes] = made.astype(BF16)
        weights.wait("down", part)
        sum_now[...] += dot(gelu_both(made)[0].astype(BF16), weights.get("down", part))
        return unused

    lax.fori_loop(0, weights.chunks, one_part, 0)
    moves.start(hidden, hidden_out)
    made = sum_now[...].astype(BF16)
    output[...] = made
    edges[...] = edge_rows(made, rows)
    moves.end()


def forward_call(layer, rows, members, me, inputs, low, own, others, table, gain, w_qkv, w_out, w_up, w_down):
    count = inputs.shape[0]
    units = w_up.shape[2]
    handed = [
        ((count, D), BF16), ((count, D), BF16), ((D // GROUP, count, 128), F32),
        ((count, D), F32), ((count, units), BF16),
    ]
    return call(
        functools.partial(forward_kernel, layer, rows, members),
        (shape((count, D), BF16), shape((2 * rows, D), BF16)) + tuple(shape(*each) for each in handed),
        grid=(1,),
        scalars=1,
        in_specs=[fixed((count, D))] * 2
        + [fixed((2, count, D))] * members
        + [fixed(table.shape), fixed(gain.shape), fixed((1, D, D), (layer, 0, 0))]
        + [ANYWHERE] * 3,
        out_specs=(fixed((count, D)), fixed((2 * rows, D))) + (ANYWHERE,) * len(handed),
        scratch=[pltpu.VMEM(*each) for each in handed]
        + [pltpu.VMEM((count, D), BF16), pltpu.VMEM((count, D), F32)]
        + weight_scratch(units)
        + attention_scratch(rows, members, count)
        + [pltpu.SemaphoreType.DMA((6 + 2 * (units // CHUNK),))],
    )(me, inputs, low, own, *others, table, gain, w_qkv, w_out, w_up, w_down)


def ffn_blocks(batches, seqs, units):
    return ((D // batches, units // seqs), (D // seqs, units // batches), (D // seqs, D // batches))


def ffn_back(layer, packs, me, middle, mixed, parts, weights, gain, packed, outs, moves, scratch, unroll):
    grad, turned_low, turned_grad, total = scratch
    row = gain_row(gain, layer)
    low, normed, inverse = normalize(middle[...], row)
    turned_low[...] = low.T
    middle[...] = normed
    turned_grad[...] = grad[...].T
    total[...] = jnp.zeros_like(total)

    def one_part(part, unused):
        active, slope = parts(part)
        grad_hidden = (dot_nt(grad[...], weights.get("down", part)) * slope).astype(BF16)
        made = dot(turned_grad[...], active.astype(BF16)).astype(BF16)
        deep, wide = packs.blocks[1]
        for column in range(CHUNK // wide):
            for seq in range(packs.seqs):
                block = made[seq * deep : (seq + 1) * deep, column * wide : (column + 1) * wide]
                packs.put_block(packed, me, 1, part * (CHUNK // wide) + column, seq, block)
        made = dot(turned_low[...], grad_hidden).astype(BF16)
        deep, wide = packs.blocks[0]
        for column in range(CHUNK // wide):
            for batch in range(packs.batches):
                block = made[batch * deep : (batch + 1) * deep, column * wide : (column + 1) * wide]
                packs.put_block(packed, me, 0, batch, part * (CHUNK // wide) + column, block)
        total[...] += dot_nt(grad_hidden, weights.get("up", part))
        return unused

    lax.fori_loop(0, weights.chunks, one_part, 0, unroll=unroll)
    packs.send(packed, outs, moves, 0, packs.starts[2])
    back, gain_sum = normalize_back(total[...], middle[...], inverse, row)
    grad_middle = grad[...].astype(F32) + back
    branch = grad_middle.astype(BF16)
    packs.put_all(packed, me, 2, dot(branch.T, mixed[...]).astype(BF16), True)
    packs.send(packed, outs, moves, packs.starts[2], packs.rows)
    return grad_middle, dot_nt(branch, weights.get("out")).astype(BF16), gain_sum


def ffn_back_scratch(count):
    return [
        pltpu.VMEM((count, D), BF16),
        pltpu.VMEM((D, count), BF16),
        pltpu.VMEM((D, count), BF16),
        pltpu.VMEM((count, D), F32),
    ]


def ffn_back_kernel(
    layer, rows, members, packs, me, grad_ref, carried, middle_ref, mixed_ref, hidden_ref, gain,
    w_out, w_up, w_down, *refs,
):
    outs = refs[: len(packs.shapes())]
    (
        grad_gain, grad_middle, grad_mixed,
        middle, mixed, hidden, out, up, down, grad, turned_low, turned_grad, total, packed, sems,
    ) = refs[len(outs) :]
    weights = Weights(sems, layer, (w_out, w_up, w_down), (out, up, down))
    moves = Moves(sems, weights.copies + weights.chunks)
    came = moves.start(middle_ref, middle)

    def hidden_copy(part):
        lanes = pl.ds(pl.multiple_of(part * CHUNK, CHUNK), CHUNK)
        return pltpu.make_async_copy(
            hidden_ref.at[:, lanes], hidden.at[:, lanes], sems.at[weights.copies + part]
        )

    for part in range(weights.chunks):
        weights.copy("down", part).start()
        hidden_copy(part).start()
        weights.copy("up", part).start()
    weights.copy("out").start()
    late = moves.start(mixed_ref, mixed)
    moves.open = []
    value = grad_ref[...]
    count = value.shape[0]
    span = count // rows
    early = jnp.where(me[0] == members - 1, 1, 0)
    line = iota((count, 2 * rows), 1)
    place = iota((count, 2 * rows), 0) == (line // 2 + 1 - early) * span - 2 + line % 2
    grad[...] = (value.astype(F32) + dot(picks(place), carried[...])).astype(BF16)

    def parts(part):
        hidden_copy(part).wait()
        weights.wait("down", part)
        weights.wait("up", part)
        lanes = pl.ds(pl.multiple_of(part * CHUNK, CHUNK), CHUNK)
        return gelu_both(hidden[:, lanes].astype(F32))

    came.wait()
    late.wait()
    weights.wait("out")
    made = ffn_back(
        layer, packs, me, middle, mixed, parts, weights, gain, packed, outs, moves,
        (grad, turned_low, turned_grad, total), 1,
    )
    grad_middle[...], grad_mixed[...], grad_gain[...] = made
    moves.end()


def ffn_back_call(
    layer, rows, members, batches, seqs, order, me, grad, carried, middle, mixed, hidden, gain, w_out, w_up, w_down
):
    count = grad.shape[0]
    units = w_up.shape[2]
    packs = Packs(batches, seqs, order, ffn_blocks(batches, seqs, units))
    return call(
        functools.partial(ffn_back_kernel, layer, rows, members, packs),
        packs.shapes() + (shape((1, D), F32), shape((count, D), F32), shape((count, D), BF16)),
        grid=(1,),
        scalars=1,
        in_specs=[fixed((count, D)), fixed((2 * rows, D)), ANYWHERE, ANYWHERE, ANYWHERE, fixed(gain.shape)]
        + [ANYWHERE] * 3,
        out_specs=packs.specs() + (fixed((1, D)), fixed((count, D)), fixed((count, D))),
        scratch=[pltpu.VMEM((count, D), F32), pltpu.VMEM((count, D), BF16), pltpu.VMEM((count, units), BF16)]
        + weight_scratch(units)
        + ffn_back_scratch(count)
        + [packs.scratch()[0], pltpu.SemaphoreType.DMA((3 + 3 * (units // CHUNK) + 2 * packs.slots,))],
    )(me, grad, carried, middle, mixed, hidden, gain, w_out, w_up, w_down)


def middle_kernel(layer, rows, members, packs, me, inputs, low, own, *refs):
    others = refs[: members - 1]
    (
        grad_ref, table, gain, w_qkv, w_out, w_up, w_down,
        output, *refs,
    ) = refs[members - 1 :]
    outs = refs[: len(packs.shapes())]
    grad_gain, grad_middle, grad_queries, *refs = refs[len(outs) :]
    pieces = refs[:members]
    queries, mixed, logsum, middle, active, slope, grad_mixed, packed, *scratch = refs[members:]
    held, attention, back, ffn, sems = scratch[:3], scratch[3:7], scratch[7:11], scratch[11:15], scratch[15]
    parts = range(w_up.shape[2] // CHUNK)
    weights = Weights(sems, layer, (w_out, w_up, w_down), held)
    moves = Moves(sems, weights.copies)
    weights.start()
    queries[...] = make_queries(low, w_qkv, table)
    attend(rows, members, me, queries, own, others, mixed, logsum, attention)
    weights.wait("out")
    total = inputs[...].astype(F32) + dot(mixed[...], weights.get("out"))
    middle[...] = total
    normed = normalize(total, gain_row(gain, layer))[0]
    for part in parts:
        lanes = pl.ds(part * CHUNK, CHUNK)
        weights.wait("up", part)
        one, other = gelu_both(dot(normed, weights.get("up", part)))
        active[:, lanes], slope[:, lanes] = one.astype(BF16), other
        weights.wait("down", part)
        total = total + dot(active[:, lanes], weights.get("down", part))
    output[...] = total.astype(BF16)
    ffn[0][...] = grad_ref[...]

    def part_of(part):
        lanes = pl.ds(pl.multiple_of(part * CHUNK, CHUNK), CHUNK)
        return active[:, lanes], slope[:, lanes]

    made = ffn_back(
        layer, packs, me, middle, mixed, part_of, weights, gain, packed, outs, moves, ffn, True
    )
    grad_middle[...], grad_mixed[...], grad_gain[...] = made
    for group in range(D // GROUP):
        sources = [lane_part(each, group) for each in (queries, own, *others, mixed)]
        targets = [lane_part(each, group) for each in (grad_mixed, grad_queries, *pieces)]
        attention_back_part(
            rows, members, *sources, logsum.at[pl.ds(group, 1)], *targets, *attention, *back
        )
    moves.end()


def middle_call(
    layer, rows, members, batches, seqs, order, me, inputs, low, own, others, grad, table, gain,
    w_qkv, w_out, w_up, w_down,
):
    count = inputs.shape[0]
    units = w_up.shape[2]
    packs = Packs(batches, seqs, order, ffn_blocks(batches, seqs, units))
    made = call(
        functools.partial(middle_kernel, layer, rows, members, packs),
        (shape((count, D), BF16),)
        + packs.shapes()
        + (shape((1, D), F32), shape((count, D), F32), shape((count, D), BF16))
        + (shape((2, count, D), BF16),) * members,
        grid=(1,),
        scalars=1,
        in_specs=[fixed((count, D))] * 2
        + [fixed((2, count, D))] * members
        + [fixed((count, D)), fixed(table.shape), fixed(gain.shape)]
        + [fixed((1, D, D), (layer, 0, 0))]
        + [ANYWHERE] * 3,
        out_specs=(fixed((count, D)),)
        + packs.specs()
        + (fixed((1, D)), fixed((count, D)), fixed((count, D)))
        + (fixed((2, count, D)),) * members,
        scratch=[
            pltpu.VMEM((count, D), BF16),
            pltpu.VMEM((count, D), BF16),
            pltpu.VMEM((D // GROUP, count, 128), F32),
            pltpu.VMEM((count, D), F32),
            pltpu.VMEM((count, units), BF16),
            pltpu.VMEM((count, units), F32),
            pltpu.VMEM((count, D), BF16),
            packs.scratch()[0],
        ]
        + weight_scratch(units)
        + attention_scratch(rows, members, count)
        + attention_back_scratch(rows, members, count)
        + ffn_back_scratch(count)
        + [pltpu.SemaphoreType.DMA((1 + 2 * (units // CHUNK) + 2 * packs.slots,))],
    )(me, inputs, low, own, *others, grad, table, gain, w_qkv, w_out, w_up, w_down)
    cut = 4 + len(packs.shapes())
    return (*made[:cut], made[cut:])


def joined_blocks(batches, seqs, other):
    return ((3 * D // seqs, D // batches), other)


def joined_back(layer, packs, me, inputs, grad_queries, sources, rest):
    grad_middle, came, table, gain, w_qkv, grad_gain, turned, packed, outs, moves = rest
    row = gain_row(gain, layer)
    low, normed, inverse = normalize(inputs[...].astype(F32), row)
    joined = []
    for part in range(3):
        if part == 0:
            value = [lanes[...].astype(F32) * DH ** (-0.5) for lanes in grad_queries]
        else:
            value = [sum([source[part - 1].astype(F32) for source in lanes]) for lanes in sources]
        value = jnp.concatenate(value, 1)
        if part < 2:
            value = rotate(value, table[...], True)
        joined.append(value.astype(BF16))
        turned[part * D : (part + 1) * D, :] = joined[part].T
    deep, wide = packs.blocks[0]

    def one_block(seq, unused):
        made = dot(turned[pl.ds(pl.multiple_of(seq * deep, deep), deep), :], low).astype(BF16)
        for batch in range(packs.batches):
            packs.put_block(packed, me, 0, batch, seq, made[:, batch * wide : (batch + 1) * wide])
        return unused

    lax.fori_loop(0, packs.seqs, one_block, 0)
    packs.send(packed, outs, moves, 0, packs.starts[1])
    back = 0.0
    for copy in came:
        copy.wait()
    for part in range(3):
        back = back + dot_nt(joined[part], w_qkv[:, part * D : (part + 1) * D])
    value, gain_sum = normalize_back(back, normed, inverse, row)
    grad_gain[...] = gain_sum
    return grad_middle[...] + value


def split_sources(refs, members, cuts):
    rest = refs[cuts:]
    sources = [rest[cut * members : (cut + 1) * members] for cut in range(cuts)]
    return (refs[:cuts], sources, rest[cuts * members :])


def source_specs(count, members, cuts):
    wide = D // cuts
    return [fixed((count, wide))] * cuts + [fixed((2, count, wide))] * (members * cuts)


def embed_back_kernel(layer, members, cuts, packs, me, inputs, *refs):
    grad_queries, sources, refs = split_sources(refs, members, cuts)
    (
        middle_in, table, gain, w_in, tokens, gain_attn_1, gain_ffn_0, gain_ffn_1,
        stays, leaves, sums, grad_inputs, gain_attn_0, turned, grad_middle, w_qkv, packed, sems,
    ) = refs
    moves = Moves(sems)
    came = [moves.start(w_in.at[layer], w_qkv), moves.start(middle_in, grad_middle)]
    moves.open = []
    value = joined_back(
        layer, packs, me, inputs, grad_queries, sources,
        (grad_middle, came, table, gain, w_qkv, gain_attn_0, turned, packed, (stays, leaves), moves),
    ).astype(BF16)
    grad_inputs[...] = value
    onehot = picks(tokens[...] == iota((VOCAB, tokens.shape[1]), 0))
    packs.put_all(packed, me, 1, dot(onehot, value).astype(BF16), False)
    packs.send(packed, (stays, leaves), moves, packs.starts[1], packs.rows)
    tiles = D // 128
    for number, ref in enumerate((gain_attn_0, gain_attn_1, gain_ffn_0, gain_ffn_1)):
        for tile in range(tiles):
            place = number * tiles + tile
            sums[place : place + 1, :] = ref[:, tile * 128 : (tile + 1) * 128]
    at, extra = packs.slots * packs.rows, 8 * tiles
    for number, piece in enumerate(in_two(sums[...])):
        packed[at + number * 4 * tiles : at + (number + 1) * 4 * tiles, :] = piece
    moves.start(packed.at[pl.ds(at, extra)], leaves.at[pl.ds(at // 2, extra)])
    moves.end()


def embed_back_call(
    layer, batches, seqs, order, me, inputs, grad_queries, sources, grad_middle, table, gain, w_qkv,
    tokens, *gains,
):
    count = inputs.shape[0]
    cuts, members = len(sources), len(sources[0])
    packs = Packs(batches, seqs, order, joined_blocks(batches, seqs, (VOCAB // batches, D // seqs)))
    summed = 4 * D // 128
    return call(
        functools.partial(embed_back_kernel, layer, members, cuts, packs),
        packs.shapes(2 * summed) + (shape((summed, 128), F32), shape((count, D), BF16)),
        grid=(1,),
        scalars=1,
        in_specs=[fixed((count, D))]
        + source_specs(count, members, cuts)
        + [ANYWHERE, fixed(table.shape), fixed(gain.shape), ANYWHERE, fixed(tokens.shape)]
        + [fixed((1, D))] * 3,
        out_specs=packs.specs() + (fixed((summed, 128)), fixed((count, D))),
        scratch=[
            pltpu.VMEM((1, D), F32),
            pltpu.VMEM((3 * D, count), BF16),
            pltpu.VMEM((count, D), F32),
            pltpu.VMEM((D, 3 * D), BF16),
            packs.scratch(2 * summed)[0],
            pltpu.SemaphoreType.DMA((3 + 2 * packs.slots,)),
        ],
    )(me, inputs, *grad_queries, *sum(sources, []), grad_middle, table, gain, w_qkv, tokens, *gains)


def pool_back_kernel(layer, rows, members, cuts, packs, me, inputs, *refs):
    grad_queries, sources, refs = split_sources(refs, members, cuts)
    middle_in, table, gain, w_in, grouped_in, pool_in, *refs = refs
    outs = refs[: len(packs.shapes())]
    grad_gain, grad_first, edges, turned, grad_middle, w_qkv, grouped, w_pool, packed, sems = refs[len(outs) :]
    moves = Moves(sems)
    came = [moves.start(w_in.at[layer], w_qkv), moves.start(middle_in, grad_middle)]
    late = [moves.start(grouped_in, grouped), moves.start(pool_in, w_pool)]
    moves.open = []
    value = joined_back(
        layer, packs, me, inputs, grad_queries, sources,
        (grad_middle, came, table, gain, w_qkv, grad_gain, turned, packed, outs, moves),
    ).astype(BF16)
    for copy in late:
        copy.wait()
    packs.put_all(packed, me, 1, dot(value.T, grouped[...]).astype(BF16), True)
    packs.send(packed, outs, moves, packs.starts[1], packs.rows)
    count = value.shape[0]
    short = count // rows
    span = grad_first.shape[0] // rows
    parts = [dot_nt(value, w_pool[third * D : (third + 1) * D, :]).astype(BF16) for third in range(3)]
    line = iota((2 * rows, count), 0)
    found = 0.0
    for third in range(2):
        pick = (iota((2 * rows, count), 1) == (line // 2) * short) & (line % 2 == third)
        found = found + dot(picks(pick), parts[third])
    edges[...] = found.astype(BF16)
    for row in range(rows):
        total = 0.0
        for third in range(3):
            pick = picks(iota((span, short), 0) == 3 * iota((span, short), 1) + third - 2)
            total = total + dot(pick, parts[third][row * short : (row + 1) * short, :])
        grad_first[row * span : (row + 1) * span, :] = total.astype(BF16)
    moves.end()


def pool_back_call(
    layer, rows, span, batches, seqs, order, me, inputs, grad_queries, sources, grad_middle, table,
    gain, w_qkv, grouped, w_pool,
):
    count = inputs.shape[0]
    cuts, members = len(sources), len(sources[0])
    packs = Packs(batches, seqs, order, joined_blocks(batches, seqs, (D // seqs, 3 * D // batches)))
    return call(
        functools.partial(pool_back_kernel, layer, rows, members, cuts, packs),
        packs.shapes() + (shape((1, D), F32), shape((rows * span, D), BF16), shape((2 * rows, D), BF16)),
        grid=(1,),
        scalars=1,
        in_specs=[fixed((count, D))]
        + source_specs(count, members, cuts)
        + [ANYWHERE, fixed(table.shape), fixed(gain.shape), ANYWHERE, ANYWHERE, ANYWHERE],
        out_specs=packs.specs() + (fixed((1, D)), fixed((rows * span, D)), fixed((2 * rows, D))),
        scratch=[
            pltpu.VMEM((3 * D, count), BF16),
            pltpu.VMEM((count, D), F32),
            pltpu.VMEM((D, 3 * D), BF16),
            pltpu.VMEM(grouped.shape, BF16),
            pltpu.VMEM(w_pool.shape, BF16),
            packs.scratch()[0],
            pltpu.SemaphoreType.DMA((4 + 2 * packs.slots,)),
        ],
    )(me, inputs, *grad_queries, *sum(sources, []), grad_middle, table, gain, w_qkv, grouped, w_pool)


def angles(positions):
    half_size = DH // 2
    freqs = 10000.0 ** (-jnp.arange(half_size).astype(jnp.float32) / half_size)
    phase = positions.astype(jnp.float32)[:, None] * jnp.tile(freqs, 4)[None, :]
    lane = jnp.arange(4 * half_size)[None, :]
    sine = jnp.sin(phase) * jnp.where(lane < 3 * half_size, -1.0, 1.0)
    return jnp.where(lane < 2 * half_size, jnp.cos(phase), sine)


class Plan:
    def __init__(self, rows):
        self.S = lax.axis_size("seq")
        self.B = lax.axis_size("batch")
        self.R = rows
        self.P = self.S // rows
        self.s = lax.axis_index("seq")
        self.b = lax.axis_index("batch")
        self.z = self.s // self.P
        self.h = self.s % self.P // 2 * 2 + self.b % 2

    def device(self, pair, z, y, core):
        return (z * self.P + y) * self.B + 2 * pair + core

    def exchange(self, value):
        moves = []
        for apart in range(self.R):
            perm = []
            for pair in range(self.B // 2):
                for z in range(self.R):
                    for y in range(self.P):
                        for core in range(2):
                            other = self.device(pair, z ^ apart, y // 2 * 2 + core, y % 2)
                            perm.append((self.device(pair, z, y, core), other))
            piece = lax.dynamic_index_in_dim(value, self.z ^ apart, 0, keepdims=False)
            moves.append(lax.ppermute(piece, AXES, perm))
        got, bit = moves, 1
        while bit < self.R:
            flip = (self.z // bit) % 2 == 1
            got = [jnp.where(flip, got[n ^ bit], got[n]) for n in range(self.R)]
            bit *= 2
        return (jnp.stack(got), moves)

    def shift(self, value, by):
        perm = []
        for pair in range(self.B // 2):
            for z in range(self.R):
                for batch in range(2):
                    for member in range(self.P):
                        to = (member + by) % self.P
                        perm.append((
                            self.device(pair, z, member // 2 * 2 + batch, member % 2),
                            self.device(pair, z, to // 2 * 2 + batch, to % 2),
                        ))
        return lax.ppermute(value, AXES, perm)

    def others(self, value):
        return [self.shift(value, by) for by in range(1, self.P)]

    def swap(self, value, axis, bit):
        count = lax.axis_size(axis)
        return lax.ppermute(value, axis, [(n, n ^ bit) for n in range(count)])

    def bits(self, axis):
        count = lax.axis_size(axis)
        return [1 << n for n in range(count.bit_length() - 1)]

    def order(self, *axes):
        return [(axis, bit) for axis in axes for bit in self.bits(axis)]


def behind(value, *others):
    return lax.optimization_barrier((value, others))[0]


class Halving:
    def __init__(self, plan, order, stays, leaves=None):
        self.plan, self.order = plan, order
        self.terms, self.count, self.leaves = [(stays, 0, stays.shape[0])], stays.shape[0], []
        if leaves is not None:
            self.leaves = [(leaves, 0, leaves.shape[0])]

    def sum(self, start, stop):
        made = 0.0
        for array, first, last in self.terms:
            if first <= start and stop <= last:
                made = made + array[start - first : stop - first].astype(F32)
        return made

    def add(self, cuts=1):
        self.count //= 2
        size = self.count // cuts
        self.leaves = []
        for cut in reversed(range(cuts)):
            made = self.sum(self.count + cut * size, self.count + (cut + 1) * size).astype(BF16)
            self.leaves.append((made, cut * size, (cut + 1) * size))
        return [made for made, start, stop in self.leaves]

    def send(self):
        (axis, bit), self.order = self.order[0], self.order[1:]
        got = [self.plan.swap(made, axis, bit) for made, start, stop in self.leaves]
        self.terms += [(each, start, stop) for each, (made, start, stop) in zip(got, self.leaves)]
        return got

    def wait(self, *others):
        array, start, stop = self.terms[0]
        self.terms[0] = (behind(array, *others), start, stop)

    def rest(self):
        return [array for array, start, stop in self.terms if start == 0]


def body(
    tokens, loss_mask, cotangent, embed, gain_attn, w_qkv, w_out, gain_ffn, w_up, w_down, w_pool
):
    plan = Plan(tokens.shape[0])
    rows, span = tokens.shape
    short = loss_mask.shape[1]
    members, batches, seqs = plan.P, plan.B, plan.S
    units = w_up.shape[2]
    groups = D // GROUP
    every, along = plan.order("batch", "seq"), plan.order("seq")
    crossed = every[:1] + along[:1] + every[1:-len(along)] + along[1:]
    me = jnp.stack([plan.h, plan.b, plan.s]).astype(jnp.int32)

    token_line = plan.exchange(tokens)[0].reshape(1, rows * span)

    def places(length):
        block = jnp.arange(rows, dtype=jnp.int32)[:, None] * members + plan.h
        return (block * length + jnp.arange(length, dtype=jnp.int32)[None]).reshape(-1)

    first_angles, second_angles = angles(places(span)), angles(places(short))

    ffn_layout = ffn_blocks(batches, seqs, units)
    pool_layout = joined_blocks(batches, seqs, (D // seqs, 3 * D // batches))
    embed_layout = joined_blocks(batches, seqs, (VOCAB // batches, D // seqs))

    def scatter(value, axis):
        return lax.psum_scatter(value, axis, scatter_dimension=0, tiled=True)

    inputs, low, own_0 = embed_call(0, token_line, embed, gain_attn, w_qkv, first_angles)
    others_0 = plan.others(own_0)
    start_grad, start_moves = plan.exchange(cotangent * loss_mask.astype(BF16)[..., None])
    first_low, edges, queries_0, mixed_0, logsum_0, middle_0, hidden_0 = forward_call(
        0, rows, members, me, inputs, low, own_0, others_0, first_angles, gain_ffn, w_qkv, w_out, w_up, w_down
    )
    edge = plan.shift(edges, 1)

    grouped, pooled, low, own_1 = pool_call(
        1, rows, members, me, behind(first_low, *start_moves), edge, w_pool, gain_attn, w_qkv, second_angles
    )
    others_1 = plan.others(own_1)
    second_low, packed, gain_ffn_1, grad_middle, grad_queries, pieces = middle_call(
        1, rows, members, batches, seqs, along, me, pooled, low, own_1, others_1, start_grad.reshape(-1, D),
        second_angles, gain_ffn, w_qkv, w_out, w_up, w_down,
    )
    ffn_1 = Halving(plan, along, scatter(packed, "batch"))
    others = [plan.shift(pieces[by], -by) for by in range(1, members)]
    outs, out_moves = plan.exchange(
        jnp.concatenate([first_low.reshape(rows, span, D), second_low.reshape(rows, short, D)], 1)
    )
    near, far = out_moves[: rows // 2], out_moves[rows // 2 :]
    packed, gain_attn_1, grad_first, edges = pool_back_call(
        1, rows, span, batches, seqs, along, me, pooled, [grad_queries], [[pieces[0]] + others],
        grad_middle, second_angles, gain_attn, w_qkv, grouped, w_pool,
    )
    pool_1 = Halving(plan, along, scatter(packed, "batch"))
    carried = plan.shift(edges, -1)

    stays, leaves, gain_ffn_0, grad_middle, grad_mixed = ffn_back_call(
        0, rows, members, batches, seqs, crossed, me, behind(grad_first, *near), carried, middle_0, mixed_0,
        hidden_0, gain_ffn, w_out, w_up, w_down,
    )
    ffn_0 = Halving(plan, crossed, stays, leaves)
    got = ffn_0.send()
    leaving = ffn_1.add()
    got += ffn_1.send()
    got += far[::2]
    grad_mixed = behind(grad_mixed, *leaving)
    grad_queries, sources = [], []
    for group in range(groups):
        grad, pieces = attention_back_call(
            rows, members, me, queries_0, own_0, others_0, mixed_0, logsum_0, grad_mixed, [group]
        )
        grad_queries.append(grad)
        sources.append([pieces[0]] + [plan.shift(pieces[by], -by) for by in range(1, members)])
        ffn_0.wait(grad, *got)
        ffn_1.wait(grad, *got)
        if group == 0:
            leaving = ffn_0.add(2) + ffn_1.add()
            late = ffn_0.send()
            got = [late.pop(0)] + ffn_1.send() + far[1::2]
            grad_mixed = behind(grad_mixed, *leaving)
        else:
            leaving = ffn_1.add()
            got = late + ffn_1.send()
            leaving += ffn_0.add()
            got += ffn_0.send()
    stays, leaves, sums, grad_inputs = embed_back_call(
        0, batches, seqs, every, me, inputs, [behind(grad, *leaving) for grad in grad_queries], sources,
        grad_middle, first_angles, gain_attn, w_qkv, token_line, gain_attn_1, gain_ffn_0, gain_ffn_1,
    )

    leaves = behind(leaves, *got)
    for step, (axis, bit) in enumerate(every):
        came = plan.swap(leaves, axis, bit)
        if step == 1:
            input_grad = plan.exchange(behind(grad_inputs, leaves).reshape(rows, span, D))[0]
        for chain in (pool_1, ffn_1, ffn_0) if step else (pool_1,):
            if chain.order:
                chain.wait(leaves)
                chain.add()
                chain.send()
        if step < len(every) - 1:
            stays, leaves, sums = halve_call(stays, came, sums)
    made = finish_call(
        (ffn_layout, pool_layout, embed_layout),
        [ffn_0.rest(), ffn_1.rest(), pool_1.rest()],
        stays, sums, came,
    )
    qkv_grad, out_grad, up_grad, down_grad, pool_grad, embed_grad, gain_attn_grad, gain_ffn_grad = made
    return (
        outs[:, :span],
        outs[:, span:],
        input_grad.astype(F32),
        embed_grad,
        gain_attn_grad,
        jnp.swapaxes(qkv_grad, 1, 2),
        jnp.swapaxes(out_grad, 1, 2),
        gain_ffn_grad,
        up_grad,
        jnp.swapaxes(down_grad, 1, 2),
        pool_grad.T,
    )


def solution(mesh):
    in_specs = (
        P("batch", "seq"),
        P("batch", "seq"),
        P("batch", "seq", None),
        P(),
        P(),
        P(),
        P(),
        P(),
        P(),
        P(),
        P(),
    )
    out_specs = (
        P("batch", "seq", None),
        P("batch", "seq", None),
        P("batch", "seq", None),
        P("batch", "seq"),
        P(),
        P(None, "batch", "seq"),
        P(None, "batch", "seq"),
        P(),
        P(None, "batch", "seq"),
        P(None, "batch", "seq"),
        P("batch", "seq"),
    )
    return jax.shard_map(body, mesh=mesh, in_specs=in_specs, out_specs=out_specs, check_vma=False)
```
